128 devices in a mesh: slab: 32 (over y_hi, z, x), lvl: 4 (over y_lo, core).
Axes of the slice: x: 4, y: 4 (y_hi: 2, y_lo: 2; y = y_hi * 2 + y_lo), z: 4, core: 2. Of those that a mesh axis runs over, the one named last changes fastest.
Arguments:
- fine_state: float32 [32, 4, 5, 32, 1024], P('slab', 'lvl'), as said below
- coarse_state: float32 [32, 4, 5, 32, 1024], P('slab', 'lvl'), as said below
- partner: int32 [32, 4], P(None, 'lvl'), may hold values from 0 to 31, as said below
- mig_slot: int32 [32, 4], P(None, 'lvl'), may hold values from 0 to 0
- neighbours: int32 [32, 4, 6], P(None, 'lvl'), may hold values from -1 to 31, as said below
- work: int32 [32, 4], P(None, 'lvl'), may hold values from 1 to 4
- coarse_link: int32 [32, 4], P('slab', 'lvl'), may hold values from -1 to 95, as said below
Outputs:
- fine_out: float32 [32, 4, 5, 32, 1024], P('slab', 'lvl')
- coarse_out: float32 [32, 4, 5, 32, 1024], P('slab', 'lvl')
The draws below stay inside these ranges and needn't reach their ends.
Inputs may be any that keep to these rules, and one draw needn't show every extreme that they name: `fine_state`: density and pressure of every cell lie in 0.6 .. 1.5 and each velocity component in -0.3 .. 0.3; the arrays hold density, the three momenta and the total energy for a ratio of specific heats of 1.4. `coarse_state`: same law as the fine patches. An involution: partner[s, l] is s (no migration) or s XOR 2 ** b for some bit b; in every lvl column every bit of the slab index is used by some pair. `neighbours`: codes are slot codes before migration, -1 where there is no fine neighbour; symmetric: if the patch at code a has b across face f, then b has a across face f XOR 1. The fine patches of one lvl index form a lattice of 8 by 2 by 2 patches. `coarse_link`: -1 or c * 24 + f * 4 + q with c a lvl index, f a face of the fine patch and q a quarter of the coarse face; several fine faces may name the same place.
All inputs are finite; a program needn't handle non-finite values.
Results may differ from the reference program's by a relative error of at most 0.0003.
Values sent between devices are 32-bit elements; how exact they have to be, the bound alone decides.
A program may use at most 192 MiB of HBM per device.

```python
import jax
import jax.numpy as jnp
from jax import lax

C = 32
NF = 5
P_DEV = 1
WMAX = 4
SLOTS = 32
N_SLAB = 32
N_LVL = 4


def field_stack(key, leading, exponent):
    subkeys = jax.random.split(key, 5)
    dims_all = leading + (C, C * C)
    rows_iota = jnp.arange(C, dtype=jnp.int32)[:, None]
    cols_iota = jnp.arange(C * C, dtype=jnp.int32)[None, :]
    along_x = (1 - 2 * (rows_iota % 2)).astype(jnp.float32) * jnp.ones((1, C * C), jnp.float32)
    along_y = (1 - 2 * (cols_iota // C % 2)).astype(jnp.float32) * jnp.ones((C, 1), jnp.float32)
    along_z = (1 - 2 * (cols_iota % 2)).astype(jnp.float32) * jnp.ones((C, 1), jnp.float32)
    pattern = (along_x + along_y + along_z) / 3.0
    signs_all = [along_x, along_y, along_z]

    def spread(subkey, bottom, top_value):
        uniform_draw = jax.random.uniform(subkey, dims_all, jnp.float32)
        return bottom + (top_value - bottom) * uniform_draw ** exponent
    density = 1.05 + pattern * spread(subkeys[0], 0.15, 0.45)
    pressure = 1.05 + pattern * spread(subkeys[1], 0.15, 0.45)
    velocity = [signs_all[direction] * spread(subkeys[2 + direction], 0.1, 0.3) for direction in range(3)]
    squared = velocity[0] * velocity[0] + velocity[1] * velocity[1] + velocity[2] * velocity[2]
    energy = pressure / 0.4 + 0.5 * density * squared
    momenta = [density * component for component in velocity]
    return jnp.stack([density] + momenta + [energy], axis=-3)


def draw_fine_state(key, part):
    key = jax.random.fold_in(key, 11)
    exponent = 1.0
    return field_stack(key, (SLOTS, N_LVL), exponent)


def draw_coarse_state(key, part):
    key = jax.random.fold_in(key, 12)
    exponent = 1.0
    return field_stack(key, (N_SLAB, N_LVL), exponent)


def pair_column(key):
    device_count = N_SLAB
    bit_total = device_count.bit_length() - 1
    indices = jnp.arange(device_count, dtype=jnp.int32)
    paired = indices
    for bit_number in range(bit_total):
        across = jnp.bitwise_xor(indices, 1 << bit_number)
        unpaired = paired == indices
        usable = unpaired & unpaired[across]
        chosen = jnp.min(jnp.where(usable, indices, device_count))
        joined = ((indices == chosen) | (across == chosen)) & (chosen < device_count)
        paired = jnp.where(joined, across, paired)
    coin_key, shift_key = jax.random.split(key)
    coins = jax.random.randint(coin_key, (bit_total, device_count), 0, 2)
    for bit_number in range(bit_total):
        across = jnp.bitwise_xor(indices, 1 << bit_number)
        unpaired = paired == indices
        lower_end = jnp.minimum(indices, across)
        joined = unpaired & unpaired[across] & (coins[bit_number][lower_end] == 1)
        paired = jnp.where(joined, across, paired)
    offset = jax.random.randint(shift_key, (), 0, device_count).astype(jnp.int32)
    turned = jnp.bitwise_xor(indices, offset)
    return jnp.bitwise_xor(paired[turned], offset).astype(jnp.int32)


def draw_partner(key, part):
    key = jax.random.fold_in(key, 13)
    columns = jax.vmap(pair_column)(jax.random.split(key, N_LVL))
    return jnp.transpose(columns).astype(jnp.int32)


def draw_mig_slot(key, part):
    key = jax.random.fold_in(key, 14)
    return jax.random.randint(key, (N_SLAB, N_LVL), 0, P_DEV).astype(jnp.int32)


def lattice_column(key):
    positions = jnp.arange(SLOTS, dtype=jnp.int32)
    along_x = positions // 4
    along_y = positions // 2 % 2
    along_z = positions % 2
    rows_x = SLOTS // 4
    candidates = jnp.stack([positions - 4, positions + 4, positions - 2, positions + 2, positions - 1, positions + 1], axis=1)
    present = jnp.stack([along_x > 0, along_x < rows_x - 1, along_y == 1, along_y == 0, along_z == 1, along_z == 0], axis=1)
    stored_at = jax.random.permutation(key, SLOTS).astype(jnp.int32)
    labels = jnp.where(present, stored_at[jnp.clip(candidates, 0, SLOTS - 1)], -1)
    return jnp.zeros((SLOTS, 6), jnp.int32).at[stored_at].set(labels)


def draw_neighbours(key, part):
    key = jax.random.fold_in(key, 15)
    columns = jax.vmap(lattice_column)(jax.random.split(key, N_LVL))
    return jnp.transpose(columns, (1, 0, 2)).astype(jnp.int32)


def draw_work(key, part):
    key = jax.random.fold_in(key, 16)
    heavy_key, light_key, trim_key, pick_key = jax.random.split(key, 4)
    heavy = jax.random.randint(heavy_key, (N_SLAB, N_LVL), 0, 16) == 0
    forced = jax.random.randint(pick_key, (N_LVL,), 0, N_SLAB)
    heavy = heavy | (jnp.arange(N_SLAB)[:, None] == forced[None, :])
    heavy_slots = jnp.repeat(heavy, P_DEV, axis=0)
    light = 1 + (jax.random.randint(light_key, (SLOTS, N_LVL), 0, 3) == 0).astype(jnp.int32)
    trimmed = WMAX - (jax.random.randint(trim_key, (SLOTS, N_LVL), 0, 4) == 0).astype(jnp.int32)
    leading_slot = jnp.arange(SLOTS)[:, None] == forced[None, :] * P_DEV
    return jnp.where(leading_slot, WMAX, jnp.where(heavy_slots, trimmed, light)).astype(jnp.int32)


def draw_coarse_link(key, part):
    key = jax.random.fold_in(key, 17)
    code_key, empty_key, spot_key, place_key, quarter_key, pick_key, mix_key = jax.random.split(key, 7)
    slot_codes = jax.random.randint(code_key, (SLOTS, N_LVL), 0, N_LVL * 24)
    face_ids = jnp.arange(6, dtype=jnp.int32)
    hot_lvl = jax.random.randint(place_key, (6,), 0, N_LVL)
    hot_quarter = jax.random.randint(quarter_key, (6,), 0, 4)
    hot_codes = (hot_lvl * 24 + face_ids * 4 + hot_quarter).astype(jnp.int32)
    hot_pick = jax.random.randint(pick_key, (SLOTS, N_LVL), 0, 6)
    use_hot = jax.random.randint(mix_key, (SLOTS, N_LVL), 0, 8) != 0
    slot_codes = jnp.where(use_hot, hot_codes[hot_pick], slot_codes)
    vacant = jax.random.randint(empty_key, (SLOTS, N_LVL), 0, 4) == 0
    slot_codes = jnp.where(vacant, -1, slot_codes)
    spot = jax.random.randint(spot_key, (), 0, SLOTS * N_LVL)
    flat_index = jnp.arange(SLOTS * N_LVL).reshape(SLOTS, N_LVL)
    slot_codes = jnp.where(flat_index == spot, N_LVL * 24 - 1, slot_codes)
    slot_codes = jnp.where(flat_index == (spot + 1) % (SLOTS * N_LVL), -1, slot_codes)
    return slot_codes.astype(jnp.int32)


def setup_inputs(seed: int = 0) -> dict:
    streams_of = jax.random.split(jax.random.key(seed), 8)
    fine_state = draw_fine_state(jax.random.fold_in(streams_of[7], 71), 0)
    coarse_state = draw_coarse_state(jax.random.fold_in(streams_of[7], 71), 0)
    partner = draw_partner(jax.random.fold_in(streams_of[7], 71), 0)
    mig_slot = draw_mig_slot(jax.random.fold_in(streams_of[7], 71), 0)
    neighbours = draw_neighbours(jax.random.fold_in(streams_of[7], 71), 0)
    work = draw_work(jax.random.fold_in(streams_of[7], 71), 0)
    coarse_link = draw_coarse_link(jax.random.fold_in(streams_of[7], 71), 0)
    return dict(fine_state=fine_state, coarse_state=coarse_state, partner=partner, mig_slot=mig_slot, neighbours=neighbours, work=work, coarse_link=coarse_link)


ADIABATIC = 1.4
COARSE_STEP = 0.035
FLIPPED = (1, 0, 3, 2, 5, 4)
SIGNS = (-1.0, 1.0, -1.0, 1.0, -1.0, 1.0)
HIGHEST = lax.Precision.HIGHEST

def euler_flux(conserved, direction):
    density = conserved[..., 0, :, :, :]
    momenta = conserved[..., 1:4, :, :, :]
    energy = conserved[..., 4, :, :, :]
    velocity = momenta / density[..., None, :, :, :]
    kinetic = 0.5 * lax.optimization_barrier(jnp.sum(momenta * velocity, axis=-4))
    pressure = (ADIABATIC - 1.0) * (energy - kinetic)
    normal = velocity[..., direction, :, :, :]
    wave_speed = jnp.abs(normal) + jnp.sqrt(ADIABATIC * pressure / density)
    momentum_flux = momenta * normal[..., None, :, :, :]
    momentum_flux = momentum_flux.at[..., direction, :, :, :].add(pressure)
    mass_flux = momenta[..., direction, :, :, :]
    energy_flux = (energy + pressure) * normal
    flux_all = jnp.concatenate([mass_flux[..., None, :, :, :], momentum_flux, energy_flux[..., None, :, :, :]], axis=-4)
    return (flux_all, wave_speed)

def rusanov(left_side, right_side, direction):
    flux_left, speed_left = euler_flux(left_side, direction)
    flux_right, speed_right = euler_flux(right_side, direction)
    fastest = jnp.maximum(speed_left, speed_right)
    return 0.5 * (flux_left + flux_right) - 0.5 * fastest[..., None, :, :, :] * (right_side - left_side)

def advance(conserved, ghosts):
    divergence = None
    boundary = []
    for direction in range(3):
        spatial = conserved.ndim - 3 + direction
        lower_face = jnp.expand_dims(ghosts[..., 2 * direction, :, :, :], spatial)
        upper_face = jnp.expand_dims(ghosts[..., 2 * direction + 1, :, :, :], spatial)
        extended = jnp.concatenate([lower_face, conserved, upper_face], axis=spatial)
        cells_plus = extended.shape[spatial]
        left_side = lax.slice_in_dim(extended, 0, cells_plus - 1, axis=spatial)
        right_side = lax.slice_in_dim(extended, 1, cells_plus, axis=spatial)
        interface = rusanov(left_side, right_side, direction)
        faces_along = interface.shape[spatial]
        change = lax.slice_in_dim(interface, 1, faces_along, axis=spatial) - lax.slice_in_dim(interface, 0, faces_along - 1, axis=spatial)
        divergence = change if divergence is None else divergence + change
        boundary.append(lax.index_in_dim(interface, 0, spatial, keepdims=False))
        boundary.append(lax.index_in_dim(interface, faces_along - 1, spatial, keepdims=False))
    return (divergence, jnp.stack(boundary, axis=-4))

def face_layers(conserved):
    return jnp.stack([conserved[..., 0, :, :], conserved[..., -1, :, :], conserved[..., :, 0, :], conserved[..., :, -1, :], conserved[..., :, :, 0], conserved[..., :, :, -1]], axis=-4)

def coarsen(faces):
    half_cells = faces.shape[-1] // 2
    blocks = faces.reshape(faces.shape[:-2] + (half_cells, 2, half_cells, 2))
    return 0.25 * (blocks[..., 0, :, 0] + blocks[..., 1, :, 0] + blocks[..., 0, :, 1] + blocks[..., 1, :, 1])

def place_quarters(quartered):
    leading = quartered.shape[:-4]
    half_cells = quartered.shape[-1]
    fields = quartered.shape[-3]
    quarter_grid = quartered.reshape(leading + (2, 2, fields, half_cells, half_cells))
    grid_rank = quarter_grid.ndim
    axis_order = tuple(range(grid_rank - 5)) + (grid_rank - 3, grid_rank - 5, grid_rank - 2, grid_rank - 4, grid_rank - 1)
    return jnp.transpose(quarter_grid, axis_order).reshape(leading + (fields, 2 * half_cells, 2 * half_cells))

def expand_cover(counted, half_cells):
    leading = counted.shape[:-1]
    quarter_grid = counted.reshape(leading + (2, 2))
    spread_out = jnp.broadcast_to(quarter_grid[..., :, None, :, None], leading + (2, half_cells, 2, half_cells))
    return spread_out.reshape(leading + (2 * half_cells, 2 * half_cells))

def apply_correction(advanced, coarse_flux, totals, cover_full):
    for face_index in range(6):
        amount = SIGNS[face_index] * COARSE_STEP * (cover_full[..., face_index, None, :, :] * coarse_flux[..., face_index, :, :, :] - totals[..., face_index, :, :, :])
        edge_index = 0 if face_index % 2 == 0 else -1
        if face_index // 2 == 0:
            advanced = advanced.at[..., edge_index, :, :].add(amount)
        elif face_index // 2 == 1:
            advanced = advanced.at[..., :, edge_index, :].add(amount)
        else:
            advanced = advanced.at[..., :, :, edge_index].add(amount)
    return advanced

def relocate(slot_codes, partner, mig_slot, lvl_grid):
    clipped = jnp.maximum(slot_codes, 0)
    owner_slab = clipped // P_DEV
    mate_slab = partner[owner_slab, lvl_grid]
    moved_code = mate_slab * P_DEV + mig_slot[mate_slab, lvl_grid]
    shifted = jnp.where(clipped % P_DEV == mig_slot[owner_slab, lvl_grid], moved_code, slot_codes)
    return jnp.where(slot_codes < 0, slot_codes, shifted)

def fine_patch(bundle):
    patch_state, ghosts, step_count = bundle
    step_float = step_count.astype(jnp.float32)
    step_ratio = 2.0 * COARSE_STEP / step_float
    register = jnp.zeros(ghosts.shape, jnp.float32)
    for substep in range(WMAX):
        divergence, boundary = advance(patch_state, ghosts)
        active = substep < step_count
        register = jnp.where(active, register + boundary / step_float, register)
        patch_state = jnp.where(active, patch_state - step_ratio * divergence, patch_state)
    return (patch_state, register)

def coarse_patch(patch_state):
    ghosts = face_layers(patch_state)
    divergence, boundary = advance(patch_state, ghosts)
    return (patch_state - COARSE_STEP * divergence, boundary)

def reference(fine_state, coarse_state, partner, mig_slot, neighbours, work, coarse_link):
    lvl_grid = jnp.arange(N_LVL, dtype=jnp.int32)[None, :]
    slot_codes = jnp.broadcast_to(jnp.arange(SLOTS, dtype=jnp.int32)[:, None], (SLOTS, N_LVL))
    anchor = relocate(slot_codes, partner, mig_slot, lvl_grid)
    migrated = fine_state[anchor, lvl_grid].reshape(SLOTS, N_LVL, NF, C, C, C)
    step_count = work[anchor, lvl_grid]
    linked = relocate(neighbours[anchor, lvl_grid], partner, mig_slot, lvl_grid[:, :, None])
    layers = face_layers(migrated)
    flipped = jnp.stack([layers[:, :, face_index] for face_index in FLIPPED], axis=2)
    face_grid = jnp.arange(6, dtype=jnp.int32)[None, None, :]
    fetched = flipped[jnp.maximum(linked, 0), lvl_grid[:, :, None], face_grid]
    ghosts = jnp.where((linked >= 0)[..., None, None, None], fetched, layers)
    flat_count = SLOTS * N_LVL
    fine_next, register = lax.map(fine_patch, (migrated.reshape(flat_count, NF, C, C, C), ghosts.reshape(flat_count, 6, NF, C, C), step_count.reshape(flat_count)))
    fine_out = fine_next.reshape(SLOTS, N_LVL, NF, C, C * C)
    advanced, coarse_flux = lax.map(coarse_patch, coarse_state.reshape(N_SLAB * N_LVL, NF, C, C, C))
    coarsened = coarsen(register).reshape(N_SLAB, P_DEV, N_LVL, 6, NF, C // 2, C // 2)
    chooser = (coarse_link[:, :, None] == jnp.arange(N_LVL * 24, dtype=jnp.int32)[None, None, :]).astype(jnp.float32)
    chooser = chooser.reshape(N_SLAB, P_DEV, N_LVL, N_LVL, 6, 4)
    summed = jnp.einsum('splcfq,splfxab->scfqxab', chooser, coarsened, precision=HIGHEST)
    counted = lax.optimization_barrier(jnp.sum(chooser, axis=(1, 2)))
    summed = jnp.stack([summed[:, :, face_index] for face_index in FLIPPED], axis=2)
    counted = jnp.stack([counted[:, :, face_index] for face_index in FLIPPED], axis=2)
    totals = place_quarters(summed)
    cover_full = expand_cover(counted, C // 2)
    coarse_out = apply_correction(advanced.reshape(N_SLAB, N_LVL, NF, C, C, C), coarse_flux.reshape(N_SLAB, N_LVL, 6, NF, C, C), totals, cover_full)
    return (fine_out, coarse_out.reshape(N_SLAB, N_LVL, NF, C, C * C))
```

```python
import functools

import jax
import jax.numpy as jnp
from jax import lax
from jax.experimental import pallas as pl
from jax.experimental.pallas import tpu as pltpu
from jax.sharding import PartitionSpec as P

MESH = pl.DeviceIdType.MESH
F32 = jnp.float32
COARSE_STEP = 0.035
TILE = (8, 128)
PATCH = (5, 32, 8, 128)
CHUNK = 4
PIECES = 32 // CHUNK
HALF = PIECES // 2


def lanes():
    return lax.broadcasted_iota(jnp.int32, TILE, 1)


def rows():
    return lax.broadcasted_iota(jnp.int32, TILE, 0)


def primitives(cells):
    density, mom_x, mom_y, mom_z, energy = cells
    inverse = 1.0 / density
    vel = [mom_x * inverse, mom_y * inverse, mom_z * inverse]
    kinetic = 0.5 * (mom_x * vel[0] + mom_y * vel[1] + mom_z * vel[2])
    pressure = 0.4 * (energy - kinetic)
    half_sound = 0.5 * jnp.sqrt(1.4 * pressure * inverse)
    return (*vel, pressure, half_sound)


def half_flux(cells, prims, direction):
    half_normal = 0.5 * prims[direction]
    pressure, half_sound = prims[3], prims[4]
    flux = [cells[1 + i] * half_normal for i in range(3)]
    flux[direction] = flux[direction] + 0.5 * pressure
    flux.append((cells[4] + pressure) * half_normal)
    return flux, jnp.abs(half_normal) + half_sound


def interface(low, low_flux, low_speed, high, high_flux, high_speed, direction, sign=None):
    fastest = jnp.maximum(low_speed, high_speed)
    if sign is not None:
        fastest = fastest * sign
    out = [0.5 * (low[1 + direction] + high[1 + direction]) - fastest * (high[0] - low[0])]
    for i in range(4):
        out.append((low_flux[i] + high_flux[i]) - fastest * (high[1 + i] - low[1 + i]))
    return out


def z_up(v):
    return pltpu.roll(v, 127, 1)


def z_down(v):
    return pltpu.roll(v, 1, 1)


def y_up(v):
    return pltpu.roll(jnp.where(lanes() < 32, pltpu.roll(v, 7, 0), v), 96, 1)


def y_down(v):
    return pltpu.roll(jnp.where(lanes() >= 96, pltpu.roll(v, 1, 0), v), 32, 1)


def edge_masks(direction):
    if direction == 1:
        return (rows() == 0) & (lanes() < 32), (rows() == 7) & (lanes() >= 96)
    return lanes() % 32 == 0, lanes() % 32 == 31


def face_sign(direction):
    lower = rows() < 4 if direction == 1 else lanes() % 32 < 16
    return jnp.where(lower, -1.0, 1.0).astype(F32)


def across(cells, prims, direction, outer):
    up, down = (y_up, y_down) if direction == 1 else (z_up, z_down)
    flux, speed = half_flux(cells, prims, direction)
    inner = interface(
        cells, flux, speed, [up(v) for v in cells], [up(v) for v in flux], up(speed), direction
    )
    border = outer(flux, speed)
    lower, upper = edge_masks(direction)
    change = [
        jnp.where(upper, border[i], inner[i]) - jnp.where(lower, border[i], down(inner[i])) for i in range(5)
    ]
    return change, border


def load_plane(ref, x):
    return [ref[f, x] for f in range(5)]


def sweep(state, update):
    def prepare(x):
        cells = load_plane(state, x)
        prims = primitives(cells)
        flux, speed = half_flux(cells, prims, 0)
        return cells, prims, flux, speed

    ghost, _, ghost_flux, ghost_speed = prepare(0)
    first = prepare(1)
    lowest = interface(ghost, ghost_flux, ghost_speed, first[0], first[2], first[3], 0)

    def step(x, carried):
        cells, prims, flux, speed, below = carried
        after = prepare(x + 1)
        above = interface(cells, flux, speed, after[0], after[2], after[3], 0)
        new = update(x - 1, cells, prims, [above[i] - below[i] for i in range(5)])
        for f in range(5):
            state[f, x] = new[f]
        return (*after, above)

    last = lax.fori_loop(1, 33, step, (*first, lowest))
    return lowest, last[4]


def pack_y(flat, base, side, field, stride):
    out = None
    for g in range(4):
        part = flat[pl.ds(base + field * 8 * stride + g * 8 + 7 * side, 8, stride=32), :]
        part = pltpu.roll(part, (32 * g - 96 * side) % 128, 1)
        out = part if g == 0 else jnp.where(lanes() // 32 == g, part, out)
    return out


def pack_z(plane, x, side, out):
    return jnp.where(lanes() % 32 == x, pltpu.roll(plane, (x + 128 - 31 * side) % 128, 1), out)


def spread_y(face, field, x, side):
    row = jnp.broadcast_to(face[field, pl.ds(x // 4, 1), :], TILE)
    shift = (3 - x % 4) * 32 if side else (4 - x % 4) * 32
    return pltpu.roll(row, shift % 128, 1)


def spread_z(face, field, x, side):
    return pltpu.roll(face[field], (128 - x + 31 * side) % 128, 1)


def exchange_kernel(
    partner, neighbours, fine, migrated, ghosts,
    held, relay, faces, messages, landed,
    load_sem, ghost_send, ghost_recv, near_send, near_recv, far_send, far_recv,
    up_send, up_recv, on_send, on_recv,
):
    slab = lax.axis_index("slab")
    lvl = lax.axis_index("lvl")
    loads = [
        pltpu.make_async_copy(
            fine.at[0, 0, :, :, pl.ds(j * 128, 128)], held.at[0, :, :, j, :], load_sem.at[j]
        )
        for j in range(8)
    ]
    for copy in loads:
        copy.start()

    other_lvl = lax.rem(lvl + 2, 4)
    side_a = (slab, other_lvl)
    side_b = (slab ^ 16, other_lvl)
    barrier = pltpu.get_barrier_semaphore()
    for turn in range(1, 32):
        pl.semaphore_signal(barrier, inc=1, device_id=(slab ^ turn, lvl), device_id_type=MESH)
    for device in (side_a, side_b):
        pl.semaphore_signal(barrier, inc=1, device_id=device, device_id_type=MESH)
    pl.semaphore_wait(barrier, 33)
    for copy in loads:
        copy.wait()

    own = held.at[0]
    flat = own.reshape(5 * 32 * 8, 128)
    for f in range(5):
        faces[0, f] = own[f, 0]
        faces[1, f] = own[f, 31]
        for side in range(2):
            faces[2 + side, f] = pack_y(flat, 0, side, f, 32)

    def pack(x, carried):
        return tuple(
            pack_z(own[f, x], x, side, carried[side * 5 + f]) for side in range(2) for f in range(5)
        )

    packed = lax.fori_loop(0, 32, pack, (jnp.zeros(TILE, F32),) * 10)
    for side in range(2):
        for f in range(5):
            faces[4 + side, f] = packed[side * 5 + f]

    linked = [neighbours[slab, 0, f] for f in range(6)]
    sends = []
    for turn in range(32):
        there = slab ^ turn
        patch = partner[there, 0]
        face = jnp.int32(0)
        for f in range(1, 6):
            face = jnp.where(linked[f] == patch, f, face)
        target = messages if turn else landed
        for f in range(5):
            target[turn, f] = faces[face, f]
        if turn:
            copy = pltpu.make_async_remote_copy(
                src_ref=messages.at[turn], dst_ref=landed.at[turn],
                send_sem=ghost_send.at[turn], recv_sem=ghost_recv.at[turn],
                device_id=(there, lvl), device_id_type=MESH,
            )
            copy.start()
            sends.append(copy)

    def part(ref, c):
        return ref.at[:, pl.ds(c * CHUNK, CHUNK)]

    near, far, up, on = [], [], [], []
    for c in range(PIECES):
        for axis in range(2):
            copy = pltpu.make_async_remote_copy(
                src_ref=part(own, c), dst_ref=part(held.at[1 + 2 * axis], c),
                send_sem=near_send.at[axis, c], recv_sem=near_recv.at[axis, c],
                device_id=(slab ^ (1 if axis == 0 else 4), lvl), device_id_type=MESH,
            )
            copy.start()
            near.append(copy)
        side, piece = c % 2, c // 2
        copy = pltpu.make_async_remote_copy(
            src_ref=part(own, side * HALF + piece), dst_ref=part(relay.at[side], piece),
            send_sem=up_send.at[side, piece], recv_sem=up_recv.at[side, piece],
            device_id=side_b if side else side_a, device_id_type=MESH,
        )
        copy.start()
        up.append(copy)
    for c in range(PIECES):
        for axis in range(2):
            near[c * 2 + axis].wait_recv()
            copy = pltpu.make_async_remote_copy(
                src_ref=part(held.at[1 + 2 * axis], c), dst_ref=part(held.at[2 + 2 * axis], c),
                send_sem=far_send.at[axis, c], recv_sem=far_recv.at[axis, c],
                device_id=(slab ^ (3 if axis == 0 else 12), lvl), device_id_type=MESH,
            )
            copy.start()
            far.append(copy)
        side, piece = c % 2, c // 2
        up[c].wait_recv()
        copy = pltpu.make_async_remote_copy(
            src_ref=part(relay.at[side], piece), dst_ref=part(held.at[5], side * HALF + piece),
            send_sem=on_send.at[side, piece], recv_sem=on_recv.at[side, piece],
            device_id=side_a if side else side_b, device_id_type=MESH,
        )
        copy.start()
        on.append(copy)

    for copy in sends:
        copy.wait()
    source = partner[slab, 0]
    for f in range(6):
        there = jnp.maximum(neighbours[source, 0, f], 0) ^ slab
        for i in range(5):
            ghosts[f, i] = landed[there, i]

    for copy in far:
        copy.wait()
    for copy in on:
        copy.wait()
    for copy in near:
        copy.wait_send()
    for copy in up:
        copy.wait_send()
    apart = source ^ slab
    chosen = jnp.int32(0)
    for bit in range(5):
        chosen = chosen + (apart >= (1 << bit)).astype(jnp.int32)

    def choose(x, _):
        for f in range(5):
            migrated[f, x] = held[chosen, f, x]
        return 0

    lax.fori_loop(0, 32, choose, 0)


def fine_kernel(
    partner, neighbours, work, link, migrated, ghosts, out, message,
    state, outer_y, outer_z, register, x_register, squeezed, sem, out_sem,
):
    slab = lax.axis_index("slab")
    load = pltpu.make_async_copy(migrated, state.at[:, pl.ds(1, 32)], sem)
    load.start()
    source = partner[slab, 0]
    count = work[source, 0]
    linked = [neighbours[source, 0, f] >= 0 for f in range(6)]
    step_float = count.astype(F32)
    ratio = 2.0 * COARSE_STEP / jnp.full(TILE, step_float, F32)
    share = 1.0 / jnp.full(TILE, step_float, F32)
    code = link[0, 0]
    valid = code >= 0
    level = jnp.maximum(code, 0) // 24
    face = jnp.maximum(code, 0) % 24 // 4
    quarter = jnp.maximum(code, 0) % 4
    direction, side = face // 2, face % 2
    load.wait()

    for f in range(5):
        state[f, 0] = jnp.where(linked[0], ghosts[0, f], state[f, 1])
        state[f, 33] = jnp.where(linked[1], ghosts[1, f], state[f, 32])

    def spread(x, _):
        cells = load_plane(state, x + 1)
        for d, spreader, outer in ((1, spread_y, outer_y), (2, spread_z, outer_z)):
            lower = rows() < 4 if d == 1 else lanes() % 32 < 16
            values = []
            for f in range(5):
                low = jnp.where(linked[2 * d], spreader(ghosts.at[2 * d], f, x, 0), cells[f])
                high = jnp.where(linked[2 * d + 1], spreader(ghosts.at[2 * d + 1], f, x, 1), cells[f])
                values.append(jnp.where(lower, low, high))
            flux, speed = half_flux(values, primitives(values), d)
            for i, v in enumerate(values + flux + [speed]):
                outer[i, x] = v
        return 0

    lax.fori_loop(0, 32, spread, 0)

    for substep in range(4):
        active = substep < count

        def update(x, cells, prims, change, substep=substep, active=active):
            borders = []
            for d, outer in ((1, outer_y), (2, outer_z)):

                def border(flux, speed, d=d, outer=outer):
                    return interface(
                        cells, flux, speed, [outer[i, x] for i in range(5)],
                        [outer[5 + i, x] for i in range(4)], outer[9, x], d, face_sign(d),
                    )

                part, values = across(cells, prims, d, border)
                borders.append(values)
                change = [change[i] + part[i] for i in range(5)]
            for i in range(5):
                value = jnp.where(direction == 1, borders[0][i], borders[1][i])
                value = jnp.where(active, value * share, 0.0)
                register[i, x] = value if substep == 0 else register[i, x] + value
            return [jnp.where(active, cells[i] - ratio * change[i], cells[i]) for i in range(5)]

        lowest, highest = sweep(state, update)
        for i in range(5):
            value = jnp.where(side == 0, lowest[i], highest[i])
            value = jnp.where(active, value * share, 0.0)
            x_register[i] = value if substep == 0 else x_register[i] + value

    stores = [
        pltpu.make_async_copy(
            state.at[:, pl.ds(1, 32), j, :], out.at[0, 0, :, :, pl.ds(j * 128, 128)], out_sem.at[j]
        )
        for j in range(8)
    ]
    for copy in stores:
        copy.start()

    def pack(x, carried):
        return tuple(pack_z(register[f, x], x, side, carried[f]) for f in range(5))

    packed = lax.fori_loop(0, 32, pack, (jnp.zeros(TILE, F32),) * 5)
    flat = register.reshape(5 * 32 * 8, 128)
    source_lane = lax.broadcasted_iota(jnp.int32, (128, 128), 0)
    target_lane = lax.broadcasted_iota(jnp.int32, (128, 128), 1)
    wanted = target_lane // 32 * 64 + target_lane % 32 * 2
    squeeze = ((source_lane == wanted) & (target_lane % 32 < 16) & (target_lane < 64)).astype(F32)
    for f in range(5):
        value = jnp.where(direction == 1, pack_y(flat, 0, side, f, 32), packed[f])
        value = jnp.where(direction == 0, x_register[f], value)
        value = value + pltpu.roll(value, 127, 1)
        value = 0.25 * (value + pltpu.roll(value, 96, 1))
        squeezed[pl.ds(f * 8, 8), :] = jnp.dot(
            value, squeeze, precision=lax.Precision.HIGHEST, preferred_element_type=F32
        )
    quarter_row = jnp.where(direction == 2, quarter % 2, quarter // 2)
    quarter_col = jnp.where(direction == 2, quarter // 2, quarter % 2)
    low_lanes = lax.broadcasted_iota(jnp.int32, (4, 128), 1) < 64
    for f in range(5):
        even = squeezed[pl.ds(f * 8, 4, stride=2), :]
        odd = squeezed[pl.ds(f * 8 + 1, 4, stride=2), :]
        small = jnp.where(low_lanes, even, pltpu.roll(odd, 64, 1))
        small = jnp.where(quarter_col == 0, small, pltpu.roll(small, 16, 1))
        message[f, pl.ds(0, 4), :] = jnp.where(quarter_row == 0, small, 0.0)
        message[f, pl.ds(4, 4), :] = jnp.where(quarter_row == 1, small, 0.0)
    place = level * 6 + (face ^ 1) + 1
    inside = (rows() // 4 == quarter_row) & (lanes() % 32 // 16 == quarter_col)
    message[5] = jnp.where(inside & valid, place.astype(F32), 0.0)
    for copy in stores:
        copy.wait()


def coarse_kernel(
    message, coarse, out, state, flux_y, flux_z, flux_x, landed, totals, send_sem, recv_sem, sem,
):
    slab = lax.axis_index("slab")
    lvl = lax.axis_index("lvl")
    loads = [
        pltpu.make_async_copy(
            coarse.at[0, 0, :, :, pl.ds(j * 128, 128)], state.at[:, pl.ds(1, 32), j, :], sem.at[j]
        )
        for j in range(8)
    ]
    for copy in loads:
        copy.start()
    barrier = pltpu.get_barrier_semaphore()
    for turn in range(1, 4):
        pl.semaphore_signal(barrier, inc=1, device_id=(slab, lvl ^ turn), device_id_type=MESH)
    pl.semaphore_wait(barrier, 3)
    sends = []
    for turn in range(1, 4):
        copy = pltpu.make_async_remote_copy(
            src_ref=message, dst_ref=landed.at[turn - 1],
            send_sem=send_sem.at[turn - 1], recv_sem=recv_sem.at[turn - 1],
            device_id=(slab, lvl ^ turn), device_id_type=MESH,
        )
        copy.start()
        sends.append(copy)
    for copy in loads:
        copy.wait()
    for f in range(5):
        state[f, 0] = state[f, 1]
        state[f, 33] = state[f, 32]

    def update(x, cells, prims, change):
        for d, kept in ((1, flux_y), (2, flux_z)):

            def border(flux, speed, d=d):
                return [cells[1 + d]] + [2.0 * v for v in flux]

            part, values = across(cells, prims, d, border)
            change = [change[i] + part[i] for i in range(5)]
            for i in range(5):
                kept[i, x] = values[i]
        return [cells[i] - COARSE_STEP * change[i] for i in range(5)]

    lowest, highest = sweep(state, update)
    for i in range(5):
        flux_x[0, i] = lowest[i]
        flux_x[1, i] = highest[i]
    for copy in sends:
        copy.wait()

    for g in range(6):
        key = (lvl * 6 + g + 1).astype(F32)
        hits = [(message if n == 3 else landed.at[n])[5] == key for n in range(4)]
        for f in range(5):
            total = jnp.zeros(TILE, F32)
            for n in range(4):
                total = total + jnp.where(hits[n], (message if n == 3 else landed.at[n])[f], 0.0)
            totals[g, f] = total
        cover = jnp.zeros(TILE, F32)
        for n in range(4):
            cover = cover + jnp.where(hits[n], 1.0, 0.0)
        totals[g, 5] = cover

    for side, x in ((0, 1), (1, 32)):
        for f in range(5):
            amount = totals[side, 5] * flux_x[side, f] - totals[side, f]
            state[f, x] = state[f, x] + (COARSE_STEP if side else -COARSE_STEP) * amount

    def correct(x, _):
        cells = load_plane(state, x + 1)
        for d, spreader, kept in ((1, spread_y, flux_y), (2, spread_z, flux_z)):
            lower, upper = edge_masks(d)
            weight = COARSE_STEP * face_sign(d) * (lower | upper).astype(F32)

            def both(f, d=d, spreader=spreader, upper=upper):
                low = spreader(totals.at[2 * d], f, x, 0)
                high = spreader(totals.at[2 * d + 1], f, x, 1)
                return jnp.where(upper, high, low)

            cover = both(5)
            for f in range(5):
                cells[f] = cells[f] + weight * (cover * kept[f, x] - both(f))
        for f in range(5):
            state[f, x + 1] = cells[f]
        return 0

    lax.fori_loop(0, 32, correct, 0)
    stores = [
        pltpu.make_async_copy(
            state.at[:, pl.ds(1, 32), j, :], out.at[0, 0, :, :, pl.ds(j * 128, 128)], sem.at[j]
        )
        for j in range(8)
    ]
    for copy in stores:
        copy.start()
    for copy in stores:
        copy.wait()


SMEM = pl.BlockSpec(memory_space=pltpu.SMEM)
VMEM = pl.BlockSpec(memory_space=pltpu.VMEM)
ANY = pl.BlockSpec(memory_space=pl.ANY)
DMA = pltpu.SemaphoreType.DMA
LIMIT = 40 * 1024 * 1024


def exchange(partner, neighbours, fine_state):
    return pl.pallas_call(
        exchange_kernel,
        out_shape=(jax.ShapeDtypeStruct(PATCH, F32), jax.ShapeDtypeStruct((6, 5, *TILE), F32)),
        in_specs=[SMEM, SMEM, ANY],
        out_specs=(VMEM, VMEM),
        scratch_shapes=[
            pltpu.VMEM((6, *PATCH), F32),
            pltpu.VMEM((2, 5, 16, *TILE), F32),
            pltpu.VMEM((6, 5, *TILE), F32),
            pltpu.VMEM((32, 5, *TILE), F32),
            pltpu.VMEM((32, 5, *TILE), F32),
            DMA((8,)), DMA((32,)), DMA((32,)),
            DMA((2, PIECES)), DMA((2, PIECES)), DMA((2, PIECES)), DMA((2, PIECES)),
            DMA((2, HALF)), DMA((2, HALF)), DMA((2, HALF)), DMA((2, HALF)),
        ],
        compiler_params=pltpu.CompilerParams(collective_id=0, has_side_effects=True, vmem_limit_bytes=LIMIT),
        name="exchange",
    )(partner, neighbours, fine_state)


def fine_steps(partner, neighbours, work, link, migrated, ghosts, shape):
    return pl.pallas_call(
        fine_kernel,
        out_shape=(jax.ShapeDtypeStruct(shape, F32), jax.ShapeDtypeStruct((6, *TILE), F32)),
        in_specs=[SMEM, SMEM, SMEM, SMEM, ANY, VMEM],
        out_specs=(ANY, VMEM),
        scratch_shapes=[
            pltpu.VMEM((5, 34, *TILE), F32),
            pltpu.VMEM((10, 32, *TILE), F32),
            pltpu.VMEM((10, 32, *TILE), F32),
            pltpu.VMEM(PATCH, F32),
            pltpu.VMEM((5, *TILE), F32),
            pltpu.VMEM((40, 128), F32),
            DMA, DMA((8,)),
        ],
        compiler_params=pltpu.CompilerParams(vmem_limit_bytes=LIMIT),
        name="fine_steps",
    )(partner, neighbours, work, link, migrated, ghosts)


def coarse_step(message, coarse_state):
    return pl.pallas_call(
        coarse_kernel,
        out_shape=jax.ShapeDtypeStruct(coarse_state.shape, F32),
        in_specs=[VMEM, ANY],
        out_specs=ANY,
        scratch_shapes=[
            pltpu.VMEM((5, 34, *TILE), F32),
            pltpu.VMEM(PATCH, F32),
            pltpu.VMEM(PATCH, F32),
            pltpu.VMEM((2, 5, *TILE), F32),
            pltpu.VMEM((3, 6, *TILE), F32),
            pltpu.VMEM((6, 6, *TILE), F32),
            DMA((3,)), DMA((3,)), DMA((8,)),
        ],
        compiler_params=pltpu.CompilerParams(collective_id=1, has_side_effects=True, vmem_limit_bytes=LIMIT),
        name="coarse_step",
    )(message, coarse_state)


def body(fine_state, coarse_state, partner, mig_slot, neighbours, work, coarse_link):
    del mig_slot
    migrated, ghosts = exchange(partner, neighbours, fine_state)
    fine_out, message = fine_steps(partner, neighbours, work, coarse_link, migrated, ghosts, fine_state.shape)
    return fine_out, coarse_step(message, coarse_state)


def solution(mesh):
    return jax.shard_map(
        body,
        mesh=mesh,
        in_specs=(
            P("slab", "lvl", None, None, None),
            P("slab", "lvl", None, None, None),
            P(None, "lvl"),
            P(None, "lvl"),
            P(None, "lvl", None),
            P(None, "lvl"),
            P("slab", "lvl"),
        ),
        out_specs=(P("slab", "lvl", None, None, None), P("slab", "lvl", None, None, None)),
        check_vma=False,
    )
```

```python
import functools

import jax
import jax.numpy as jnp
from jax import lax
from jax.experimental import pallas as pl
from jax.experimental.pallas import tpu as pltpu
from jax.sharding import PartitionSpec as P

MESH = pl.DeviceIdType.MESH
F32 = jnp.float32
COARSE_STEP = 0.035
TILE = (8, 128)
PATCH = (5, 32, 8, 128)
CHUNK = 4
PIECES = 32 // CHUNK
HALF = PIECES // 2


def lanes():
    return lax.broadcasted_iota(jnp.int32, TILE, 1)


def rows():
    return lax.broadcasted_iota(jnp.int32, TILE, 0)


def primitives(cells):
    density, mom_x, mom_y, mom_z, energy = cells
    inverse = 1.0 / density
    vel = [mom_x * inverse, mom_y * inverse, mom_z * inverse]
    kinetic = 0.5 * (mom_x * vel[0] + mom_y * vel[1] + mom_z * vel[2])
    pressure = 0.4 * (energy - kinetic)
    half_sound = 0.5 * jnp.sqrt(1.4 * pressure * inverse)
    return (*vel, pressure, half_sound)


def half_flux(cells, prims, direction):
    half_normal = 0.5 * prims[direction]
    pressure, half_sound = prims[3], prims[4]
    flux = [cells[1 + i] * half_normal for i in range(3)]
    flux[direction] = flux[direction] + 0.5 * pressure
    flux.append((cells[4] + pressure) * half_normal)
    return flux, jnp.abs(half_normal) + half_sound


def interface(low, low_flux, low_speed, high, high_flux, high_speed, direction, sign=None):
    fastest = jnp.maximum(low_speed, high_speed)
    if sign is not None:
        fastest = fastest * sign
    out = [0.5 * (low[1 + direction] + high[1 + direction]) - fastest * (high[0] - low[0])]
    for i in range(4):
        out.append((low_flux[i] + high_flux[i]) - fastest * (high[1 + i] - low[1 + i]))
    return out


def z_up(v):
    return pltpu.roll(v, 127, 1)


def z_down(v):
    return pltpu.roll(v, 1, 1)


def y_up(v):
    return pltpu.roll(jnp.where(lanes() < 32, pltpu.roll(v, 7, 0), v), 96, 1)


def y_down(v):
    return pltpu.roll(jnp.where(lanes() >= 96, pltpu.roll(v, 1, 0), v), 32, 1)


def edge_masks(direction):
    if direction == 1:
        return (rows() == 0) & (lanes() < 32), (rows() == 7) & (lanes() >= 96)
    return lanes() % 32 == 0, lanes() % 32 == 31


def face_sign(direction):
    lower = rows() < 4 if direction == 1 else lanes() % 32 < 16
    return jnp.where(lower, -1.0, 1.0).astype(F32)


def across(cells, prims, direction, outer):
    up, down = (y_up, y_down) if direction == 1 else (z_up, z_down)
    flux, speed = half_flux(cells, prims, direction)
    inner = interface(
        cells, flux, speed, [up(v) for v in cells], [up(v) for v in flux], up(speed), direction
    )
    border = outer(flux, speed)
    lower, upper = edge_masks(direction)
    change = [
        jnp.where(upper, border[i], inner[i]) - jnp.where(lower, border[i], down(inner[i])) for i in range(5)
    ]
    return change, border


def load_plane(ref, x):
    return [ref[f, x] for f in range(5)]


def sweep(state, update):
    def prepare(x):
        cells = load_plane(state, x)
        prims = primitives(cells)
        flux, speed = half_flux(cells, prims, 0)
        return cells, prims, flux, speed

    ghost, _, ghost_flux, ghost_speed = prepare(0)
    first = prepare(1)
    lowest = interface(ghost, ghost_flux, ghost_speed, first[0], first[2], first[3], 0)

    def step(x, carried):
        cells, prims, flux, speed, below = carried
        after = prepare(x + 1)
        above = interface(cells, flux, speed, after[0], after[2], after[3], 0)
        new = update(x - 1, cells, prims, [above[i] - below[i] for i in range(5)])
        for f in range(5):
            state[f, x] = new[f]
        return (*after, above)

    last = lax.fori_loop(1, 33, step, (*first, lowest), unroll=4)
    return lowest, last[4]


def pack_y(flat, base, side, field, stride):
    out = None
    for g in range(4):
        part = flat[pl.ds(base + field * 8 * stride + g * 8 + 7 * side, 8, stride=32), :]
        part = pltpu.roll(part, (32 * g - 96 * side) % 128, 1)
        out = part if g == 0 else jnp.where(lanes() // 32 == g, part, out)
    return out


def pack_z(plane, x, side, out):
    return jnp.where(lanes() % 32 == x, pltpu.roll(plane, (x + 128 - 31 * side) % 128, 1), out)


def spread_y(face, field, x, side):
    row = jnp.broadcast_to(face[field, pl.ds(x // 4, 1), :], TILE)
    shift = (3 - x % 4) * 32 if side else (4 - x % 4) * 32
    return pltpu.roll(row, shift % 128, 1)


def spread_z(face, field, x, side):
    return pltpu.roll(face[field], (128 - x + 31 * side) % 128, 1)


def exchange_kernel(
    partner, neighbours, fine, migrated, ghosts,
    held, relay, faces, messages, landed,
    load_sem, ghost_send, ghost_recv, near_send, near_recv, far_send, far_recv,
    up_send, up_recv, on_send, on_recv,
):
    slab = lax.axis_index("slab")
    lvl = lax.axis_index("lvl")
    loads = [
        pltpu.make_async_copy(
            fine.at[0, 0, :, :, pl.ds(j * 128, 128)], held.at[0, :, :, j, :], load_sem.at[j]
        )
        for j in range(8)
    ]
    for copy in loads:
        copy.start()

    other_lvl = lax.rem(lvl + 2, 4)
    side_a = (slab, other_lvl)
    side_b = (slab ^ 16, other_lvl)
    barrier = pltpu.get_barrier_semaphore()
    for turn in range(1, 32):
        pl.semaphore_signal(barrier, inc=1, device_id=(slab ^ turn, lvl), device_id_type=MESH)
    for device in (side_a, side_b):
        pl.semaphore_signal(barrier, inc=1, device_id=device, device_id_type=MESH)
    pl.semaphore_wait(barrier, 33)
    for copy in loads:
        copy.wait()

    own = held.at[0]
    flat = own.reshape(5 * 32 * 8, 128)
    for f in range(5):
        faces[0, f] = own[f, 0]
        faces[1, f] = own[f, 31]
        for side in range(2):
            faces[2 + side, f] = pack_y(flat, 0, side, f, 32)

    def pack(x, carried):
        return tuple(
            pack_z(own[f, x], x, side, carried[side * 5 + f]) for side in range(2) for f in range(5)
        )

    packed = lax.fori_loop(0, 32, pack, (jnp.zeros(TILE, F32),) * 10, unroll=4)
    for side in range(2):
        for f in range(5):
            faces[4 + side, f] = packed[side * 5 + f]

    linked = [neighbours[slab, 0, f] for f in range(6)]
    sends = []
    for turn in range(32):
        there = slab ^ turn
        patch = partner[there, 0]
        face = jnp.int32(0)
        for f in range(1, 6):
            face = jnp.where(linked[f] == patch, f, face)
        target = messages if turn else landed
        for f in range(5):
            target[turn, f] = faces[face, f]
        if turn:
            copy = pltpu.make_async_remote_copy(
                src_ref=messages.at[turn], dst_ref=landed.at[turn],
                send_sem=ghost_send.at[turn], recv_sem=ghost_recv.at[turn],
                device_id=(there, lvl), device_id_type=MESH,
            )
            copy.start()
            sends.append(copy)

    def part(ref, c):
        return ref.at[:, pl.ds(c * CHUNK, CHUNK)]

    near, far, up, on = [], [], [], []
    for c in range(PIECES):
        for axis in range(2):
            copy = pltpu.make_async_remote_copy(
                src_ref=part(own, c), dst_ref=part(held.at[1 + 2 * axis], c),
                send_sem=near_send.at[axis, c], recv_sem=near_recv.at[axis, c],
                device_id=(slab ^ (1 if axis == 0 else 4), lvl), device_id_type=MESH,
            )
            copy.start()
            near.append(copy)
        side, piece = c % 2, c // 2
        copy = pltpu.make_async_remote_copy(
            src_ref=part(own, side * HALF + piece), dst_ref=part(relay.at[side], piece),
            send_sem=up_send.at[side, piece], recv_sem=up_recv.at[side, piece],
            device_id=side_b if side else side_a, device_id_type=MESH,
        )
        copy.start()
        up.append(copy)
    for c in range(PIECES):
        for axis in range(2):
            near[c * 2 + axis].wait_recv()
            copy = pltpu.make_async_remote_copy(
                src_ref=part(held.at[1 + 2 * axis], c), dst_ref=part(held.at[2 + 2 * axis], c),
                send_sem=far_send.at[axis, c], recv_sem=far_recv.at[axis, c],
                device_id=(slab ^ (3 if axis == 0 else 12), lvl), device_id_type=MESH,
            )
            copy.start()
            far.append(copy)
        side, piece = c % 2, c // 2
        up[c].wait_recv()
        copy = pltpu.make_async_remote_copy(
            src_ref=part(relay.at[side], piece), dst_ref=part(held.at[5], side * HALF + piece),
            send_sem=on_send.at[side, piece], recv_sem=on_recv.at[side, piece],
            device_id=side_a if side else side_b, device_id_type=MESH,
        )
        copy.start()
        on.append(copy)

    for copy in sends:
        copy.wait()
    source = partner[slab, 0]
    for f in range(6):
        there = jnp.maximum(neighbours[source, 0, f], 0) ^ slab
        for i in range(5):
            ghosts[f, i] = landed[there, i]

    for copy in far:
        copy.wait()
    for copy in on:
        copy.wait()
    for copy in near:
        copy.wait_send()
    for copy in up:
        copy.wait_send()
    apart = source ^ slab
    chosen = jnp.int32(0)
    for bit in range(5):
        chosen = chosen + (apart >= (1 << bit)).astype(jnp.int32)

    def choose(x, _):
        for f in range(5):
            migrated[f, x] = held[chosen, f, x]
        return 0

    lax.fori_loop(0, 32, choose, 0, unroll=4)


def fine_kernel(
    partner, neighbours, work, link, migrated, ghosts, out, message,
    state, outer_y, outer_z, register, x_register, squeezed, sem, out_sem,
):
    slab = lax.axis_index("slab")
    load = pltpu.make_async_copy(migrated, state.at[:, pl.ds(1, 32)], sem)
    load.start()
    source = partner[slab, 0]
    count = work[source, 0]
    linked = [neighbours[source, 0, f] >= 0 for f in range(6)]
    step_float = count.astype(F32)
    ratio = 2.0 * COARSE_STEP / jnp.full(TILE, step_float, F32)
    share = 1.0 / jnp.full(TILE, step_float, F32)
    code = link[0, 0]
    valid = code >= 0
    level = jnp.maximum(code, 0) // 24
    face = jnp.maximum(code, 0) % 24 // 4
    quarter = jnp.maximum(code, 0) % 4
    direction, side = face // 2, face % 2
    load.wait()

    for f in range(5):
        state[f, 0] = jnp.where(linked[0], ghosts[0, f], state[f, 1])
        state[f, 33] = jnp.where(linked[1], ghosts[1, f], state[f, 32])

    def spread(x, _):
        cells = load_plane(state, x + 1)
        for d, spreader, outer in ((1, spread_y, outer_y), (2, spread_z, outer_z)):
            lower = rows() < 4 if d == 1 else lanes() % 32 < 16
            values = []
            for f in range(5):
                low = jnp.where(linked[2 * d], spreader(ghosts.at[2 * d], f, x, 0), cells[f])
                high = jnp.where(linked[2 * d + 1], spreader(ghosts.at[2 * d + 1], f, x, 1), cells[f])
                values.append(jnp.where(lower, low, high))
            flux, speed = half_flux(values, primitives(values), d)
            for i, v in enumerate(values + flux + [speed]):
                outer[i, x] = v
        return 0

    lax.fori_loop(0, 32, spread, 0, unroll=4)

    for substep in range(4):
        active = substep < count

        def update(x, cells, prims, change, substep=substep, active=active):
            borders = []
            for d, outer in ((1, outer_y), (2, outer_z)):

                def border(flux, speed, d=d, outer=outer):
                    return interface(
                        cells, flux, speed, [outer[i, x] for i in range(5)],
                        [outer[5 + i, x] for i in range(4)], outer[9, x], d, face_sign(d),
                    )

                part, values = across(cells, prims, d, border)
                borders.append(values)
                change = [change[i] + part[i] for i in range(5)]
            for i in range(5):
                value = jnp.where(direction == 1, borders[0][i], borders[1][i])
                value = jnp.where(active, value * share, 0.0)
                register[i, x] = value if substep == 0 else register[i, x] + value
            return [jnp.where(active, cells[i] - ratio * change[i], cells[i]) for i in range(5)]

        lowest, highest = sweep(state, update)
        for i in range(5):
            value = jnp.where(side == 0, lowest[i], highest[i])
            value = jnp.where(active, value * share, 0.0)
            x_register[i] = value if substep == 0 else x_register[i] + value

    stores = [
        pltpu.make_async_copy(
            state.at[:, pl.ds(1, 32), j, :], out.at[0, 0, :, :, pl.ds(j * 128, 128)], out_sem.at[j]
        )
        for j in range(8)
    ]
    for copy in stores:
        copy.start()

    def pack(x, carried):
        return tuple(pack_z(register[f, x], x, side, carried[f]) for f in range(5))

    packed = lax.fori_loop(0, 32, pack, (jnp.zeros(TILE, F32),) * 5, unroll=4)
    flat = register.reshape(5 * 32 * 8, 128)
    source_lane = lax.broadcasted_iota(jnp.int32, (128, 128), 0)
    target_lane = lax.broadcasted_iota(jnp.int32, (128, 128), 1)
    wanted = target_lane // 32 * 64 + target_lane % 32 * 2
    squeeze = ((source_lane == wanted) & (target_lane % 32 < 16) & (target_lane < 64)).astype(F32)
    for f in range(5):
        value = jnp.where(direction == 1, pack_y(flat, 0, side, f, 32), packed[f])
        value = jnp.where(direction == 0, x_register[f], value)
        value = value + pltpu.roll(value, 127, 1)
        value = 0.25 * (value + pltpu.roll(value, 96, 1))
        squeezed[pl.ds(f * 8, 8), :] = jnp.dot(
            value, squeeze, precision=lax.Precision.HIGHEST, preferred_element_type=F32
        )
    quarter_row = jnp.where(direction == 2, quarter % 2, quarter // 2)
    quarter_col = jnp.where(direction == 2, quarter // 2, quarter % 2)
    low_lanes = lax.broadcasted_iota(jnp.int32, (4, 128), 1) < 64
    for f in range(5):
        even = squeezed[pl.ds(f * 8, 4, stride=2), :]
        odd = squeezed[pl.ds(f * 8 + 1, 4, stride=2), :]
        small = jnp.where(low_lanes, even, pltpu.roll(odd, 64, 1))
        small = jnp.where(quarter_col == 0, small, pltpu.roll(small, 16, 1))
        message[f, pl.ds(0, 4), :] = jnp.where(quarter_row == 0, small, 0.0)
        message[f, pl.ds(4, 4), :] = jnp.where(quarter_row == 1, small, 0.0)
    place = level * 6 + (face ^ 1) + 1
    inside = (rows() // 4 == quarter_row) & (lanes() % 32 // 16 == quarter_col)
    message[5] = jnp.where(inside & valid, place.astype(F32), 0.0)
    for copy in stores:
        copy.wait()


def coarse_kernel(
    message, coarse, out, state, flux_y, flux_z, flux_x, landed, totals, send_sem, recv_sem, sem,
):
    slab = lax.axis_index("slab")
    lvl = lax.axis_index("lvl")
    loads = [
        pltpu.make_async_copy(
            coarse.at[0, 0, :, :, pl.ds(j * 128, 128)], state.at[:, pl.ds(1, 32), j, :], sem.at[j]
        )
        for j in range(8)
    ]
    for copy in loads:
        copy.start()
    barrier = pltpu.get_barrier_semaphore()
    for turn in range(1, 4):
        pl.semaphore_signal(barrier, inc=1, device_id=(slab, lvl ^ turn), device_id_type=MESH)
    pl.semaphore_wait(barrier, 3)
    sends = []
    for turn in range(1, 4):
        copy = pltpu.make_async_remote_copy(
            src_ref=message, dst_ref=landed.at[turn - 1],
            send_sem=send_sem.at[turn - 1], recv_sem=recv_sem.at[turn - 1],
            device_id=(slab, lvl ^ turn), device_id_type=MESH,
        )
        copy.start()
        sends.append(copy)
    for copy in loads:
        copy.wait()
    for f in range(5):
        state[f, 0] = state[f, 1]
        state[f, 33] = state[f, 32]

    def update(x, cells, prims, change):
        for d, kept in ((1, flux_y), (2, flux_z)):

            def border(flux, speed, d=d):
                return [cells[1 + d]] + [2.0 * v for v in flux]

            part, values = across(cells, prims, d, border)
            change = [change[i] + part[i] for i in range(5)]
            for i in range(5):
                kept[i, x] = values[i]
        return [cells[i] - COARSE_STEP * change[i] for i in range(5)]

    lowest, highest = sweep(state, update)
    for i in range(5):
        flux_x[0, i] = lowest[i]
        flux_x[1, i] = highest[i]
    for copy in sends:
        copy.wait()

    for g in range(6):
        key = (lvl * 6 + g + 1).astype(F32)
        hits = [(message if n == 3 else landed.at[n])[5] == key for n in range(4)]
        for f in range(5):
            total = jnp.zeros(TILE, F32)
            for n in range(4):
                total = total + jnp.where(hits[n], (message if n == 3 else landed.at[n])[f], 0.0)
            totals[g, f] = total
        cover = jnp.zeros(TILE, F32)
        for n in range(4):
            cover = cover + jnp.where(hits[n], 1.0, 0.0)
        totals[g, 5] = cover

    for side, x in ((0, 1), (1, 32)):
        for f in range(5):
            amount = totals[side, 5] * flux_x[side, f] - totals[side, f]
            state[f, x] = state[f, x] + (COARSE_STEP if side else -COARSE_STEP) * amount

    def correct(x, _):
        cells = load_plane(state, x + 1)
        for d, spreader, kept in ((1, spread_y, flux_y), (2, spread_z, flux_z)):
            lower, upper = edge_masks(d)
            weight = COARSE_STEP * face_sign(d) * (lower | upper).astype(F32)

            def both(f, d=d, spreader=spreader, upper=upper):
                low = spreader(totals.at[2 * d], f, x, 0)
                high = spreader(totals.at[2 * d + 1], f, x, 1)
                return jnp.where(upper, high, low)

            cover = both(5)
            for f in range(5):
                cells[f] = cells[f] + weight * (cover * kept[f, x] - both(f))
        for f in range(5):
            state[f, x + 1] = cells[f]
        return 0

    lax.fori_loop(0, 32, correct, 0, unroll=4)
    stores = [
        pltpu.make_async_copy(
            state.at[:, pl.ds(1, 32), j, :], out.at[0, 0, :, :, pl.ds(j * 128, 128)], sem.at[j]
        )
        for j in range(8)
    ]
    for copy in stores:
        copy.start()
    for copy in stores:
        copy.wait()


SMEM = pl.BlockSpec(memory_space=pltpu.SMEM)
VMEM = pl.BlockSpec(memory_space=pltpu.VMEM)
ANY = pl.BlockSpec(memory_space=pl.ANY)
DMA = pltpu.SemaphoreType.DMA
LIMIT = 40 * 1024 * 1024


def exchange(partner, neighbours, fine_state):
    return pl.pallas_call(
        exchange_kernel,
        out_shape=(jax.ShapeDtypeStruct(PATCH, F32), jax.ShapeDtypeStruct((6, 5, *TILE), F32)),
        in_specs=[SMEM, SMEM, ANY],
        out_specs=(VMEM, VMEM),
        scratch_shapes=[
            pltpu.VMEM((6, *PATCH), F32),
            pltpu.VMEM((2, 5, 16, *TILE), F32),
            pltpu.VMEM((6, 5, *TILE), F32),
            pltpu.VMEM((32, 5, *TILE), F32),
            pltpu.VMEM((32, 5, *TILE), F32),
            DMA((8,)), DMA((32,)), DMA((32,)),
            DMA((2, PIECES)), DMA((2, PIECES)), DMA((2, PIECES)), DMA((2, PIECES)),
            DMA((2, HALF)), DMA((2, HALF)), DMA((2, HALF)), DMA((2, HALF)),
        ],
        compiler_params=pltpu.CompilerParams(collective_id=0, has_side_effects=True, vmem_limit_bytes=LIMIT),
        name="exchange",
    )(partner, neighbours, fine_state)


def fine_steps(partner, neighbours, work, link, migrated, ghosts, shape):
    return pl.pallas_call(
        fine_kernel,
        out_shape=(jax.ShapeDtypeStruct(shape, F32), jax.ShapeDtypeStruct((6, *TILE), F32)),
        in_specs=[SMEM, SMEM, SMEM, SMEM, ANY, VMEM],
        out_specs=(ANY, VMEM),
        scratch_shapes=[
            pltpu.VMEM((5, 34, *TILE), F32),
            pltpu.VMEM((10, 32, *TILE), F32),
            pltpu.VMEM((10, 32, *TILE), F32),
            pltpu.VMEM(PATCH, F32),
            pltpu.VMEM((5, *TILE), F32),
            pltpu.VMEM((40, 128), F32),
            DMA, DMA((8,)),
        ],
        compiler_params=pltpu.CompilerParams(vmem_limit_bytes=LIMIT),
        name="fine_steps",
    )(partner, neighbours, work, link, migrated, ghosts)


def coarse_step(message, coarse_state):
    return pl.pallas_call(
        coarse_kernel,
        out_shape=jax.ShapeDtypeStruct(coarse_state.shape, F32),
        in_specs=[VMEM, ANY],
        out_specs=ANY,
        scratch_shapes=[
            pltpu.VMEM((5, 34, *TILE), F32),
            pltpu.VMEM(PATCH, F32),
            pltpu.VMEM(PATCH, F32),
            pltpu.VMEM((2, 5, *TILE), F32),
            pltpu.VMEM((3, 6, *TILE), F32),
            pltpu.VMEM((6, 6, *TILE), F32),
            DMA((3,)), DMA((3,)), DMA((8,)),
        ],
        compiler_params=pltpu.CompilerParams(collective_id=1, has_side_effects=True, vmem_limit_bytes=LIMIT),
        name="coarse_step",
    )(message, coarse_state)


def body(fine_state, coarse_state, partner, mig_slot, neighbours, work, coarse_link):
    del mig_slot
    migrated, ghosts = exchange(partner, neighbours, fine_state)
    fine_out, message = fine_steps(partner, neighbours, work, coarse_link, migrated, ghosts, fine_state.shape)
    return fine_out, coarse_step(message, coarse_state)


def solution(mesh):
    return jax.shard_map(
        body,
        mesh=mesh,
        in_specs=(
            P("slab", "lvl", None, None, None),
            P("slab", "lvl", None, None, None),
            P(None, "lvl"),
            P(None, "lvl"),
            P(None, "lvl", None),
            P(None, "lvl"),
            P("slab", "lvl"),
        ),
        out_specs=(P("slab", "lvl", None, None, None), P("slab", "lvl", None, None, None)),
        check_vma=False,
    )
```

```python
import jax
import jax.numpy as jnp
from jax import lax
from jax.experimental import pallas as pl
from jax.experimental.pallas import tpu as pltpu
from jax.sharding import PartitionSpec as P

MESH = pl.DeviceIdType.MESH
F32 = jnp.float32
COARSE_STEP = 0.035
TILE = (8, 128)
PATCH = (5, 32, 8, 128)
CHUNK = 4
CHUNKS = 32 // CHUNK
NOTE = CHUNKS
PLANES = 35
ORDER = (0, 1, 2, 3, 4, 5, NOTE, 6, 7)


def lanes():
    return lax.broadcasted_iota(jnp.int32, TILE, 1)


def rows():
    return lax.broadcasted_iota(jnp.int32, TILE, 0)


def primitives(cells):
    density, mom_x, mom_y, mom_z, energy = cells
    inverse = 1.0 / density
    vel = [mom_x * inverse, mom_y * inverse, mom_z * inverse]
    kinetic = 0.5 * (mom_x * vel[0] + mom_y * vel[1] + mom_z * vel[2])
    pressure = 0.4 * (energy - kinetic)
    half_sound = 0.5 * jnp.sqrt(1.4 * pressure * inverse)
    return (*vel, pressure, half_sound)


def half_flux(cells, prims, direction):
    half_normal = 0.5 * prims[direction]
    pressure, half_sound = prims[3], prims[4]
    flux = [cells[1 + i] * half_normal for i in range(3)]
    flux[direction] = flux[direction] + 0.5 * pressure
    flux.append((cells[4] + pressure) * half_normal)
    return flux, jnp.abs(half_normal) + half_sound


def interface(low, low_flux, low_speed, high, high_flux, high_speed, direction, sign=None):
    fastest = jnp.maximum(low_speed, high_speed)
    if sign is not None:
        fastest = fastest * sign
    out = [0.5 * (low[1 + direction] + high[1 + direction]) - fastest * (high[0] - low[0])]
    for i in range(4):
        out.append((low_flux[i] + high_flux[i]) - fastest * (high[1 + i] - low[1 + i]))
    return out


def z_up(v):
    return pltpu.roll(v, 127, 1)


def z_down(v):
    return pltpu.roll(v, 1, 1)


def y_up(v):
    return pltpu.roll(jnp.where(lanes() < 32, pltpu.roll(v, 7, 0), v), 96, 1)


def y_down(v):
    return pltpu.roll(jnp.where(lanes() >= 96, pltpu.roll(v, 1, 0), v), 32, 1)


def edge_masks(direction):
    if direction == 1:
        return (rows() == 0) & (lanes() < 32), (rows() == 7) & (lanes() >= 96)
    return lanes() % 32 == 0, lanes() % 32 == 31


def face_sign(direction):
    lower = rows() < 4 if direction == 1 else lanes() % 32 < 16
    return jnp.where(lower, -1.0, 1.0).astype(F32)


def across(cells, prims, direction, outer):
    up, down = (y_up, y_down) if direction == 1 else (z_up, z_down)
    flux, speed = half_flux(cells, prims, direction)
    inner = interface(
        cells, flux, speed, [up(v) for v in cells], [up(v) for v in flux], up(speed), direction
    )
    border = outer(flux, speed)
    lower, upper = edge_masks(direction)
    change = [
        jnp.where(upper, border[i], inner[i]) - jnp.where(lower, border[i], down(inner[i])) for i in range(5)
    ]
    return change, border


def load_plane(ref, x):
    return [ref[f, x] for f in range(5)]


def prepare(state, x):
    cells = load_plane(state, x)
    prims = primitives(cells)
    flux, speed = half_flux(cells, prims, 0)
    return cells, prims, flux, speed


def lowest_interface(state):
    ghost, _, ghost_flux, ghost_speed = prepare(state, 0)
    first, _, flux, speed = prepare(state, 1)
    return interface(ghost, ghost_flux, ghost_speed, first, flux, speed, 0)


def advance(state, first, count, below, update):
    cells, prims, flux, speed = prepare(state, first)
    for n in range(count):
        after = prepare(state, first + n + 1)
        above = interface(cells, flux, speed, after[0], after[2], after[3], 0)
        new = update(first + n - 1, cells, prims, [above[i] - below[i] for i in range(5)])
        for f in range(5):
            state[f, first + n] = new[f]
        cells, prims, flux, speed = after
        below = above
    return below


def pack_y(flat, first, side):
    out = None
    for g in range(4):
        part = flat[pl.ds(first + g * 8 + 7 * side, 8, stride=32), :]
        part = pltpu.roll(part, (32 * g - 96 * side) % 128, 1)
        out = part if g == 0 else jnp.where(lanes() // 32 == g, part, out)
    return out


def pack_z(plane, x, side, out):
    return jnp.where(lanes() % 32 == x, pltpu.roll(plane, (x + 128 - 31 * side) % 128, 1), out)


def pack_z_faces(ref, first):
    def pack(x, carried):
        return tuple(
            pack_z(ref[f, first + x], x, side, carried[side * 5 + f]) for side in range(2) for f in range(5)
        )

    return lax.fori_loop(0, 32, pack, (jnp.zeros(TILE, F32),) * 10, unroll=4)


def spread_y(face, field, x, side):
    row = jnp.broadcast_to(face[field, pl.ds(x // 4, 1), :], TILE)
    shift = (3 - x % 4) * 32 if side else (4 - x % 4) * 32
    return pltpu.roll(row, shift % 128, 1)


def spread_z(face, field, x, side):
    return pltpu.roll(face[field], (128 - x + 31 * side) % 128, 1)


def step_kernel(
    partner, neighbours, work, link, fine, coarse, fine_result, coarse_result,
    held, relay, faces, messages, landed, ghosts, marks,
    outer_y, outer_z, register, x_register, carry, squeezed,
    coarse_state, flux_y, flux_z, flux_x, note, notes, totals,
    load_sem, coarse_sem, ghost_send, ghost_recv, mark_send, mark_recv, note_send, note_recv,
    near_send, near_recv, far_send, far_recv, up_send, up_recv, on_send, on_recv,
):
    slab = lax.axis_index("slab")
    lvl = lax.axis_index("lvl")
    other_lvl = lvl ^ 2
    own = held.at[0]

    def loads_of(source, target, sem):
        return [
            pltpu.make_async_copy(
                source.at[0, 0, :, :, pl.ds(j * 128, 128)], target.at[:, pl.ds(1, 32), j, :], sem.at[j]
            )
            for j in range(8)
        ]

    fine_loads = loads_of(fine, own, load_sem)
    coarse_loads = loads_of(coarse, coarse_state, coarse_sem)
    for copy in fine_loads + coarse_loads:
        copy.start()

    barrier = pltpu.get_barrier_semaphore()
    greeted = [(slab ^ turn, lvl) for turn in range(1, 32)]
    greeted += [(slab, lvl ^ turn) for turn in range(1, 4)] + [(slab ^ 16, other_lvl)]
    for device in greeted:
        pl.semaphore_signal(barrier, inc=1, device_id=device, device_id_type=MESH)

    code = link[0, 0]
    valid = code >= 0
    level = jnp.maximum(code, 0) // 24
    face = jnp.maximum(code, 0) % 24 // 4
    quarter = jnp.maximum(code, 0) % 4
    marks[0] = jnp.full(TILE, face.astype(F32), F32)
    apart = partner[0, slab] ^ slab
    chosen = jnp.int32(0)
    for bit in range(5):
        chosen = chosen + (apart >= (1 << bit)).astype(jnp.int32)

    def choose(values):
        out = values[0]
        for n in range(1, 6):
            out = jnp.where(chosen == n, values[n], out)
        return out

    for copy in fine_loads:
        copy.wait()
    flat = own.reshape(5 * PLANES * 8, 128)
    for f in range(5):
        faces[0, f] = own[f, 1]
        faces[1, f] = own[f, 32]
        for side in range(2):
            faces[2 + side, f] = pack_y(flat, (f * PLANES + 1) * 8, side)
    packed = pack_z_faces(own, 1)
    for side in range(2):
        for f in range(5):
            faces[4 + side, f] = packed[side * 5 + f]

    pl.semaphore_wait(barrier, len(greeted))

    linked = [neighbours[f, 0, slab] for f in range(6)]
    ghost_copies = []
    for turn in range(1, 32):
        there = slab ^ turn
        which = jnp.int32(0)
        for f in range(1, 6):
            which = jnp.where(linked[f] == there, f, which)
        for f in range(5):
            messages[turn, f] = faces[which, f]
        copy = pltpu.make_async_remote_copy(
            src_ref=messages.at[turn], dst_ref=landed.at[turn],
            send_sem=ghost_send.at[turn], recv_sem=ghost_recv.at[turn],
            device_id=(there, lvl), device_id_type=MESH,
        )
        copy.start()
        ghost_copies.append(copy)
    mark_copies = []
    for bit in range(5):
        copy = pltpu.make_async_remote_copy(
            src_ref=marks.at[0], dst_ref=marks.at[1 + bit],
            send_sem=mark_send.at[bit], recv_sem=mark_recv.at[bit],
            device_id=(slab ^ (1 << bit), lvl), device_id_type=MESH,
        )
        copy.start()
        mark_copies.append(copy)

    for copy in coarse_loads:
        copy.wait()
    for f in range(5):
        coarse_state[f, 0] = coarse_state[f, 1]
        coarse_state[f, 33] = coarse_state[f, 32]

    def coarse_update(x, cells, prims, change):
        for d, kept in ((1, flux_y), (2, flux_z)):

            def border(flux, speed, d=d):
                return [cells[1 + d]] + [2.0 * v for v in flux]

            part, values = across(cells, prims, d, border)
            change = [change[i] + part[i] for i in range(5)]
            for i in range(5):
                kept[i, x] = values[i]
        return [cells[i] - COARSE_STEP * change[i] for i in range(5)]

    lowest = lowest_interface(coarse_state)

    def coarse_chunk(c, below):
        return tuple(advance(coarse_state, 1 + c * CHUNK, CHUNK, below, coarse_update))

    highest = lax.fori_loop(0, CHUNKS, coarse_chunk, tuple(lowest))
    for i in range(5):
        flux_x[0, i] = lowest[i]
        flux_x[1, i] = highest[i]

    for copy in ghost_copies + mark_copies:
        copy.wait_recv()
    present = [linked[f] >= 0 for f in range(6)]
    for f in range(6):
        turn = jnp.maximum(linked[f], 0) ^ slab
        for i in range(5):
            ghosts[f, i] = landed[turn, i]
    for f in range(5):
        own[f, 0] = jnp.where(present[0], ghosts[0, f], own[f, 1])
        own[f, 33] = jnp.where(present[1], ghosts[1, f], own[f, 32])
    mark = choose([marks[n] for n in range(6)])
    along_y = (mark == 2.0) | (mark == 3.0)

    count = work[0, slab]
    steps = jnp.full(TILE, count.astype(F32), F32)
    ratio = 2.0 * COARSE_STEP / steps
    share = 1.0 / steps

    def spread(x):
        cells = load_plane(own, x + 1)
        for d, spreader, outer in ((1, spread_y, outer_y), (2, spread_z, outer_z)):
            lower = rows() < 4 if d == 1 else lanes() % 32 < 16
            values = []
            for f in range(5):
                low = jnp.where(present[2 * d], spreader(ghosts.at[2 * d], f, x, 0), cells[f])
                high = jnp.where(present[2 * d + 1], spreader(ghosts.at[2 * d + 1], f, x, 1), cells[f])
                values.append(jnp.where(lower, low, high))
            flux, speed = half_flux(values, primitives(values), d)
            for i, v in enumerate(values + flux + [speed]):
                outer[i, x] = v

    def updater(substep):
        active = substep < count

        def update(x, cells, prims, change):
            borders = []
            for d, outer in ((1, outer_y), (2, outer_z)):

                def border(flux, speed, d=d, outer=outer):
                    return interface(
                        cells, flux, speed, [outer[i, x] for i in range(5)],
                        [outer[5 + i, x] for i in range(4)], outer[9, x], d, face_sign(d),
                    )

                part, values = across(cells, prims, d, border)
                borders.append(values)
                change = [change[i] + part[i] for i in range(5)]
            for i in range(5):
                value = jnp.where(along_y, borders[0][i], borders[1][i])
                value = jnp.where(active, value * share, 0.0)
                register[i, x] = value if substep == 0 else register[i, x] + value
            return [jnp.where(active, cells[i] - ratio * change[i], cells[i]) for i in range(5)]

        return update

    def outermost(substep, side, values):
        for i in range(5):
            value = jnp.where(substep < count, values[i] * share, 0.0)
            x_register[side, i] = value if substep == 0 else x_register[side, i] + value

    def span(ref, piece):
        if isinstance(piece, int) and piece == NOTE:
            return ref.at[:, pl.ds(34, 1)]
        return ref.at[:, pl.ds(1 + piece * CHUNK, CHUNK)]

    def near(axis, piece):
        return pltpu.make_async_remote_copy(
            src_ref=span(own, piece), dst_ref=span(held.at[1 + 2 * axis], piece),
            send_sem=near_send.at[axis, piece], recv_sem=near_recv.at[axis, piece],
            device_id=(slab ^ (4 if axis else 1), lvl), device_id_type=MESH,
        )

    def far(axis, piece):
        return pltpu.make_async_remote_copy(
            src_ref=span(held.at[1 + 2 * axis], piece), dst_ref=span(held.at[2 + 2 * axis], piece),
            send_sem=far_send.at[axis, piece], recv_sem=far_recv.at[axis, piece],
            device_id=(slab ^ (12 if axis else 3), lvl), device_id_type=MESH,
        )

    def up(piece):
        return pltpu.make_async_remote_copy(
            src_ref=span(own, piece), dst_ref=span(relay, piece),
            send_sem=up_send.at[piece], recv_sem=up_recv.at[piece],
            device_id=(slab ^ (piece % 2 * 16), other_lvl), device_id_type=MESH,
        )

    def on(piece):
        return pltpu.make_async_remote_copy(
            src_ref=span(relay, piece), dst_ref=span(held.at[5], piece),
            send_sem=on_send.at[piece], recv_sem=on_recv.at[piece],
            device_id=(slab ^ ((piece + 1) % 2 * 16), other_lvl), device_id_type=MESH,
        )

    def send(piece):
        near(0, piece).start()
        near(1, piece).start()
        up(piece).start()

    def forward(piece):
        for axis in range(2):
            near(axis, piece).wait_recv()
            far(axis, piece).start()
        up(piece).wait_recv()
        on(piece).start()

    def arrive(piece):
        far(0, piece).wait_recv()
        far(1, piece).wait_recv()
        on(piece).wait_recv()

    for x in range(3):
        spread(x)
    for substep in range(4):
        lowest = lowest_interface(own)
        outermost(substep, 0, lowest)
        below = advance(own, 1, 3 - substep, lowest, updater(substep)) if substep < 3 else lowest
        for i in range(5):
            carry[substep, i] = below[i]

    def wave(c, _):
        for n in range(CHUNK):
            spread(c * CHUNK - 1 + n)
        for substep in range(4):
            below = [carry[substep, i] for i in range(5)]
            below = advance(own, c * CHUNK - substep, CHUNK, below, updater(substep))
            for i in range(5):
                carry[substep, i] = below[i]

        @pl.when(c < 7)
        def _():
            send(c - 1)

        @pl.when((c == 4) | (c == 6))
        def _():
            forward(c // 2 - 2)

        return 0

    lax.fori_loop(1, CHUNKS, wave, 0)
    spread(31)
    for substep in range(4):
        below = [carry[substep, i] for i in range(5)]
        outermost(substep, 1, advance(own, 32 - substep, substep + 1, below, updater(substep)))
    forward(2)

    packed = pack_z_faces(register, 0)
    flat = register.reshape(5 * 32 * 8, 128)
    source_lane = lax.broadcasted_iota(jnp.int32, (128, 128), 0)
    target_lane = lax.broadcasted_iota(jnp.int32, (128, 128), 1)
    wanted = target_lane // 32 * 64 + target_lane % 32 * 2
    squeeze = ((source_lane == wanted) & (target_lane % 32 < 16) & (target_lane < 64)).astype(F32)
    for f in range(5):
        options = [x_register[0, f], x_register[1, f], pack_y(flat, f * 256, 0), pack_y(flat, f * 256, 1)]
        value = packed[5 + f]
        for n, option in enumerate([*options, packed[f]]):
            value = jnp.where(mark == float(n), option, value)
        value = value + pltpu.roll(value, 127, 1)
        value = 0.25 * (value + pltpu.roll(value, 96, 1))
        squeezed[pl.ds(f * 8, 8), :] = jnp.dot(
            value, squeeze, precision=lax.Precision.HIGHEST, preferred_element_type=F32
        )
    low_lanes = lax.broadcasted_iota(jnp.int32, (4, 128), 1) < 64
    for f in range(5):
        even = squeezed[pl.ds(f * 8, 4, stride=2), :]
        odd = squeezed[pl.ds(f * 8 + 1, 4, stride=2), :]
        own[f, 34, pl.ds(0, 4), :] = jnp.where(low_lanes, even, pltpu.roll(odd, 64, 1))
        own[f, 34, pl.ds(4, 4), :] = jnp.zeros((4, 128), F32)

    for piece in ORDER[6:]:
        send(piece)

    direction = face // 2
    quarter_row = jnp.where(direction == 2, quarter % 2, quarter // 2)
    quarter_col = jnp.where(direction == 2, quarter // 2, quarter % 2)
    note_copies = [
        pltpu.make_async_remote_copy(
            src_ref=note, dst_ref=notes.at[turn - 1],
            send_sem=note_send.at[turn - 1], recv_sem=note_recv.at[turn - 1],
            device_id=(slab, lvl ^ turn), device_id_type=MESH,
        )
        for turn in range(1, 4)
    ]

    def take(piece):
        arrive(piece)
        if piece != NOTE:
            for n in range(CHUNK):
                x = piece * CHUNK + n
                for f in range(5):
                    fine_result[f, x] = choose([held[k, f, x + 1] for k in range(6)])
            return
        for f in range(5):
            small = choose([held[k, f, 34, pl.ds(0, 4), :] for k in range(6)])
            small = jnp.where(quarter_col == 0, small, pltpu.roll(small, 16, 1))
            note[f, pl.ds(0, 4), :] = jnp.where(quarter_row == 0, small, 0.0)
            note[f, pl.ds(4, 4), :] = jnp.where(quarter_row == 1, small, 0.0)
        place = level * 6 + (face ^ 1) + 1
        inside = (rows() // 4 == quarter_row) & (lanes() % 32 // 16 == quarter_col)
        note[5] = jnp.where(inside & valid, place.astype(F32), 0.0)
        for copy in note_copies:
            copy.start()

    for piece in range(3, 6):
        forward(piece)
        take(piece - 3)
    forward(NOTE)
    take(3)
    forward(6)
    take(4)
    take(5)
    take(NOTE)
    forward(7)
    take(6)

    for copy in note_copies:
        copy.wait_recv()
    for g in range(6):
        key = (lvl * 6 + g + 1).astype(F32)
        parts = [note if n == 3 else notes.at[n] for n in range(4)]
        hits = [part[5] == key for part in parts]
        for f in range(5):
            total = jnp.zeros(TILE, F32)
            for n in range(4):
                total = total + jnp.where(hits[n], parts[n][f], 0.0)
            totals[g, f] = total
        cover = jnp.zeros(TILE, F32)
        for n in range(4):
            cover = cover + jnp.where(hits[n], 1.0, 0.0)
        totals[g, 5] = cover

    for side, x in ((0, 1), (1, 32)):
        for f in range(5):
            amount = totals[side, 5] * flux_x[side, f] - totals[side, f]
            coarse_state[f, x] = coarse_state[f, x] + (COARSE_STEP if side else -COARSE_STEP) * amount

    def correct(x, _):
        cells = load_plane(coarse_state, x + 1)
        for d, spreader, kept in ((1, spread_y, flux_y), (2, spread_z, flux_z)):
            lower, upper = edge_masks(d)
            weight = COARSE_STEP * face_sign(d) * (lower | upper).astype(F32)

            def both(f, d=d, spreader=spreader, upper=upper):
                low = spreader(totals.at[2 * d], f, x, 0)
                high = spreader(totals.at[2 * d + 1], f, x, 1)
                return jnp.where(upper, high, low)

            cover = both(5)
            for f in range(5):
                cells[f] = cells[f] + weight * (cover * kept[f, x] - both(f))
        for f in range(5):
            coarse_result[f, x] = cells[f]
        return 0

    lax.fori_loop(0, 32, correct, 0, unroll=4)
    take(7)

    for copy in ghost_copies + mark_copies + note_copies:
        copy.wait_send()
    for piece in range(CHUNKS + 1):
        for axis in range(2):
            near(axis, piece).wait_send()
            far(axis, piece).wait_send()
        up(piece).wait_send()
        on(piece).wait_send()


def write_kernel(fine_result, coarse_result, fine_out, coarse_out, sem):
    copies = [
        pltpu.make_async_copy(
            source.at[:, :, j, :], target.at[0, 0, :, :, pl.ds(j * 128, 128)], sem.at[n, j]
        )
        for n, (source, target) in enumerate(((fine_result, fine_out), (coarse_result, coarse_out)))
        for j in range(8)
    ]
    for copy in copies:
        copy.start()
    for copy in copies:
        copy.wait()


SMEM = pl.BlockSpec(memory_space=pltpu.SMEM)
VMEM = pl.BlockSpec(memory_space=pltpu.VMEM)
HBM = pl.BlockSpec(memory_space=pltpu.HBM)
DMA = pltpu.SemaphoreType.DMA
LIMIT = 40 * 1024 * 1024


def step(partner, neighbours, work, link, fine_state, coarse_state):
    pieces = CHUNKS + 1
    return pl.pallas_call(
        step_kernel,
        out_shape=(jax.ShapeDtypeStruct(PATCH, F32), jax.ShapeDtypeStruct(PATCH, F32)),
        in_specs=[SMEM, SMEM, SMEM, SMEM, HBM, HBM],
        out_specs=(VMEM, VMEM),
        scratch_shapes=[
            pltpu.VMEM((6, 5, PLANES, *TILE), F32),
            pltpu.VMEM((5, PLANES, *TILE), F32),
            pltpu.VMEM((6, 5, *TILE), F32),
            pltpu.VMEM((32, 5, *TILE), F32),
            pltpu.VMEM((32, 5, *TILE), F32),
            pltpu.VMEM((6, 5, *TILE), F32),
            pltpu.VMEM((6, *TILE), F32),
            pltpu.VMEM((10, 32, *TILE), F32),
            pltpu.VMEM((10, 32, *TILE), F32),
            pltpu.VMEM(PATCH, F32),
            pltpu.VMEM((2, 5, *TILE), F32),
            pltpu.VMEM((4, 5, *TILE), F32),
            pltpu.VMEM((40, 128), F32),
            pltpu.VMEM((5, 34, *TILE), F32),
            pltpu.VMEM(PATCH, F32),
            pltpu.VMEM(PATCH, F32),
            pltpu.VMEM((2, 5, *TILE), F32),
            pltpu.VMEM((6, *TILE), F32),
            pltpu.VMEM((3, 6, *TILE), F32),
            pltpu.VMEM((6, 6, *TILE), F32),
            DMA((8,)), DMA((8,)), DMA((32,)), DMA((32,)), DMA((5,)), DMA((5,)), DMA((3,)), DMA((3,)),
            DMA((2, pieces)), DMA((2, pieces)), DMA((2, pieces)), DMA((2, pieces)),
            DMA((pieces,)), DMA((pieces,)), DMA((pieces,)), DMA((pieces,)),
        ],
        compiler_params=pltpu.CompilerParams(collective_id=0, has_side_effects=True, vmem_limit_bytes=LIMIT),
        name="step",
    )(partner, neighbours, work, link, fine_state, coarse_state)


def write(fine_result, coarse_result, shape):
    return pl.pallas_call(
        write_kernel,
        out_shape=(jax.ShapeDtypeStruct(shape, F32),) * 2,
        in_specs=[VMEM, VMEM],
        out_specs=(HBM, HBM),
        scratch_shapes=[DMA((2, 8))],
        name="write",
    )(fine_result, coarse_result)


def body(fine_state, coarse_state, partner, mig_slot, neighbours, work, coarse_link):
    del mig_slot
    results = step(
        partner.T, jnp.transpose(neighbours, (2, 1, 0)), work.T, coarse_link, fine_state, coarse_state
    )
    return write(*results, fine_state.shape)


def solution(mesh):
    return jax.shard_map(
        body,
        mesh=mesh,
        in_specs=(
            P("slab", "lvl", None, None, None),
            P("slab", "lvl", None, None, None),
            P(None, "lvl"),
            P(None, "lvl"),
            P(None, "lvl", None),
            P(None, "lvl"),
            P("slab", "lvl"),
        ),
        out_specs=(P("slab", "lvl", None, None, None), P("slab", "lvl", None, None, None)),
        check_vma=False,
    )
```

```python
import jax
import jax.numpy as jnp
from jax import lax
from jax.experimental import pallas as pl
from jax.experimental.pallas import tpu as pltpu
from jax.sharding import PartitionSpec as P

MESH = pl.DeviceIdType.MESH
F32 = jnp.float32
COARSE_STEP = 0.035
TILE = (8, 128)
PATCH = (5, 32, 8, 128)
CHUNK = 4
CHUNKS = 32 // CHUNK
FIRST = 1
COARSE_BREAK = 4


def lanes():
    return lax.broadcasted_iota(jnp.int32, TILE, 1)


def rows():
    return lax.broadcasted_iota(jnp.int32, TILE, 0)


def primitives(cells):
    density, mom_x, mom_y, mom_z, energy = cells
    inverse = 1.0 / density
    vel = [mom_x * inverse, mom_y * inverse, mom_z * inverse]
    kinetic = 0.5 * (mom_x * vel[0] + mom_y * vel[1] + mom_z * vel[2])
    pressure = 0.4 * (energy - kinetic)
    half_sound = 0.5 * jnp.sqrt(1.4 * pressure * inverse)
    return (*vel, pressure, half_sound)


def half_flux(cells, prims, direction):
    half_normal = 0.5 * prims[direction]
    pressure, half_sound = prims[3], prims[4]
    flux = [cells[1 + i] * half_normal for i in range(3)]
    flux[direction] = flux[direction] + 0.5 * pressure
    flux.append((cells[4] + pressure) * half_normal)
    return flux, jnp.abs(half_normal) + half_sound


def interface(low, low_flux, low_speed, high, high_flux, high_speed, direction, sign=None):
    fastest = jnp.maximum(low_speed, high_speed)
    if sign is not None:
        fastest = fastest * sign
    out = [0.5 * (low[1 + direction] + high[1 + direction]) - fastest * (high[0] - low[0])]
    for i in range(4):
        out.append((low_flux[i] + high_flux[i]) - fastest * (high[1 + i] - low[1 + i]))
    return out


def z_up(v):
    return pltpu.roll(v, 127, 1)


def z_down(v):
    return pltpu.roll(v, 1, 1)


def y_up(v):
    return pltpu.roll(jnp.where(lanes() < 32, pltpu.roll(v, 7, 0), v), 96, 1)


def y_down(v):
    return pltpu.roll(jnp.where(lanes() >= 96, pltpu.roll(v, 1, 0), v), 32, 1)


def edge_masks(direction):
    if direction == 1:
        return (rows() == 0) & (lanes() < 32), (rows() == 7) & (lanes() >= 96)
    return lanes() % 32 == 0, lanes() % 32 == 31


def face_sign(direction):
    lower = rows() < 4 if direction == 1 else lanes() % 32 < 16
    return jnp.where(lower, -1.0, 1.0).astype(F32)


def across(cells, prims, direction, outer):
    up, down = (y_up, y_down) if direction == 1 else (z_up, z_down)
    flux, speed = half_flux(cells, prims, direction)
    inner = interface(
        cells, flux, speed, [up(v) for v in cells], [up(v) for v in flux], up(speed), direction
    )
    border = outer(flux, speed)
    lower, upper = edge_masks(direction)
    change = [
        jnp.where(upper, border[i], inner[i]) - jnp.where(lower, border[i], down(inner[i])) for i in range(5)
    ]
    return change, border


def load_plane(ref, x):
    return [ref[f, x] for f in range(5)]


def prepare(state, x):
    cells = load_plane(state, x)
    prims = primitives(cells)
    flux, speed = half_flux(cells, prims, 0)
    return cells, prims, flux, speed


def lowest_interface(state):
    ghost, _, ghost_flux, ghost_speed = prepare(state, 0)
    first, _, flux, speed = prepare(state, 1)
    return interface(ghost, ghost_flux, ghost_speed, first, flux, speed, 0)


def advance(state, first, count, below, update):
    cells, prims, flux, speed = prepare(state, first)
    for n in range(count):
        after = prepare(state, first + n + 1)
        above = interface(cells, flux, speed, after[0], after[2], after[3], 0)
        new = update(first + n - 1, cells, prims, [above[i] - below[i] for i in range(5)])
        for f in range(5):
            state[f, first + n] = new[f]
        cells, prims, flux, speed = after
        below = above
    return below


def pack_y(flat, first, side):
    out = None
    for g in range(4):
        part = flat[pl.ds(first + g * 8 + 7 * side, 8, stride=32), :]
        part = pltpu.roll(part, (32 * g - 96 * side) % 128, 1)
        out = part if g == 0 else jnp.where(lanes() // 32 == g, part, out)
    return out


def pack_z(plane, x, side, out):
    return jnp.where(lanes() % 32 == x, pltpu.roll(plane, (x + 128 - 31 * side) % 128, 1), out)


def pack_z_faces(ref, first):
    def pack(x, carried):
        return tuple(
            pack_z(ref[f, first + x], x, side, carried[side * 5 + f]) for side in range(2) for f in range(5)
        )

    return lax.fori_loop(0, 32, pack, (jnp.zeros(TILE, F32),) * 10, unroll=4)


def spread_y(face, field, x, side):
    row = jnp.broadcast_to(face[field, pl.ds(x // 4, 1), :], TILE)
    shift = (3 - x % 4) * 32 if side else (4 - x % 4) * 32
    return pltpu.roll(row, shift % 128, 1)


def spread_z(face, field, x, side):
    return pltpu.roll(face[field], (128 - x + 31 * side) % 128, 1)


def step_kernel(
    partner, neighbours, work, link, fine, coarse, fine_out, coarse_out,
    held, relay, faces, messages, landed, ghosts,
    state, outer_y, outer_z, register, x_register, packed_z, carry, squeezed,
    coarse_state, flux_y, flux_z, flux_x, note, notes, totals,
    load_sem, coarse_sem, store_sem, coarse_store_sem, ghost_send, ghost_recv, note_send, note_recv,
    near_send, near_recv, far_send, far_recv, up_send, up_recv, on_send, on_recv,
):
    slab = lax.axis_index("slab")
    lvl = lax.axis_index("lvl")
    other_lvl = lvl ^ 2
    own = held.at[0]

    def loads_of(source, target, sem):
        return [
            pltpu.make_async_copy(source.at[0, 0, :, :, pl.ds(j * 128, 128)], target.at[:, :, j, :], sem.at[j])
            for j in range(8)
        ]

    fine_loads = loads_of(fine, own, load_sem)
    coarse_loads = loads_of(coarse, coarse_state.at[:, pl.ds(1, 32)], coarse_sem)
    for copy in fine_loads + coarse_loads:
        copy.start()

    barrier = pltpu.get_barrier_semaphore()
    greeted = [(slab ^ turn, lvl) for turn in range(1, 32)]
    greeted += [(slab, lvl ^ turn) for turn in range(1, 4)] + [(slab ^ 16, other_lvl)]
    for device in greeted:
        pl.semaphore_signal(barrier, inc=1, device_id=device, device_id_type=MESH)

    def span(ref, piece):
        return ref.at[:, pl.ds(piece * CHUNK, CHUNK)]

    def near(axis, piece):
        return pltpu.make_async_remote_copy(
            src_ref=span(own, piece), dst_ref=span(held.at[1 + 2 * axis], piece),
            send_sem=near_send.at[axis, piece], recv_sem=near_recv.at[axis, piece],
            device_id=(slab ^ (4 if axis else 1), lvl), device_id_type=MESH,
        )

    def far(axis, piece):
        return pltpu.make_async_remote_copy(
            src_ref=span(held.at[1 + 2 * axis], piece), dst_ref=span(held.at[2 + 2 * axis], piece),
            send_sem=far_send.at[axis, piece], recv_sem=far_recv.at[axis, piece],
            device_id=(slab ^ (12 if axis else 3), lvl), device_id_type=MESH,
        )

    def up(piece):
        return pltpu.make_async_remote_copy(
            src_ref=span(own, piece), dst_ref=span(relay, piece),
            send_sem=up_send.at[piece], recv_sem=up_recv.at[piece],
            device_id=(slab ^ (piece % 2 * 16), other_lvl), device_id_type=MESH,
        )

    def on(piece):
        return pltpu.make_async_remote_copy(
            src_ref=span(relay, piece), dst_ref=span(held.at[5], piece),
            send_sem=on_send.at[piece], recv_sem=on_recv.at[piece],
            device_id=(slab ^ ((piece + 1) % 2 * 16), other_lvl), device_id_type=MESH,
        )

    def send(piece):
        near(0, piece).start()
        near(1, piece).start()
        up(piece).start()

    def forward(piece):
        for axis in range(2):
            near(axis, piece).wait_recv()
            far(axis, piece).start()
        up(piece).wait_recv()
        on(piece).start()

    def arrive(piece):
        far(0, piece).wait_recv()
        far(1, piece).wait_recv()
        on(piece).wait_recv()

    for copy in fine_loads:
        copy.wait()
    pl.semaphore_wait(barrier, len(greeted))
    for piece in range(FIRST):
        send(piece)

    flat = own.reshape(5 * 32 * 8, 128)
    for f in range(5):
        faces[0, f] = own[f, 0]
        faces[1, f] = own[f, 31]
        for side in range(2):
            faces[2 + side, f] = pack_y(flat, f * 256, side)
    packed = pack_z_faces(own, 0)
    for side in range(2):
        for f in range(5):
            faces[4 + side, f] = packed[side * 5 + f]

    mine = [neighbours[f, 0, slab] for f in range(6)]
    ghost_copies = []
    for turn in range(32):
        there = slab ^ turn
        patch = partner[0, there]
        which = jnp.int32(0)
        for f in range(1, 6):
            which = jnp.where(mine[f] == patch, f, which)
        target = messages if turn else landed
        for f in range(5):
            target[turn, f] = faces[which, f]
        if turn:
            copy = pltpu.make_async_remote_copy(
                src_ref=messages.at[turn], dst_ref=landed.at[turn],
                send_sem=ghost_send.at[turn], recv_sem=ghost_recv.at[turn],
                device_id=(there, lvl), device_id_type=MESH,
            )
            copy.start()
            ghost_copies.append(copy)
    for piece in range(FIRST, CHUNKS):
        send(piece)

    for copy in coarse_loads:
        copy.wait()
    for f in range(5):
        coarse_state[f, 0] = coarse_state[f, 1]
        coarse_state[f, 33] = coarse_state[f, 32]

    def coarse_update(x, cells, prims, change):
        for d, kept in ((1, flux_y), (2, flux_z)):

            def border(flux, speed, d=d):
                return [cells[1 + d]] + [2.0 * v for v in flux]

            part, values = across(cells, prims, d, border)
            change = [change[i] + part[i] for i in range(5)]
            for i in range(5):
                kept[i, x] = values[i]
        return [cells[i] - COARSE_STEP * change[i] for i in range(5)]

    lowest = lowest_interface(coarse_state)

    def coarse_chunk(c, below):
        return tuple(advance(coarse_state, 1 + c * CHUNK, CHUNK, below, coarse_update))

    highest = lax.fori_loop(0, COARSE_BREAK, coarse_chunk, tuple(lowest))
    forward(0)
    highest = lax.fori_loop(COARSE_BREAK, CHUNKS, coarse_chunk, highest)
    for i in range(5):
        flux_x[0, i] = lowest[i]
        flux_x[1, i] = highest[i]

    code = link[0, 0]
    valid = code >= 0
    level = jnp.maximum(code, 0) // 24
    face = jnp.maximum(code, 0) % 24 // 4
    quarter = jnp.maximum(code, 0) % 4
    direction, side = face // 2, face % 2
    quarter_row = jnp.where(direction == 2, quarter % 2, quarter // 2)
    quarter_col = jnp.where(direction == 2, quarter // 2, quarter % 2)

    source = partner[0, slab]
    apart = source ^ slab
    chosen = jnp.int32(0)
    for bit in range(5):
        chosen = chosen + (apart >= (1 << bit)).astype(jnp.int32)
    linked = [neighbours[f, 0, source] for f in range(6)]
    present = [linked[f] >= 0 for f in range(6)]
    count = work[0, source]
    steps = jnp.full(TILE, count.astype(F32), F32)
    ratio = 2.0 * COARSE_STEP / steps
    share = 1.0 / steps

    def choose(piece):
        for n in range(CHUNK):
            x = piece * CHUNK + n
            for f in range(5):
                value = held[0, f, x]
                for k in range(1, 6):
                    value = jnp.where(chosen == k, held[k, f, x], value)
                state[f, x + 1] = value

    def spread(x):
        cells = load_plane(state, x + 1)
        for d, spreader, outer in ((1, spread_y, outer_y), (2, spread_z, outer_z)):
            lower = rows() < 4 if d == 1 else lanes() % 32 < 16
            values = []
            for f in range(5):
                low = jnp.where(present[2 * d], spreader(ghosts.at[2 * d], f, x, 0), cells[f])
                high = jnp.where(present[2 * d + 1], spreader(ghosts.at[2 * d + 1], f, x, 1), cells[f])
                values.append(jnp.where(lower, low, high))
            flux, speed = half_flux(values, primitives(values), d)
            for i, v in enumerate(values + flux + [speed]):
                outer[i, x] = v

    def updater(substep):
        active = substep < count

        def update(x, cells, prims, change):
            borders = []
            for d, outer in ((1, outer_y), (2, outer_z)):

                def border(flux, speed, d=d, outer=outer):
                    return interface(
                        cells, flux, speed, [outer[i, x] for i in range(5)],
                        [outer[5 + i, x] for i in range(4)], outer[9, x], d, face_sign(d),
                    )

                part, values = across(cells, prims, d, border)
                borders.append(values)
                change = [change[i] + part[i] for i in range(5)]
            for i in range(5):
                value = jnp.where(direction == 1, borders[0][i], borders[1][i])
                value = jnp.where(active, value * share, 0.0)
                register[i, x] = value if substep == 0 else register[i, x] + value
            return [jnp.where(active, cells[i] - ratio * change[i], cells[i]) for i in range(5)]

        return update

    def outermost(substep, wanted, values):
        for i in range(5):
            value = jnp.where((substep < count) & (side == wanted), values[i] * share, 0.0)
            x_register[i] = value if substep == 0 and wanted == 0 else x_register[i] + value

    def pack_register(first, planes):
        for f in range(5):
            value = packed_z[f]
            for n in range(planes):
                value = pack_z(register[f, first + n], first + n, side, value)
            packed_z[f] = value

    def stores_of(piece):
        first = pl.multiple_of(piece * 8, 8)
        return [
            pltpu.make_async_copy(
                state.at[:, pl.ds(first + 1, 8), j, :],
                fine_out.at[0, 0, :, pl.ds(first, 8), pl.ds(j * 128, 128)],
                store_sem.at[piece, j],
            )
            for j in range(8)
        ]

    forward(1)
    for copy in ghost_copies:
        copy.wait_recv()
    for f in range(6):
        turn = jnp.maximum(linked[f], 0) ^ slab
        for i in range(5):
            ghosts[f, i] = landed[turn, i]
    arrive(0)
    choose(0)
    for f in range(5):
        state[f, 0] = jnp.where(present[0], ghosts[0, f], state[f, 1])
        packed_z[f] = jnp.zeros(TILE, F32)
    for x in range(CHUNK - 1):
        spread(x)
    for substep in range(4):
        lowest = lowest_interface(state)
        outermost(substep, 0, lowest)
        reach = CHUNK - 1 - substep
        below = advance(state, 1, reach, lowest, updater(substep)) if reach > 0 else lowest
        for i in range(5):
            carry[substep, i] = below[i]

    def wave(c, _):
        @pl.when(c < CHUNKS - 1)
        def _():
            forward(c + 1)

        arrive(c)
        choose(c)
        for n in range(CHUNK):
            spread(c * CHUNK - 1 + n)
        for substep in range(4):
            below = [carry[substep, i] for i in range(5)]
            below = advance(state, c * CHUNK - substep, CHUNK, below, updater(substep))
            for i in range(5):
                carry[substep, i] = below[i]
        pack_register((c - 1) * CHUNK, CHUNK)

        @pl.when(c % 2 == 0)
        def _():
            for copy in stores_of(c // 2 - 1):
                copy.start()

        return 0

    lax.fori_loop(1, CHUNKS, wave, 0)
    for f in range(5):
        state[f, 33] = jnp.where(present[1], ghosts[1, f], state[f, 32])
    spread(31)
    for substep in range(4):
        below = [carry[substep, i] for i in range(5)]
        outermost(substep, 1, advance(state, 32 - substep, substep + 1, below, updater(substep)))
    pack_register(32 - CHUNK, CHUNK)

    flat = register.reshape(5 * 32 * 8, 128)
    source_lane = lax.broadcasted_iota(jnp.int32, (128, 128), 0)
    target_lane = lax.broadcasted_iota(jnp.int32, (128, 128), 1)
    wanted = target_lane // 32 * 64 + target_lane % 32 * 2
    squeeze = ((source_lane == wanted) & (target_lane % 32 < 16) & (target_lane < 64)).astype(F32)
    for f in range(5):
        value = jnp.where(direction == 1, pack_y(flat, f * 256, side), packed_z[f])
        value = jnp.where(direction == 0, x_register[f], value)
        value = value + pltpu.roll(value, 127, 1)
        squeezed[pl.ds(f * 8, 8), :] = 0.25 * (value + pltpu.roll(value, 96, 1))
    squeezed[...] = jnp.dot(
        squeezed[...], squeeze, precision=lax.Precision.HIGHEST, preferred_element_type=F32
    )
    low_lanes = lax.broadcasted_iota(jnp.int32, (4, 128), 1) < 64
    for f in range(5):
        even = squeezed[pl.ds(f * 8, 4, stride=2), :]
        odd = squeezed[pl.ds(f * 8 + 1, 4, stride=2), :]
        small = jnp.where(low_lanes, even, pltpu.roll(odd, 64, 1))
        small = jnp.where(quarter_col == 0, small, pltpu.roll(small, 16, 1))
        note[f, pl.ds(0, 4), :] = jnp.where(quarter_row == 0, small, 0.0)
        note[f, pl.ds(4, 4), :] = jnp.where(quarter_row == 1, small, 0.0)
    place = level * 6 + (face ^ 1) + 1
    inside = (rows() // 4 == quarter_row) & (lanes() % 32 // 16 == quarter_col)
    note[5] = jnp.where(inside & valid, place.astype(F32), 0.0)
    note_copies = []
    for turn in range(1, 4):
        copy = pltpu.make_async_remote_copy(
            src_ref=note, dst_ref=notes.at[turn - 1],
            send_sem=note_send.at[turn - 1], recv_sem=note_recv.at[turn - 1],
            device_id=(slab, lvl ^ turn), device_id_type=MESH,
        )
        copy.start()
        note_copies.append(copy)
    for copy in stores_of(3):
        copy.start()

    for copy in ghost_copies:
        copy.wait_send()
    for piece in range(CHUNKS):
        for axis in range(2):
            near(axis, piece).wait_send()
            far(axis, piece).wait_send()
        up(piece).wait_send()
        on(piece).wait_send()

    for copy in note_copies:
        copy.wait_recv()
    for g in range(6):
        key = (lvl * 6 + g + 1).astype(F32)
        parts = [note if n == 3 else notes.at[n] for n in range(4)]
        hits = [part[5] == key for part in parts]
        for f in range(5):
            total = jnp.zeros(TILE, F32)
            for n in range(4):
                total = total + jnp.where(hits[n], parts[n][f], 0.0)
            totals[g, f] = total
        cover = jnp.zeros(TILE, F32)
        for n in range(4):
            cover = cover + jnp.where(hits[n], 1.0, 0.0)
        totals[g, 5] = cover

    for end, x in ((0, 1), (1, 32)):
        for f in range(5):
            amount = totals[end, 5] * flux_x[end, f] - totals[end, f]
            coarse_state[f, x] = coarse_state[f, x] + (COARSE_STEP if end else -COARSE_STEP) * amount

    def correct(x):
        cells = load_plane(coarse_state, x + 1)
        for d, spreader, kept in ((1, spread_y, flux_y), (2, spread_z, flux_z)):
            lower, upper = edge_masks(d)
            weight = COARSE_STEP * face_sign(d) * (lower | upper).astype(F32)

            def both(f, d=d, spreader=spreader, upper=upper):
                low = spreader(totals.at[2 * d], f, x, 0)
                high = spreader(totals.at[2 * d + 1], f, x, 1)
                return jnp.where(upper, high, low)

            cover = both(5)
            for f in range(5):
                cells[f] = cells[f] + weight * (cover * kept[f, x] - both(f))
        for f in range(5):
            coarse_state[f, x + 1] = cells[f]

    def coarse_stores_of(piece):
        first = pl.multiple_of(piece * 8, 8)
        return [
            pltpu.make_async_copy(
                coarse_state.at[:, pl.ds(first + 1, 8), j, :],
                coarse_out.at[0, 0, :, pl.ds(first, 8), pl.ds(j * 128, 128)],
                coarse_store_sem.at[piece, j],
            )
            for j in range(8)
        ]

    def correct_eight(piece, _):
        for n in range(8):
            correct(piece * 8 + n)
        for copy in coarse_stores_of(piece):
            copy.start()
        return 0

    lax.fori_loop(0, 4, correct_eight, 0)
    for copy in note_copies:
        copy.wait_send()
    for piece in range(4):
        for copy in stores_of(piece) + coarse_stores_of(piece):
            copy.wait()


def write_kernel(fine_result, coarse_result, fine_out, coarse_out, sem):
    copies = [
        pltpu.make_async_copy(source.at[0, 0, f], target.at[0, 0, f], sem.at[n, f])
        for n, (source, target) in enumerate(((fine_result, fine_out), (coarse_result, coarse_out)))
        for f in range(5)
    ]
    for copy in copies:
        copy.start()
    for copy in copies:
        copy.wait()


SMEM = pl.BlockSpec(memory_space=pltpu.SMEM)
HBM = pl.BlockSpec(memory_space=pltpu.HBM)
DMA = pltpu.SemaphoreType.DMA
LIMIT = 60 * 1024 * 1024


def step(partner, neighbours, work, link, fine_state, coarse_state):
    return pl.pallas_call(
        step_kernel,
        out_shape=(jax.ShapeDtypeStruct(fine_state.shape, F32), jax.ShapeDtypeStruct(coarse_state.shape, F32)),
        in_specs=[SMEM, SMEM, SMEM, SMEM, HBM, HBM],
        out_specs=(HBM, HBM),
        scratch_shapes=[
            pltpu.VMEM((6, *PATCH), F32),
            pltpu.VMEM(PATCH, F32),
            pltpu.VMEM((6, 5, *TILE), F32),
            pltpu.VMEM((32, 5, *TILE), F32),
            pltpu.VMEM((32, 5, *TILE), F32),
            pltpu.VMEM((6, 5, *TILE), F32),
            pltpu.VMEM((5, 34, *TILE), F32),
            pltpu.VMEM((10, 32, *TILE), F32),
            pltpu.VMEM((10, 32, *TILE), F32),
            pltpu.VMEM(PATCH, F32),
            pltpu.VMEM((5, *TILE), F32),
            pltpu.VMEM((5, *TILE), F32),
            pltpu.VMEM((4, 5, *TILE), F32),
            pltpu.VMEM((40, 128), F32),
            pltpu.VMEM((5, 34, *TILE), F32),
            pltpu.VMEM(PATCH, F32),
            pltpu.VMEM(PATCH, F32),
            pltpu.VMEM((2, 5, *TILE), F32),
            pltpu.VMEM((6, *TILE), F32),
            pltpu.VMEM((3, 6, *TILE), F32),
            pltpu.VMEM((6, 6, *TILE), F32),
            DMA((8,)), DMA((8,)), DMA((4, 8)), DMA((4, 8)), DMA((32,)), DMA((32,)), DMA((3,)), DMA((3,)),
            DMA((2, CHUNKS)), DMA((2, CHUNKS)), DMA((2, CHUNKS)), DMA((2, CHUNKS)),
            DMA((CHUNKS,)), DMA((CHUNKS,)), DMA((CHUNKS,)), DMA((CHUNKS,)),
        ],
        compiler_params=pltpu.CompilerParams(collective_id=0, has_side_effects=True, vmem_limit_bytes=LIMIT),
        name="step",
    )(partner, neighbours, work, link, fine_state, coarse_state)


def write(fine_result, coarse_result):
    return pl.pallas_call(
        write_kernel,
        out_shape=tuple(jax.ShapeDtypeStruct(v.shape, F32) for v in (fine_result, coarse_result)),
        in_specs=[HBM, HBM],
        out_specs=(HBM, HBM),
        scratch_shapes=[DMA((2, 5))],
        compiler_params=pltpu.CompilerParams(vmem_limit_bytes=LIMIT),
        name="write",
    )(fine_result, coarse_result)


def body(fine_state, coarse_state, partner, mig_slot, neighbours, work, coarse_link):
    del mig_slot
    results = step(
        partner.T, jnp.transpose(neighbours, (2, 1, 0)), work.T, coarse_link, fine_state, coarse_state
    )
    return write(*results)


def solution(mesh):
    return jax.shard_map(
        body,
        mesh=mesh,
        in_specs=(
            P("slab", "lvl", None, None, None),
            P("slab", "lvl", None, None, None),
            P(None, "lvl"),
            P(None, "lvl"),
            P(None, "lvl", None),
            P(None, "lvl"),
            P("slab", "lvl"),
        ),
        out_specs=(P("slab", "lvl", None, None, None), P("slab", "lvl", None, None, None)),
        check_vma=False,
    )
```

```python
import jax
import jax.numpy as jnp
from jax import lax
from jax.experimental import pallas as pl
from jax.experimental.pallas import tpu as pltpu
from jax.sharding import PartitionSpec as P

MESH = pl.DeviceIdType.MESH
F32 = jnp.float32
COARSE_STEP = 0.035
TILE = (8, 128)
PATCH = (5, 32, 8, 128)
CHUNK = 4
CHUNKS = 32 // CHUNK
PIECE = 2
PIECES = 32 // PIECE
FIRST = 2
QUEUE = 4
BESIDE = 4
AHEAD = 4


def lanes():
    return lax.broadcasted_iota(jnp.int32, TILE, 1)


def rows():
    return lax.broadcasted_iota(jnp.int32, TILE, 0)


def primitives(cells):
    density, mom_x, mom_y, mom_z, energy = cells
    inverse = 1.0 / density
    vel = [mom_x * inverse, mom_y * inverse, mom_z * inverse]
    kinetic = 0.5 * (mom_x * vel[0] + mom_y * vel[1] + mom_z * vel[2])
    pressure = 0.4 * (energy - kinetic)
    half_sound = 0.5 * jnp.sqrt(1.4 * pressure * inverse)
    return (*vel, pressure, half_sound)


def half_flux(cells, prims, direction):
    half_normal = 0.5 * prims[direction]
    pressure, half_sound = prims[3], prims[4]
    flux = [cells[1 + i] * half_normal for i in range(3)]
    flux[direction] = flux[direction] + 0.5 * pressure
    flux.append((cells[4] + pressure) * half_normal)
    return flux, jnp.abs(half_normal) + half_sound


def interface(low, low_flux, low_speed, high, high_flux, high_speed, direction, sign=None):
    fastest = jnp.maximum(low_speed, high_speed)
    if sign is not None:
        fastest = fastest * sign
    out = [0.5 * (low[1 + direction] + high[1 + direction]) - fastest * (high[0] - low[0])]
    for i in range(4):
        out.append((low_flux[i] + high_flux[i]) - fastest * (high[1 + i] - low[1 + i]))
    return out


def z_up(v):
    return pltpu.roll(v, 127, 1)


def z_down(v):
    return pltpu.roll(v, 1, 1)


def y_up(v):
    return pltpu.roll(jnp.where(lanes() < 32, pltpu.roll(v, 7, 0), v), 96, 1)


def y_down(v):
    return pltpu.roll(jnp.where(lanes() >= 96, pltpu.roll(v, 1, 0), v), 32, 1)


def edge_masks(direction):
    if direction == 1:
        return (rows() == 0) & (lanes() < 32), (rows() == 7) & (lanes() >= 96)
    return lanes() % 32 == 0, lanes() % 32 == 31


def face_sign(direction):
    lower = rows() < 4 if direction == 1 else lanes() % 32 < 16
    return jnp.where(lower, -1.0, 1.0).astype(F32)


def across(cells, prims, direction, outer):
    up, down = (y_up, y_down) if direction == 1 else (z_up, z_down)
    flux, speed = half_flux(cells, prims, direction)
    inner = interface(
        cells, flux, speed, [up(v) for v in cells], [up(v) for v in flux], up(speed), direction
    )
    border = outer(flux, speed)
    lower, upper = edge_masks(direction)
    change = [
        jnp.where(upper, border[i], inner[i]) - jnp.where(lower, border[i], down(inner[i])) for i in range(5)
    ]
    return change, border


def each(first, last, act):
    def one(i, _):
        act(i)
        return 0

    lax.fori_loop(first, last, one, 0)


def load_plane(ref, x):
    return [ref[f, x] for f in range(5)]


def prepare(state, x):
    cells = load_plane(state, x)
    prims = primitives(cells)
    flux, speed = half_flux(cells, prims, 0)
    return cells, prims, flux, speed


def lowest_interface(state):
    ghost, _, ghost_flux, ghost_speed = prepare(state, 0)
    first, _, flux, speed = prepare(state, 1)
    return interface(ghost, ghost_flux, ghost_speed, first, flux, speed, 0)


def advance(state, first, count, below, update):
    cells, prims, flux, speed = prepare(state, first)
    for n in range(count):
        after = prepare(state, first + n + 1)
        above = interface(cells, flux, speed, after[0], after[2], after[3], 0)
        new = update(first + n - 1, cells, prims, [above[i] - below[i] for i in range(5)])
        for f in range(5):
            state[f, first + n] = new[f]
        cells, prims, flux, speed = after
        below = above
    return below


def pack_y(flat, first, side):
    out = None
    for g in range(4):
        part = flat[pl.ds(first + g * 8 + 7 * side, 8, stride=32), :]
        part = pltpu.roll(part, (32 * g - 96 * side) % 128, 1)
        out = part if g == 0 else jnp.where(lanes() // 32 == g, part, out)
    return out


def pack_z(plane, x, side, out):
    return jnp.where(lanes() % 32 == x, pltpu.roll(plane, (x + 128 - 31 * side) % 128, 1), out)


def pack_z_faces(ref, first):
    def pack(x, carried):
        return tuple(
            pack_z(ref[f, first + x], x, side, carried[side * 5 + f]) for side in range(2) for f in range(5)
        )

    return lax.fori_loop(0, 32, pack, (jnp.zeros(TILE, F32),) * 10, unroll=4)


def spread_y(face, field, x, side):
    row = jnp.broadcast_to(face[field, pl.ds(x // 4, 1), :], TILE)
    shift = (3 - x % 4) * 32 if side else (4 - x % 4) * 32
    return pltpu.roll(row, shift % 128, 1)


def spread_z(face, field, x, side):
    return pltpu.roll(face[field], (128 - x + 31 * side) % 128, 1)


def step_kernel(
    partner, neighbours, work, link, fine, coarse, fine_out, coarse_out, amounts,
    held, relay, faces, messages, landed, ghosts,
    state, outer_y, outer_z, register, x_register, packed_z, carry, squeezed,
    coarse_state, flux_y, flux_z, flux_faces, note, notes,
    load_sem, coarse_sem, store_sem, coarse_store_sem, ghost_send, ghost_recv, note_send, note_recv,
    near_send, near_recv, far_send, far_recv, up_send, up_recv, on_send, on_recv,
):
    slab = lax.axis_index("slab")
    lvl = lax.axis_index("lvl")
    other_lvl = lvl ^ 2
    own = held.at[0]

    def loads_of(source, target, sem):
        return [
            pltpu.make_async_copy(source.at[0, 0, :, :, pl.ds(j * 128, 128)], target.at[:, :, j, :], sem.at[j])
            for j in range(8)
        ]

    fine_loads = loads_of(fine, own, load_sem)
    coarse_loads = loads_of(coarse, coarse_state.at[:, pl.ds(1, 32)], coarse_sem)
    for copy in fine_loads + coarse_loads:
        copy.start()

    barrier = pltpu.get_barrier_semaphore()

    def greet(device):
        pl.semaphore_signal(barrier, inc=1, device_id=device, device_id_type=MESH)

    each(1, 32, lambda turn: greet((slab ^ turn, lvl)))
    each(1, 4, lambda turn: greet((slab, lvl ^ turn)))
    greet((slab ^ 16, other_lvl))

    def span(ref, piece):
        return ref.at[:, pl.ds(piece * PIECE, PIECE)]

    def near(axis, piece):
        return pltpu.make_async_remote_copy(
            src_ref=span(own, piece), dst_ref=span(held.at[1 + 2 * axis], piece),
            send_sem=near_send.at[axis, piece], recv_sem=near_recv.at[axis, piece],
            device_id=(slab ^ (4 if axis else 1), lvl), device_id_type=MESH,
        )

    def far(axis, piece):
        return pltpu.make_async_remote_copy(
            src_ref=span(held.at[1 + 2 * axis], piece), dst_ref=span(held.at[2 + 2 * axis], piece),
            send_sem=far_send.at[axis, piece], recv_sem=far_recv.at[axis, piece],
            device_id=(slab ^ (12 if axis else 3), lvl), device_id_type=MESH,
        )

    def up(piece):
        return pltpu.make_async_remote_copy(
            src_ref=span(own, piece), dst_ref=span(relay, piece),
            send_sem=up_send.at[piece], recv_sem=up_recv.at[piece],
            device_id=(slab ^ (piece % 2 * 16), other_lvl), device_id_type=MESH,
        )

    def on(piece):
        return pltpu.make_async_remote_copy(
            src_ref=span(relay, piece), dst_ref=span(held.at[5], piece),
            send_sem=on_send.at[piece], recv_sem=on_recv.at[piece],
            device_id=(slab ^ ((piece + 1) % 2 * 16), other_lvl), device_id_type=MESH,
        )

    def send(piece):
        near(0, piece).start()
        near(1, piece).start()
        up(piece).start()

    def forward(piece):
        for axis in range(2):
            near(axis, piece).wait_recv()
            far(axis, piece).start()
        up(piece).wait_recv()
        on(piece).start()

    def relay_on(piece):
        forward(piece)

        @pl.when(piece + QUEUE < PIECES)
        def _():
            send(piece + QUEUE)

    def arrive(piece):
        far(0, piece).wait_recv()
        far(1, piece).wait_recv()
        on(piece).wait_recv()

    for copy in fine_loads:
        copy.wait()
    pl.semaphore_wait(barrier, 35)
    each(0, FIRST, send)

    flat = own.reshape(5 * 32 * 8, 128)
    for f in range(5):
        faces[0, f] = own[f, 0]
        faces[1, f] = own[f, 31]
        for side in range(2):
            faces[2 + side, f] = pack_y(flat, f * 256, side)
    packed = pack_z_faces(own, 0)
    for side in range(2):
        for f in range(5):
            faces[4 + side, f] = packed[side * 5 + f]

    mine = [neighbours[f, 0, slab] for f in range(6)]

    def compose(turn, target):
        patch = partner[0, slab ^ turn]
        which = jnp.int32(0)
        for f in range(1, 6):
            which = jnp.where(mine[f] == patch, f, which)
        for f in range(5):
            target[turn, f] = faces[which, f]

    def ghost(turn):
        return pltpu.make_async_remote_copy(
            src_ref=messages.at[turn], dst_ref=landed.at[turn],
            send_sem=ghost_send.at[turn], recv_sem=ghost_recv.at[turn],
            device_id=(slab ^ turn, lvl), device_id_type=MESH,
        )

    def send_ghost(turn):
        compose(turn, messages)
        ghost(turn).start()

    compose(0, landed)
    each(1, 32, send_ghost)
    each(FIRST, QUEUE, send)

    for copy in coarse_loads:
        copy.wait()
    for f in range(5):
        coarse_state[f, 0] = coarse_state[f, 1]
        coarse_state[f, 33] = coarse_state[f, 32]

    def coarse_update(x, cells, prims, change):
        for d, kept in ((1, flux_y), (2, flux_z)):

            def border(flux, speed, d=d):
                return [cells[1 + d]] + [2.0 * v for v in flux]

            part, values = across(cells, prims, d, border)
            change = [change[i] + part[i] for i in range(5)]
            for i in range(5):
                kept[i, x] = values[i]
        return [cells[i] - COARSE_STEP * change[i] for i in range(5)]

    lowest = lowest_interface(coarse_state)

    def coarse_chunk(c, below):
        return tuple(advance(coarse_state, 1 + c * CHUNK, CHUNK, below, coarse_update))


    def coarse_part(n, below):
        below = lax.fori_loop(n * CHUNKS // BESIDE, (n + 1) * CHUNKS // BESIDE, coarse_chunk, below)
        relay_on(n)
        return below

    highest = lax.fori_loop(0, BESIDE, coarse_part, tuple(lowest))
    coarse_store = pltpu.make_async_copy(coarse_state.at[:, pl.ds(1, 32)], coarse_out, coarse_store_sem)
    coarse_store.start()
    for f in range(5):
        flux_faces[0, f] = lowest[f]
        flux_faces[1, f] = highest[f]
        for end in range(2):
            flux_faces[2 + end, f] = pack_y(flux_y.reshape(5 * 32 * 8, 128), f * 256, end)
    packed = pack_z_faces(flux_z, 0)
    for end in range(2):
        for f in range(5):
            flux_faces[4 + end, f] = packed[end * 5 + f]

    code = link[0, 0]
    valid = code >= 0
    level = jnp.maximum(code, 0) // 24
    face = jnp.maximum(code, 0) % 24 // 4
    quarter = jnp.maximum(code, 0) % 4
    direction, side = face // 2, face % 2
    quarter_row = jnp.where(direction == 2, quarter % 2, quarter // 2)
    quarter_col = jnp.where(direction == 2, quarter // 2, quarter % 2)

    source = partner[0, slab]
    apart = source ^ slab
    chosen = jnp.int32(0)
    for bit in range(5):
        chosen = chosen + (apart >= (1 << bit)).astype(jnp.int32)
    linked = [neighbours[f, 0, source] for f in range(6)]
    present = [linked[f] >= 0 for f in range(6)]
    count = work[0, source]
    steps = jnp.full(TILE, count.astype(F32), F32)
    ratio = 2.0 * COARSE_STEP / steps
    share = 1.0 / steps

    def choose(first, planes):
        for n in range(planes):
            for f in range(5):
                value = held[0, f, first + n]
                for k in range(1, 6):
                    value = jnp.where(chosen == k, held[k, f, first + n], value)
                state[f, first + n + 1] = value

    def spread(x):
        cells = load_plane(state, x + 1)
        for d, spreader, outer in ((1, spread_y, outer_y), (2, spread_z, outer_z)):
            lower = rows() < 4 if d == 1 else lanes() % 32 < 16
            values = []
            for f in range(5):
                low = jnp.where(present[2 * d], spreader(ghosts.at[2 * d], f, x, 0), cells[f])
                high = jnp.where(present[2 * d + 1], spreader(ghosts.at[2 * d + 1], f, x, 1), cells[f])
                values.append(jnp.where(lower, low, high))
            flux, speed = half_flux(values, primitives(values), d)
            for i, v in enumerate(values + flux + [speed]):
                outer[i, x] = v

    def updater(substep):
        active = substep < count

        def update(x, cells, prims, change):
            borders = []
            for d, outer in ((1, outer_y), (2, outer_z)):

                def border(flux, speed, d=d, outer=outer):
                    return interface(
                        cells, flux, speed, [outer[i, x] for i in range(5)],
                        [outer[5 + i, x] for i in range(4)], outer[9, x], d, face_sign(d),
                    )

                part, values = across(cells, prims, d, border)
                borders.append(values)
                change = [change[i] + part[i] for i in range(5)]
            for i in range(5):
                value = jnp.where(direction == 1, borders[0][i], borders[1][i])
                value = jnp.where(active, value * share, 0.0)
                register[i, x] = value if substep == 0 else register[i, x] + value
            return [jnp.where(active, cells[i] - ratio * change[i], cells[i]) for i in range(5)]

        return update

    def outermost(substep, wanted, values):
        for i in range(5):
            value = jnp.where((substep < count) & (side == wanted), values[i] * share, 0.0)
            x_register[i] = value if substep == 0 and wanted == 0 else x_register[i] + value

    def pack_register(first, planes):
        for f in range(5):
            value = packed_z[f]
            for n in range(planes):
                value = pack_z(register[f, first + n], first + n, side, value)
            packed_z[f] = value

    def stores_of(piece):
        first = pl.multiple_of(piece * 8, 8)
        return [
            pltpu.make_async_copy(
                state.at[:, pl.ds(first + 1, 8), j, :],
                fine_out.at[0, 0, :, pl.ds(first, 8), pl.ds(j * 128, 128)],
                store_sem.at[piece, j],
            )
            for j in range(8)
        ]

    each(BESIDE, CHUNK // PIECE + AHEAD, relay_on)
    each(1, 32, lambda turn: ghost(turn).wait_recv())
    for f in range(6):
        turn = jnp.maximum(linked[f], 0) ^ slab
        for i in range(5):
            ghosts[f, i] = landed[turn, i]
    for piece in range(CHUNK // PIECE):
        arrive(piece)
    choose(0, CHUNK)
    for f in range(5):
        state[f, 0] = jnp.where(present[0], ghosts[0, f], state[f, 1])
        packed_z[f] = jnp.zeros(TILE, F32)
    for x in range(CHUNK - 1):
        spread(x)
    for substep in range(4):
        lowest = lowest_interface(state)
        outermost(substep, 0, lowest)
        reach = CHUNK - 1 - substep
        below = advance(state, 1, reach, lowest, updater(substep)) if reach > 0 else lowest
        for i in range(5):
            carry[substep, i] = below[i]

    def follow(first, planes):
        for n in range(planes // PIECE):
            arrive(first // PIECE + n)
        choose(first, planes)
        for n in range(planes):
            spread(first - 1 + n)
        for substep in range(4):
            below = [carry[substep, i] for i in range(5)]
            below = advance(state, first - substep, planes, below, updater(substep))
            for i in range(5):
                carry[substep, i] = below[i]

    def wave(c, _):
        for n in range(CHUNK // PIECE):
            piece = c * (CHUNK // PIECE) + AHEAD + n

            @pl.when(piece < PIECES)
            def _(piece=piece):
                relay_on(piece)

        follow(c * CHUNK, CHUNK)
        pack_register((c - 1) * CHUNK, CHUNK)

        @pl.when(c % 2 == 0)
        def _():
            for copy in stores_of(c // 2 - 1):
                copy.start()

        return 0

    lax.fori_loop(1, CHUNKS - 1, wave, 0)
    each(0, CHUNK // PIECE, lambda n: follow(32 - CHUNK + n * PIECE, PIECE))
    pack_register(32 - 2 * CHUNK, CHUNK)
    for f in range(5):
        state[f, 33] = jnp.where(present[1], ghosts[1, f], state[f, 32])
    spread(31)
    for substep in range(4):
        below = [carry[substep, i] for i in range(5)]
        outermost(substep, 1, advance(state, 32 - substep, substep + 1, below, updater(substep)))
    pack_register(32 - CHUNK, CHUNK)

    flat = register.reshape(5 * 32 * 8, 128)
    source_lane = lax.broadcasted_iota(jnp.int32, (128, 128), 0)
    target_lane = lax.broadcasted_iota(jnp.int32, (128, 128), 1)
    wanted = target_lane // 32 * 64 + target_lane % 32 * 2
    squeeze = ((source_lane == wanted) & (target_lane % 32 < 16) & (target_lane < 64)).astype(F32)
    for f in range(5):
        value = jnp.where(direction == 1, pack_y(flat, f * 256, side), packed_z[f])
        value = jnp.where(direction == 0, x_register[f], value)
        value = value + pltpu.roll(value, 127, 1)
        squeezed[pl.ds(f * 8, 8), :] = 0.25 * (value + pltpu.roll(value, 96, 1))
    squeezed[...] = jnp.dot(
        squeezed[...], squeeze, precision=lax.Precision.HIGHEST, preferred_element_type=F32
    )
    low_lanes = lax.broadcasted_iota(jnp.int32, (4, 128), 1) < 64
    for f in range(5):
        even = squeezed[pl.ds(f * 8, 4, stride=2), :]
        odd = squeezed[pl.ds(f * 8 + 1, 4, stride=2), :]
        small = jnp.where(low_lanes, even, pltpu.roll(odd, 64, 1))
        small = jnp.where(quarter_col == 0, small, pltpu.roll(small, 16, 1))
        note[f, pl.ds(0, 4), :] = jnp.where(quarter_row == 0, small, 0.0)
        note[f, pl.ds(4, 4), :] = jnp.where(quarter_row == 1, small, 0.0)
    place = level * 6 + (face ^ 1) + 1
    inside = (rows() // 4 == quarter_row) & (lanes() % 32 // 16 == quarter_col)
    note[5] = jnp.where(inside & valid, place.astype(F32), 0.0)
    note_copies = []
    for turn in range(1, 4):
        copy = pltpu.make_async_remote_copy(
            src_ref=note, dst_ref=notes.at[turn - 1],
            send_sem=note_send.at[turn - 1], recv_sem=note_recv.at[turn - 1],
            device_id=(slab, lvl ^ turn), device_id_type=MESH,
        )
        copy.start()
        note_copies.append(copy)
    for copy in stores_of(3):
        copy.start()

    each(1, 32, lambda turn: ghost(turn).wait_send())

    def sent(piece):
        for axis in range(2):
            near(axis, piece).wait_send()
            far(axis, piece).wait_send()
        up(piece).wait_send()
        on(piece).wait_send()

    each(0, PIECES, sent)

    for copy in note_copies:
        copy.wait_recv()
    for g in range(6):
        key = (lvl * 6 + g + 1).astype(F32)
        parts = [note if n == 3 else notes.at[n] for n in range(4)]
        hits = [part[5] == key for part in parts]
        cover = jnp.zeros(TILE, F32)
        for n in range(4):
            cover = cover + jnp.where(hits[n], 1.0, 0.0)
        for f in range(5):
            total = jnp.zeros(TILE, F32)
            for n in range(4):
                total = total + jnp.where(hits[n], parts[n][f], 0.0)
            amounts[g, f] = (COARSE_STEP if g % 2 else -COARSE_STEP) * (cover * flux_faces[g, f] - total)
    for copy in note_copies:
        copy.wait_send()
    coarse_store.wait()

    def stored(piece):
        for copy in stores_of(piece):
            copy.wait()

    each(0, 4, stored)


def finish_kernel(fine, coarse, amounts, fine_out, coarse_out, fine_held, state, fine_sem, coarse_sem, out_sem):
    def load(n):
        planes = pl.ds(n * 8, 8)
        return pltpu.make_async_copy(coarse.at[:, planes], state.at[:, planes], coarse_sem.at[n])

    def store(n, j):
        first = pl.multiple_of(n * 8, 8)
        return pltpu.make_async_copy(
            state.at[:, pl.ds(first, 8), j, :],
            coarse_out.at[0, 0, :, pl.ds(first, 8), pl.ds(j * 128, 128)],
            out_sem.at[n, j],
        )

    def fine_load(f):
        return pltpu.make_async_copy(fine.at[0, 0, f], fine_held.at[f], fine_sem.at[f])

    def fine_store(f):
        return pltpu.make_async_copy(fine_held.at[f], fine_out.at[0, 0, f], fine_sem.at[5 + f])

    each(0, 4, lambda n: load(n).start())
    each(0, 5, lambda f: fine_load(f).start())

    def correct(x):
        cells = load_plane(state, x)
        for d, spreader in ((1, spread_y), (2, spread_z)):
            lower, upper = edge_masks(d)
            for f in range(5):
                low = jnp.where(lower, spreader(amounts.at[2 * d], f, x, 0), 0.0)
                cells[f] = cells[f] + jnp.where(upper, spreader(amounts.at[2 * d + 1], f, x, 1), low)
        for f in range(5):
            state[f, x] = cells[f]

    def correct_eight(n):
        load(n).wait()
        for end in range(2):

            @pl.when(n == end * 3)
            def _(end=end):
                for f in range(5):
                    state[f, 31 * end] = state[f, 31 * end] + amounts[end, f]

        def correct_four(half):
            for k in range(4):
                correct(n * 8 + half * 4 + k)

        each(0, 2, correct_four)
        for j in range(8):
            store(n, j).start()

    def pass_on(f):
        fine_load(f).wait()
        fine_store(f).start()

    correct_eight(0)
    each(0, 5, pass_on)
    each(1, 4, correct_eight)
    each(0, 5, lambda f: fine_store(f).wait())

    def stored(n):
        for j in range(8):
            store(n, j).wait()

    each(0, 4, stored)


SMEM = pl.BlockSpec(memory_space=pltpu.SMEM)
VMEM = pl.BlockSpec(memory_space=pltpu.VMEM)
HBM = pl.BlockSpec(memory_space=pltpu.HBM)
DMA = pltpu.SemaphoreType.DMA
LIMIT = 60 * 1024 * 1024


def step(partner, neighbours, work, link, fine_state, coarse_state):
    return pl.pallas_call(
        step_kernel,
        out_shape=(
            jax.ShapeDtypeStruct(fine_state.shape, F32),
            jax.ShapeDtypeStruct(PATCH, F32),
            jax.ShapeDtypeStruct((6, 5, *TILE), F32),
        ),
        in_specs=[SMEM, SMEM, SMEM, SMEM, HBM, HBM],
        out_specs=(HBM, HBM, VMEM),
        scratch_shapes=[
            pltpu.VMEM((6, *PATCH), F32),
            pltpu.VMEM(PATCH, F32),
            pltpu.VMEM((6, 5, *TILE), F32),
            pltpu.VMEM((32, 5, *TILE), F32),
            pltpu.VMEM((32, 5, *TILE), F32),
            pltpu.VMEM((6, 5, *TILE), F32),
            pltpu.VMEM((5, 34, *TILE), F32),
            pltpu.VMEM((10, 32, *TILE), F32),
            pltpu.VMEM((10, 32, *TILE), F32),
            pltpu.VMEM(PATCH, F32),
            pltpu.VMEM((5, *TILE), F32),
            pltpu.VMEM((5, *TILE), F32),
            pltpu.VMEM((4, 5, *TILE), F32),
            pltpu.VMEM((40, 128), F32),
            pltpu.VMEM((5, 34, *TILE), F32),
            pltpu.VMEM(PATCH, F32),
            pltpu.VMEM(PATCH, F32),
            pltpu.VMEM((6, 5, *TILE), F32),
            pltpu.VMEM((6, *TILE), F32),
            pltpu.VMEM((3, 6, *TILE), F32),
            DMA((8,)), DMA((8,)), DMA((4, 8)), DMA, DMA((32,)), DMA((32,)), DMA((3,)), DMA((3,)),
            DMA((2, PIECES)), DMA((2, PIECES)), DMA((2, PIECES)), DMA((2, PIECES)),
            DMA((PIECES,)), DMA((PIECES,)), DMA((PIECES,)), DMA((PIECES,)),
        ],
        compiler_params=pltpu.CompilerParams(collective_id=0, has_side_effects=True, vmem_limit_bytes=LIMIT),
        name="step",
    )(partner, neighbours, work, link, fine_state, coarse_state)


def finish(fine_result, coarse_result, amounts):
    shape = jax.ShapeDtypeStruct(fine_result.shape, F32)
    return pl.pallas_call(
        finish_kernel,
        out_shape=(shape, shape),
        in_specs=[HBM, HBM, VMEM],
        out_specs=(HBM, HBM),
        scratch_shapes=[
            pltpu.VMEM((5, 32, 1024), F32), pltpu.VMEM(PATCH, F32), DMA((10,)), DMA((4,)), DMA((4, 8)),
        ],
        compiler_params=pltpu.CompilerParams(vmem_limit_bytes=LIMIT),
        name="finish",
    )(fine_result, coarse_result, amounts)


def body(fine_state, coarse_state, partner, mig_slot, neighbours, work, coarse_link):
    del mig_slot
    results = step(
        partner.T, jnp.transpose(neighbours, (2, 1, 0)), work.T, coarse_link, fine_state, coarse_state
    )
    return finish(*results)


def solution(mesh):
    return jax.shard_map(
        body,
        mesh=mesh,
        in_specs=(
            P("slab", "lvl", None, None, None),
            P("slab", "lvl", None, None, None),
            P(None, "lvl"),
            P(None, "lvl"),
            P(None, "lvl", None),
            P(None, "lvl"),
            P("slab", "lvl"),
        ),
        out_specs=(P("slab", "lvl", None, None, None), P("slab", "lvl", None, None, None)),
        check_vma=False,
    )
```

```python
import jax
import jax.numpy as jnp
from jax import lax
from jax.experimental import pallas as pl
from jax.experimental.pallas import tpu as pltpu
from jax.sharding import PartitionSpec as P

MESH = pl.DeviceIdType.MESH
F32 = jnp.float32
COARSE_STEP = 0.035
TILE = (8, 128)
PATCH = (5, 32, 8, 128)
CHUNK = 4
CHUNKS = 32 // CHUNK
PIECE = 2
PIECES = 32 // PIECE
FIRST = 2
QUEUE = 4
BESIDE = 4
AHEAD = 4


def lanes():
    return lax.broadcasted_iota(jnp.int32, TILE, 1)


def rows():
    return lax.broadcasted_iota(jnp.int32, TILE, 0)


def primitives(cells):
    density, mom_x, mom_y, mom_z, energy = cells
    inverse = 1.0 / density
    vel = [mom_x * inverse, mom_y * inverse, mom_z * inverse]
    kinetic = 0.5 * (mom_x * vel[0] + mom_y * vel[1] + mom_z * vel[2])
    pressure = 0.4 * (energy - kinetic)
    half_sound = 0.5 * jnp.sqrt(1.4 * pressure * inverse)
    return (*vel, pressure, half_sound)


def half_flux(cells, prims, direction):
    half_normal = 0.5 * prims[direction]
    pressure, half_sound = prims[3], prims[4]
    flux = [cells[1 + i] * half_normal for i in range(3)]
    flux[direction] = flux[direction] + 0.5 * pressure
    flux.append((cells[4] + pressure) * half_normal)
    return flux, jnp.abs(half_normal) + half_sound


def interface(low, low_flux, low_speed, high, high_flux, high_speed, direction, sign=None):
    fastest = jnp.maximum(low_speed, high_speed)
    if sign is not None:
        fastest = fastest * sign
    out = [0.5 * (low[1 + direction] + high[1 + direction]) - fastest * (high[0] - low[0])]
    for i in range(4):
        out.append((low_flux[i] + high_flux[i]) - fastest * (high[1 + i] - low[1 + i]))
    return out


def z_up(v):
    return pltpu.roll(v, 127, 1)


def z_down(v):
    return pltpu.roll(v, 1, 1)


def y_up(v):
    return pltpu.roll(jnp.where(lanes() < 32, pltpu.roll(v, 7, 0), v), 96, 1)


def y_down(v):
    return pltpu.roll(jnp.where(lanes() >= 96, pltpu.roll(v, 1, 0), v), 32, 1)


def edge_masks(direction):
    if direction == 1:
        return (rows() == 0) & (lanes() < 32), (rows() == 7) & (lanes() >= 96)
    return lanes() % 32 == 0, lanes() % 32 == 31


def face_sign(direction):
    lower = rows() < 4 if direction == 1 else lanes() % 32 < 16
    return jnp.where(lower, -1.0, 1.0).astype(F32)


def across(cells, prims, direction, outer):
    up, down = (y_up, y_down) if direction == 1 else (z_up, z_down)
    flux, speed = half_flux(cells, prims, direction)
    inner = interface(
        cells, flux, speed, [up(v) for v in cells], [up(v) for v in flux], up(speed), direction
    )
    border = outer(flux, speed)
    lower, upper = edge_masks(direction)
    change = [
        jnp.where(upper, border[i], inner[i]) - jnp.where(lower, border[i], down(inner[i])) for i in range(5)
    ]
    return change, border


def each(first, last, act):
    def one(i, _):
        act(i)
        return 0

    lax.fori_loop(first, last, one, 0)


def wait_for(ref, sem):
    pltpu.make_async_copy(ref, ref, sem).wait()


def load_plane(ref, x):
    return [ref[f, x] for f in range(5)]


def prepare(state, x):
    cells = load_plane(state, x)
    prims = primitives(cells)
    flux, speed = half_flux(cells, prims, 0)
    return cells, prims, flux, speed


def lowest_interface(state):
    ghost, _, ghost_flux, ghost_speed = prepare(state, 0)
    first, _, flux, speed = prepare(state, 1)
    return interface(ghost, ghost_flux, ghost_speed, first, flux, speed, 0)


def advance(state, first, count, below, update):
    cells, prims, flux, speed = prepare(state, first)
    for n in range(count):
        after = prepare(state, first + n + 1)
        above = interface(cells, flux, speed, after[0], after[2], after[3], 0)
        new = update(first + n - 1, cells, prims, [above[i] - below[i] for i in range(5)])
        for f in range(5):
            state[f, first + n] = new[f]
        cells, prims, flux, speed = after
        below = above
    return below


def pack_y(flat, first, side):
    out = None
    for g in range(4):
        part = flat[pl.ds(first + g * 8 + 7 * side, 8, stride=32), :]
        part = pltpu.roll(part, (32 * g - 96 * side) % 128, 1)
        out = part if g == 0 else jnp.where(lanes() // 32 == g, part, out)
    return out


def pack_z(plane, x, side, out):
    return jnp.where(lanes() % 32 == x, pltpu.roll(plane, (x + 128 - 31 * side) % 128, 1), out)


def pack_z_faces(ref, first):
    def pack(x, carried):
        return tuple(
            pack_z(ref[f, first + x], x, side, carried[side * 5 + f]) for side in range(2) for f in range(5)
        )

    return lax.fori_loop(0, 32, pack, (jnp.zeros(TILE, F32),) * 10, unroll=4)


def spread_y(face, field, x, side):
    row = jnp.broadcast_to(face[field, pl.ds(x // 4, 1), :], TILE)
    shift = (3 - x % 4) * 32 if side else (4 - x % 4) * 32
    return pltpu.roll(row, shift % 128, 1)


def spread_z(face, field, x, side):
    return pltpu.roll(face[field], (128 - x + 31 * side) % 128, 1)


def step_kernel(
    partner, neighbours, work, link, fine, coarse, fine_out, coarse_out, amounts,
    held, relay, faces, messages, landed, ghosts,
    state, outer_y, outer_z, register, x_register, packed_z, carry, squeezed,
    coarse_state, flux_y, flux_z, flux_faces, note, notes,
    load_sem, coarse_sem, store_sem, coarse_store_sem, ghost_send, ghost_recv, note_send, note_recv,
    passed, reached, ended,
):
    slab = lax.axis_index("slab")
    lvl = lax.axis_index("lvl")
    other_lvl = lvl ^ 2
    own = held.at[0]

    def loads_of(source, target, sem):
        return [
            pltpu.make_async_copy(source.at[0, 0, :, :, pl.ds(j * 128, 128)], target.at[:, :, j, :], sem)
            for j in range(8)
        ]

    fine_loads = loads_of(fine, own, load_sem)
    coarse_loads = loads_of(coarse, coarse_state.at[:, pl.ds(1, 32)], coarse_sem)
    for copy in fine_loads + coarse_loads:
        copy.start()

    barrier = pltpu.get_barrier_semaphore()

    def greet(device):
        pl.semaphore_signal(barrier, inc=1, device_id=device, device_id_type=MESH)

    each(1, 32, lambda turn: greet((slab ^ turn, lvl)))
    each(1, 4, lambda turn: greet((slab, lvl ^ turn)))
    greet((slab ^ 16, other_lvl))

    def span(ref, piece):
        return ref.at[:, pl.ds(piece * PIECE, PIECE)]

    def near(axis, piece):
        return pltpu.make_async_remote_copy(
            src_ref=span(own, piece), dst_ref=span(held.at[1 + 2 * axis], piece),
            send_sem=passed, recv_sem=reached.at[piece],
            device_id=(slab ^ (4 if axis else 1), lvl), device_id_type=MESH,
        )

    def far(axis, piece):
        return pltpu.make_async_remote_copy(
            src_ref=span(held.at[1 + 2 * axis], piece), dst_ref=span(held.at[2 + 2 * axis], piece),
            send_sem=passed, recv_sem=ended.at[piece],
            device_id=(slab ^ (12 if axis else 3), lvl), device_id_type=MESH,
        )

    def up(piece):
        return pltpu.make_async_remote_copy(
            src_ref=span(own, piece), dst_ref=span(relay, piece),
            send_sem=passed, recv_sem=reached.at[piece],
            device_id=(slab ^ (piece % 2 * 16), other_lvl), device_id_type=MESH,
        )

    def on(piece):
        return pltpu.make_async_remote_copy(
            src_ref=span(relay, piece), dst_ref=span(held.at[5], piece),
            send_sem=passed, recv_sem=ended.at[piece],
            device_id=(slab ^ ((piece + 1) % 2 * 16), other_lvl), device_id_type=MESH,
        )

    def send(piece):
        near(0, piece).start()
        near(1, piece).start()
        up(piece).start()

    def three(piece):
        return held.at[pl.ds(0, 3), :, pl.ds(piece * PIECE, PIECE)]

    def forward(piece):
        wait_for(three(piece), reached.at[piece])
        far(0, piece).start()
        far(1, piece).start()
        on(piece).start()

    def relay_on(piece):
        forward(piece)

        @pl.when(piece + QUEUE < PIECES)
        def _():
            send(piece + QUEUE)

    def arrive(piece):
        wait_for(three(piece), ended.at[piece])

    wait_for(own, load_sem)
    pl.semaphore_wait(barrier, 35)
    each(0, FIRST, send)

    flat = own.reshape(5 * 32 * 8, 128)
    for f in range(5):
        faces[0, f] = own[f, 0]
        faces[1, f] = own[f, 31]
        for side in range(2):
            faces[2 + side, f] = pack_y(flat, f * 256, side)
    packed = pack_z_faces(own, 0)
    for side in range(2):
        for f in range(5):
            faces[4 + side, f] = packed[side * 5 + f]

    mine = [neighbours[f, 0, slab] for f in range(6)]

    def compose(turn, target):
        patch = partner[0, slab ^ turn]
        which = jnp.int32(0)
        for f in range(1, 6):
            which = jnp.where(mine[f] == patch, f, which)
        for f in range(5):
            target[turn, f] = faces[which, f]

    def ghost(turn):
        return pltpu.make_async_remote_copy(
            src_ref=messages.at[turn], dst_ref=landed.at[turn],
            send_sem=ghost_send, recv_sem=ghost_recv,
            device_id=(slab ^ turn, lvl), device_id_type=MESH,
        )

    def send_ghost(turn):
        compose(turn, messages)
        ghost(turn).start()

    compose(0, landed)
    each(1, 32, send_ghost)
    each(FIRST, QUEUE, send)

    wait_for(coarse_state.at[:, pl.ds(1, 32)], coarse_sem)
    for f in range(5):
        coarse_state[f, 0] = coarse_state[f, 1]
        coarse_state[f, 33] = coarse_state[f, 32]

    def coarse_update(x, cells, prims, change):
        for d, kept in ((1, flux_y), (2, flux_z)):

            def border(flux, speed, d=d):
                return [cells[1 + d]] + [2.0 * v for v in flux]

            part, values = across(cells, prims, d, border)
            change = [change[i] + part[i] for i in range(5)]
            for i in range(5):
                kept[i, x] = values[i]
        return [cells[i] - COARSE_STEP * change[i] for i in range(5)]

    lowest = lowest_interface(coarse_state)

    def coarse_chunk(c, below):
        return tuple(advance(coarse_state, 1 + c * CHUNK, CHUNK, below, coarse_update))


    def coarse_part(n, below):
        below = lax.fori_loop(n * CHUNKS // BESIDE, (n + 1) * CHUNKS // BESIDE, coarse_chunk, below)
        relay_on(n)
        return below

    highest = lax.fori_loop(0, BESIDE, coarse_part, tuple(lowest))
    coarse_store = pltpu.make_async_copy(coarse_state.at[:, pl.ds(1, 32)], coarse_out, coarse_store_sem)
    coarse_store.start()
    for f in range(5):
        flux_faces[0, f] = lowest[f]
        flux_faces[1, f] = highest[f]
        for end in range(2):
            flux_faces[2 + end, f] = pack_y(flux_y.reshape(5 * 32 * 8, 128), f * 256, end)
    packed = pack_z_faces(flux_z, 0)
    for end in range(2):
        for f in range(5):
            flux_faces[4 + end, f] = packed[end * 5 + f]

    code = link[0, 0]
    valid = code >= 0
    level = jnp.maximum(code, 0) // 24
    face = jnp.maximum(code, 0) % 24 // 4
    quarter = jnp.maximum(code, 0) % 4
    direction, side = face // 2, face % 2
    quarter_row = jnp.where(direction == 2, quarter % 2, quarter // 2)
    quarter_col = jnp.where(direction == 2, quarter // 2, quarter % 2)

    source = partner[0, slab]
    apart = source ^ slab
    chosen = jnp.int32(0)
    for bit in range(5):
        chosen = chosen + (apart >= (1 << bit)).astype(jnp.int32)
    linked = [neighbours[f, 0, source] for f in range(6)]
    present = [linked[f] >= 0 for f in range(6)]
    count = work[0, source]
    steps = jnp.full(TILE, count.astype(F32), F32)
    ratio = 2.0 * COARSE_STEP / steps
    share = 1.0 / steps

    def choose(first, planes):
        for n in range(planes):
            for f in range(5):
                value = held[0, f, first + n]
                for k in range(1, 6):
                    value = jnp.where(chosen == k, held[k, f, first + n], value)
                state[f, first + n + 1] = value

    def spread(x):
        cells = load_plane(state, x + 1)
        for d, spreader, outer in ((1, spread_y, outer_y), (2, spread_z, outer_z)):
            lower = rows() < 4 if d == 1 else lanes() % 32 < 16
            values = []
            for f in range(5):
                low = jnp.where(present[2 * d], spreader(ghosts.at[2 * d], f, x, 0), cells[f])
                high = jnp.where(present[2 * d + 1], spreader(ghosts.at[2 * d + 1], f, x, 1), cells[f])
                values.append(jnp.where(lower, low, high))
            flux, speed = half_flux(values, primitives(values), d)
            for i, v in enumerate(values + flux + [speed]):
                outer[i, x] = v

    def updater(substep):
        active = substep < count

        def update(x, cells, prims, change):
            borders = []
            for d, outer in ((1, outer_y), (2, outer_z)):

                def border(flux, speed, d=d, outer=outer):
                    return interface(
                        cells, flux, speed, [outer[i, x] for i in range(5)],
                        [outer[5 + i, x] for i in range(4)], outer[9, x], d, face_sign(d),
                    )

                part, values = across(cells, prims, d, border)
                borders.append(values)
                change = [change[i] + part[i] for i in range(5)]
            for i in range(5):
                value = jnp.where(direction == 1, borders[0][i], borders[1][i])
                value = jnp.where(active, value * share, 0.0)
                register[i, x] = value if substep == 0 else register[i, x] + value
            return [jnp.where(active, cells[i] - ratio * change[i], cells[i]) for i in range(5)]

        return update

    def outermost(substep, wanted, values):
        for i in range(5):
            value = jnp.where((substep < count) & (side == wanted), values[i] * share, 0.0)
            x_register[i] = value if substep == 0 and wanted == 0 else x_register[i] + value

    def pack_register(first, planes):
        for f in range(5):
            value = packed_z[f]
            for n in range(planes):
                value = pack_z(register[f, first + n], first + n, side, value)
            packed_z[f] = value

    def stores_of(piece):
        first = pl.multiple_of(piece * 8, 8)
        return [
            pltpu.make_async_copy(
                state.at[:, pl.ds(first + 1, 8), j, :],
                fine_out.at[0, 0, :, pl.ds(first, 8), pl.ds(j * 128, 128)],
                store_sem,
            )
            for j in range(8)
        ]

    each(BESIDE, CHUNK // PIECE + AHEAD, relay_on)
    wait_for(landed.at[pl.ds(1, 31)], ghost_recv)
    for f in range(6):
        turn = jnp.maximum(linked[f], 0) ^ slab
        for i in range(5):
            ghosts[f, i] = landed[turn, i]
    for piece in range(CHUNK // PIECE):
        arrive(piece)
    choose(0, CHUNK)
    for f in range(5):
        state[f, 0] = jnp.where(present[0], ghosts[0, f], state[f, 1])
        packed_z[f] = jnp.zeros(TILE, F32)
    for x in range(CHUNK - 1):
        spread(x)
    for substep in range(4):
        lowest = lowest_interface(state)
        outermost(substep, 0, lowest)
        reach = CHUNK - 1 - substep
        below = advance(state, 1, reach, lowest, updater(substep)) if reach > 0 else lowest
        for i in range(5):
            carry[substep, i] = below[i]

    def follow(first, planes):
        for n in range(planes // PIECE):
            arrive(first // PIECE + n)
        choose(first, planes)
        for n in range(planes):
            spread(first - 1 + n)
        for substep in range(4):
            below = [carry[substep, i] for i in range(5)]
            below = advance(state, first - substep, planes, below, updater(substep))
            for i in range(5):
                carry[substep, i] = below[i]

    def wave(c, _):
        for n in range(CHUNK // PIECE):
            piece = c * (CHUNK // PIECE) + AHEAD + n

            @pl.when(piece < PIECES)
            def _(piece=piece):
                relay_on(piece)

        follow(c * CHUNK, CHUNK)
        pack_register((c - 1) * CHUNK, CHUNK)

        @pl.when(c % 2 == 0)
        def _():
            for copy in stores_of(c // 2 - 1):
                copy.start()

        return 0

    lax.fori_loop(1, CHUNKS - 1, wave, 0)
    each(0, CHUNK // PIECE, lambda n: follow(32 - CHUNK + n * PIECE, PIECE))
    pack_register(32 - 2 * CHUNK, CHUNK)
    for f in range(5):
        state[f, 33] = jnp.where(present[1], ghosts[1, f], state[f, 32])
    spread(31)
    for substep in range(4):
        below = [carry[substep, i] for i in range(5)]
        outermost(substep, 1, advance(state, 32 - substep, substep + 1, below, updater(substep)))
    pack_register(32 - CHUNK, CHUNK)

    flat = register.reshape(5 * 32 * 8, 128)
    source_lane = lax.broadcasted_iota(jnp.int32, (128, 128), 0)
    target_lane = lax.broadcasted_iota(jnp.int32, (128, 128), 1)
    wanted = target_lane // 32 * 64 + target_lane % 32 * 2
    squeeze = ((source_lane == wanted) & (target_lane % 32 < 16) & (target_lane < 64)).astype(F32)
    for f in range(5):
        value = jnp.where(direction == 1, pack_y(flat, f * 256, side), packed_z[f])
        value = jnp.where(direction == 0, x_register[f], value)
        value = value + pltpu.roll(value, 127, 1)
        squeezed[pl.ds(f * 8, 8), :] = 0.25 * (value + pltpu.roll(value, 96, 1))
    squeezed[...] = jnp.dot(
        squeezed[...], squeeze, precision=lax.Precision.HIGHEST, preferred_element_type=F32
    )
    low_lanes = lax.broadcasted_iota(jnp.int32, (4, 128), 1) < 64
    for f in range(5):
        even = squeezed[pl.ds(f * 8, 4, stride=2), :]
        odd = squeezed[pl.ds(f * 8 + 1, 4, stride=2), :]
        small = jnp.where(low_lanes, even, pltpu.roll(odd, 64, 1))
        small = jnp.where(quarter_col == 0, small, pltpu.roll(small, 16, 1))
        note[f, pl.ds(0, 4), :] = jnp.where(quarter_row == 0, small, 0.0)
        note[f, pl.ds(4, 4), :] = jnp.where(quarter_row == 1, small, 0.0)
    place = level * 6 + (face ^ 1) + 1
    inside = (rows() // 4 == quarter_row) & (lanes() % 32 // 16 == quarter_col)
    note[5] = jnp.where(inside & valid, place.astype(F32), 0.0)
    for turn in range(1, 4):
        copy = pltpu.make_async_remote_copy(
            src_ref=note, dst_ref=notes.at[turn - 1],
            send_sem=note_send, recv_sem=note_recv,
            device_id=(slab, lvl ^ turn), device_id_type=MESH,
        )
        copy.start()
    for copy in stores_of(3):
        copy.start()

    wait_for(messages.at[pl.ds(1, 31)], ghost_send)

    wait_for(held, passed)

    wait_for(notes, note_recv)
    for g in range(6):
        key = (lvl * 6 + g + 1).astype(F32)
        parts = [note if n == 3 else notes.at[n] for n in range(4)]
        hits = [part[5] == key for part in parts]
        cover = jnp.zeros(TILE, F32)
        for n in range(4):
            cover = cover + jnp.where(hits[n], 1.0, 0.0)
        for f in range(5):
            total = jnp.zeros(TILE, F32)
            for n in range(4):
                total = total + jnp.where(hits[n], parts[n][f], 0.0)
            amounts[g, f] = (COARSE_STEP if g % 2 else -COARSE_STEP) * (cover * flux_faces[g, f] - total)
    wait_for(notes, note_send)
    coarse_store.wait()
    wait_for(state.at[:, pl.ds(1, 32)], store_sem)


def finish_kernel(
    fine, coarse, amounts, fine_out, coarse_out, fine_held, state, fine_sem, fine_out_sem, coarse_sem, out_sem
):
    def load(n):
        planes = pl.ds(n * 8, 8)
        return pltpu.make_async_copy(coarse.at[:, planes], state.at[:, planes], coarse_sem.at[n])

    def store(n, j):
        first = pl.multiple_of(n * 8, 8)
        return pltpu.make_async_copy(
            state.at[:, pl.ds(first, 8), j, :],
            coarse_out.at[0, 0, :, pl.ds(first, 8), pl.ds(j * 128, 128)],
            out_sem,
        )

    def fine_load(f):
        return pltpu.make_async_copy(fine.at[0, 0, f], fine_held.at[f], fine_sem)

    def fine_store(f):
        return pltpu.make_async_copy(fine_held.at[f], fine_out.at[0, 0, f], fine_out_sem)

    each(0, 4, lambda n: load(n).start())
    each(0, 5, lambda f: fine_load(f).start())

    def correct(x):
        cells = load_plane(state, x)
        for d, spreader in ((1, spread_y), (2, spread_z)):
            lower, upper = edge_masks(d)
            for f in range(5):
                low = jnp.where(lower, spreader(amounts.at[2 * d], f, x, 0), 0.0)
                cells[f] = cells[f] + jnp.where(upper, spreader(amounts.at[2 * d + 1], f, x, 1), low)
        for f in range(5):
            state[f, x] = cells[f]

    def correct_eight(n):
        load(n).wait()
        for end in range(2):

            @pl.when(n == end * 3)
            def _(end=end):
                for f in range(5):
                    state[f, 31 * end] = state[f, 31 * end] + amounts[end, f]

        def correct_four(half):
            for k in range(4):
                correct(n * 8 + half * 4 + k)

        each(0, 2, correct_four)
        for j in range(8):
            store(n, j).start()

    correct_eight(0)
    wait_for(fine_held, fine_sem)
    each(0, 5, lambda f: fine_store(f).start())
    each(1, 4, correct_eight)
    wait_for(fine_held, fine_out_sem)
    wait_for(state, out_sem)


SMEM = pl.BlockSpec(memory_space=pltpu.SMEM)
VMEM = pl.BlockSpec(memory_space=pltpu.VMEM)
HBM = pl.BlockSpec(memory_space=pltpu.HBM)
DMA = pltpu.SemaphoreType.DMA
LIMIT = 60 * 1024 * 1024


def step(partner, neighbours, work, link, fine_state, coarse_state):
    return pl.pallas_call(
        step_kernel,
        out_shape=(
            jax.ShapeDtypeStruct(fine_state.shape, F32),
            jax.ShapeDtypeStruct(PATCH, F32),
            jax.ShapeDtypeStruct((6, 5, *TILE), F32),
        ),
        in_specs=[SMEM, SMEM, SMEM, SMEM, HBM, HBM],
        out_specs=(HBM, HBM, VMEM),
        scratch_shapes=[
            pltpu.VMEM((6, *PATCH), F32),
            pltpu.VMEM(PATCH, F32),
            pltpu.VMEM((6, 5, *TILE), F32),
            pltpu.VMEM((32, 5, *TILE), F32),
            pltpu.VMEM((32, 5, *TILE), F32),
            pltpu.VMEM((6, 5, *TILE), F32),
            pltpu.VMEM((5, 34, *TILE), F32),
            pltpu.VMEM((10, 32, *TILE), F32),
            pltpu.VMEM((10, 32, *TILE), F32),
            pltpu.VMEM(PATCH, F32),
            pltpu.VMEM((5, *TILE), F32),
            pltpu.VMEM((5, *TILE), F32),
            pltpu.VMEM((4, 5, *TILE), F32),
            pltpu.VMEM((40, 128), F32),
            pltpu.VMEM((5, 34, *TILE), F32),
            pltpu.VMEM(PATCH, F32),
            pltpu.VMEM(PATCH, F32),
            pltpu.VMEM((6, 5, *TILE), F32),
            pltpu.VMEM((6, *TILE), F32),
            pltpu.VMEM((3, 6, *TILE), F32),
            *(DMA,) * 9, DMA((PIECES,)), DMA((PIECES,)),
        ],
        compiler_params=pltpu.CompilerParams(collective_id=0, has_side_effects=True, vmem_limit_bytes=LIMIT),
        name="step",
    )(partner, neighbours, work, link, fine_state, coarse_state)


def finish(fine_result, coarse_result, amounts):
    shape = jax.ShapeDtypeStruct(fine_result.shape, F32)
    return pl.pallas_call(
        finish_kernel,
        out_shape=(shape, shape),
        in_specs=[HBM, HBM, VMEM],
        out_specs=(HBM, HBM),
        scratch_shapes=[
            pltpu.VMEM((5, 32, 1024), F32), pltpu.VMEM(PATCH, F32), DMA, DMA, DMA((4,)), DMA,
        ],
        compiler_params=pltpu.CompilerParams(vmem_limit_bytes=LIMIT),
        name="finish",
    )(fine_result, coarse_result, amounts)


def body(fine_state, coarse_state, partner, mig_slot, neighbours, work, coarse_link):
    del mig_slot
    results = step(
        partner.T, jnp.transpose(neighbours, (2, 1, 0)), work.T, coarse_link, fine_state, coarse_state
    )
    return finish(*results)


def solution(mesh):
    return jax.shard_map(
        body,
        mesh=mesh,
        in_specs=(
            P("slab", "lvl", None, None, None),
            P("slab", "lvl", None, None, None),
            P(None, "lvl"),
            P(None, "lvl"),
            P(None, "lvl", None),
            P(None, "lvl"),
            P("slab", "lvl"),
        ),
        out_specs=(P("slab", "lvl", None, None, None), P("slab", "lvl", None, None, None)),
        check_vma=False,
    )
```

```python
import jax
import jax.numpy as jnp
from jax import lax
from jax.experimental import pallas as pl
from jax.experimental.pallas import tpu as pltpu
from jax.sharding import PartitionSpec as P

MESH = pl.DeviceIdType.MESH
F32 = jnp.float32
COARSE_STEP = 0.035
TILE = (8, 128)
PATCH = (5, 32, 8, 128)
CHUNK = 4
CHUNKS = 32 // CHUNK
PIECE = 2
PIECES = 32 // PIECE
FIRST = 2
QUEUE = 4
BESIDE = 4
AHEAD = 4


def lanes():
    return lax.broadcasted_iota(jnp.int32, TILE, 1)


def rows():
    return lax.broadcasted_iota(jnp.int32, TILE, 0)


def primitives(cells):
    density, mom_x, mom_y, mom_z, energy = cells
    inverse = 1.0 / density
    vel = [mom_x * inverse, mom_y * inverse, mom_z * inverse]
    kinetic = 0.5 * (mom_x * vel[0] + mom_y * vel[1] + mom_z * vel[2])
    pressure = 0.4 * (energy - kinetic)
    half_sound = 0.5 * jnp.sqrt(1.4 * pressure * inverse)
    return (*vel, pressure, half_sound)


def half_flux(cells, prims, direction):
    half_normal = 0.5 * prims[direction]
    pressure, half_sound = prims[3], prims[4]
    flux = [cells[1 + i] * half_normal for i in range(3)]
    flux[direction] = flux[direction] + 0.5 * pressure
    flux.append((cells[4] + pressure) * half_normal)
    return flux, jnp.abs(half_normal) + half_sound


def interface(low, low_flux, low_speed, high, high_flux, high_speed, direction, sign=None):
    fastest = jnp.maximum(low_speed, high_speed)
    if sign is not None:
        fastest = fastest * sign
    out = [0.5 * (low[1 + direction] + high[1 + direction]) - fastest * (high[0] - low[0])]
    for i in range(4):
        out.append((low_flux[i] + high_flux[i]) - fastest * (high[1 + i] - low[1 + i]))
    return out


def z_up(v):
    return pltpu.roll(v, 127, 1)


def z_down(v):
    return pltpu.roll(v, 1, 1)


def y_up(v):
    return pltpu.roll(jnp.where(lanes() < 32, pltpu.roll(v, 7, 0), v), 96, 1)


def y_down(v):
    return pltpu.roll(jnp.where(lanes() >= 96, pltpu.roll(v, 1, 0), v), 32, 1)


def edge_masks(direction):
    if direction == 1:
        return (rows() == 0) & (lanes() < 32), (rows() == 7) & (lanes() >= 96)
    return lanes() % 32 == 0, lanes() % 32 == 31


def face_sign(direction):
    lower = rows() < 4 if direction == 1 else lanes() % 32 < 16
    return jnp.where(lower, -1.0, 1.0).astype(F32)


def across(cells, prims, direction, outer):
    up, down = (y_up, y_down) if direction == 1 else (z_up, z_down)
    flux, speed = half_flux(cells, prims, direction)
    inner = interface(
        cells, flux, speed, [up(v) for v in cells], [up(v) for v in flux], up(speed), direction
    )
    border = outer(flux, speed)
    lower, upper = edge_masks(direction)
    change = [
        jnp.where(upper, border[i], inner[i]) - jnp.where(lower, border[i], down(inner[i])) for i in range(5)
    ]
    return change, border


def each(first, last, act):
    def one(i, _):
        act(i)
        return 0

    lax.fori_loop(first, last, one, 0)


def wait_for(ref, sem):
    pltpu.make_async_copy(ref, ref, sem).wait()


def load_plane(ref, x):
    return [ref[f, x] for f in range(5)]


def prepare(state, x):
    cells = load_plane(state, x)
    prims = primitives(cells)
    flux, speed = half_flux(cells, prims, 0)
    return cells, prims, flux, speed


def lowest_interface(state):
    ghost, _, ghost_flux, ghost_speed = prepare(state, 0)
    first, _, flux, speed = prepare(state, 1)
    return interface(ghost, ghost_flux, ghost_speed, first, flux, speed, 0)


def advance(state, first, count, below, update):
    cells, prims, flux, speed = prepare(state, first)
    for n in range(count):
        after = prepare(state, first + n + 1)
        above = interface(cells, flux, speed, after[0], after[2], after[3], 0)
        new = update(first + n - 1, cells, prims, [above[i] - below[i] for i in range(5)])
        for f in range(5):
            state[f, first + n] = new[f]
        cells, prims, flux, speed = after
        below = above
    return below


def pack_y(flat, first, side):
    out = None
    for g in range(4):
        part = flat[pl.ds(first + g * 8 + 7 * side, 8, stride=32), :]
        part = pltpu.roll(part, (32 * g - 96 * side) % 128, 1)
        out = part if g == 0 else jnp.where(lanes() // 32 == g, part, out)
    return out


def pack_z(plane, x, side, out):
    return jnp.where(lanes() % 32 == x, pltpu.roll(plane, (x + 128 - 31 * side) % 128, 1), out)


def pack_z_faces(ref, first):
    def pack(x, carried):
        return tuple(
            pack_z(ref[f, first + x], x, side, carried[side * 5 + f]) for side in range(2) for f in range(5)
        )

    return lax.fori_loop(0, 32, pack, (jnp.zeros(TILE, F32),) * 10, unroll=4)


def spread_y(face, field, x, side):
    row = jnp.broadcast_to(face[field, pl.ds(x // 4, 1), :], TILE)
    shift = (3 - x % 4) * 32 if side else (4 - x % 4) * 32
    return pltpu.roll(row, shift % 128, 1)


def spread_z(face, field, x, side):
    return pltpu.roll(face[field], (128 - x + 31 * side) % 128, 1)


def step_kernel(
    partner, neighbours, work, link, fine, coarse, fine_out, coarse_out, amounts,
    held, relay, faces, messages, landed, ghosts,
    state, outer_y, outer_z, register, x_register, packed_z, carry, squeezed,
    coarse_state, flux_y, flux_z, flux_faces, note, notes,
    load_sem, coarse_sem, store_sem, coarse_store_sem, ghost_send, ghost_recv, note_send, note_recv,
    passed, reached, ended,
):
    slab = lax.axis_index("slab")
    lvl = lax.axis_index("lvl")
    other_lvl = lvl ^ 2
    own = held.at[0]

    def loads_of(source, target, sem):
        return [
            pltpu.make_async_copy(source.at[0, 0, :, :, pl.ds(j * 128, 128)], target.at[:, :, j, :], sem)
            for j in range(8)
        ]

    fine_loads = loads_of(fine, own, load_sem)
    coarse_loads = loads_of(coarse, coarse_state.at[:, pl.ds(1, 32)], coarse_sem)
    for copy in fine_loads + coarse_loads:
        copy.start()

    barrier = pltpu.get_barrier_semaphore()

    def greet(device):
        pl.semaphore_signal(barrier, inc=1, device_id=device, device_id_type=MESH)

    each(1, 32, lambda turn: greet((slab ^ turn, lvl)))
    each(1, 4, lambda turn: greet((slab, lvl ^ turn)))
    greet((slab ^ 16, other_lvl))

    def span(ref, piece):
        return ref.at[:, pl.ds(piece * PIECE, PIECE)]

    def near(axis, piece):
        return pltpu.make_async_remote_copy(
            src_ref=span(own, piece), dst_ref=span(held.at[1 + 2 * axis], piece),
            send_sem=passed, recv_sem=reached.at[piece],
            device_id=(slab ^ (4 if axis else 1), lvl), device_id_type=MESH,
        )

    def far(axis, piece):
        return pltpu.make_async_remote_copy(
            src_ref=span(held.at[1 + 2 * axis], piece), dst_ref=span(held.at[2 + 2 * axis], piece),
            send_sem=passed, recv_sem=ended.at[piece],
            device_id=(slab ^ (12 if axis else 3), lvl), device_id_type=MESH,
        )

    def up(piece):
        return pltpu.make_async_remote_copy(
            src_ref=span(own, piece), dst_ref=span(relay, piece),
            send_sem=passed, recv_sem=reached.at[piece],
            device_id=(slab ^ (piece % 2 * 16), other_lvl), device_id_type=MESH,
        )

    def on(piece):
        return pltpu.make_async_remote_copy(
            src_ref=span(relay, piece), dst_ref=span(held.at[5], piece),
            send_sem=passed, recv_sem=ended.at[piece],
            device_id=(slab ^ ((piece + 1) % 2 * 16), other_lvl), device_id_type=MESH,
        )

    def send(piece):
        near(0, piece).start()
        near(1, piece).start()
        up(piece).start()

    def three(piece):
        return held.at[pl.ds(0, 3), :, pl.ds(piece * PIECE, PIECE)]

    def forward(piece):
        wait_for(three(piece), reached.at[piece])
        far(0, piece).start()
        far(1, piece).start()
        on(piece).start()

    def relay_on(piece):
        forward(piece)

        @pl.when(piece + QUEUE < PIECES)
        def _():
            send(piece + QUEUE)

    def arrive(piece):
        wait_for(three(piece), ended.at[piece])

    wait_for(own, load_sem)
    pl.semaphore_wait(barrier, 35)
    each(0, FIRST, send)

    flat = own.reshape(5 * 32 * 8, 128)
    for f in range(5):
        faces[0, f] = own[f, 0]
        faces[1, f] = own[f, 31]
        for side in range(2):
            faces[2 + side, f] = pack_y(flat, f * 256, side)
    packed = pack_z_faces(own, 0)
    for side in range(2):
        for f in range(5):
            faces[4 + side, f] = packed[side * 5 + f]

    mine = [neighbours[f, 0, slab] for f in range(6)]

    def compose(turn, target):
        patch = partner[0, slab ^ turn]
        which = jnp.int32(0)
        for f in range(1, 6):
            which = jnp.where(mine[f] == patch, f, which)
        for f in range(5):
            target[turn, f] = faces[which, f]

    def ghost(turn):
        return pltpu.make_async_remote_copy(
            src_ref=messages.at[turn], dst_ref=landed.at[turn],
            send_sem=ghost_send, recv_sem=ghost_recv,
            device_id=(slab ^ turn, lvl), device_id_type=MESH,
        )

    def send_ghost(turn):
        compose(turn, messages)
        ghost(turn).start()

    compose(0, landed)
    each(1, 32, send_ghost)
    each(FIRST, QUEUE, send)

    wait_for(coarse_state.at[:, pl.ds(1, 32)], coarse_sem)
    for f in range(5):
        coarse_state[f, 0] = coarse_state[f, 1]
        coarse_state[f, 33] = coarse_state[f, 32]

    def coarse_update(x, cells, prims, change):
        for d, kept in ((1, flux_y), (2, flux_z)):

            def border(flux, speed, d=d):
                return [cells[1 + d]] + [2.0 * v for v in flux]

            part, values = across(cells, prims, d, border)
            change = [change[i] + part[i] for i in range(5)]
            for i in range(5):
                kept[i, x] = values[i]
        return [cells[i] - COARSE_STEP * change[i] for i in range(5)]

    lowest = lowest_interface(coarse_state)

    def coarse_chunk(c, below):
        return tuple(advance(coarse_state, 1 + c * CHUNK, CHUNK, below, coarse_update))


    def coarse_part(n, below):
        below = lax.fori_loop(n * CHUNKS // BESIDE, (n + 1) * CHUNKS // BESIDE, coarse_chunk, below)
        relay_on(n)
        return below

    highest = lax.fori_loop(0, BESIDE, coarse_part, tuple(lowest))
    coarse_store = pltpu.make_async_copy(coarse_state.at[:, pl.ds(1, 32)], coarse_out, coarse_store_sem)
    coarse_store.start()
    for f in range(5):
        flux_faces[0, f] = lowest[f]
        flux_faces[1, f] = highest[f]
        for end in range(2):
            flux_faces[2 + end, f] = pack_y(flux_y.reshape(5 * 32 * 8, 128), f * 256, end)
    packed = pack_z_faces(flux_z, 0)
    for end in range(2):
        for f in range(5):
            flux_faces[4 + end, f] = packed[end * 5 + f]

    code = link[0, 0]
    valid = code >= 0
    level = jnp.maximum(code, 0) // 24
    face = jnp.maximum(code, 0) % 24 // 4
    quarter = jnp.maximum(code, 0) % 4
    direction, side = face // 2, face % 2
    quarter_row = jnp.where(direction == 2, quarter % 2, quarter // 2)
    quarter_col = jnp.where(direction == 2, quarter // 2, quarter % 2)

    source = partner[0, slab]
    apart = source ^ slab
    chosen = jnp.int32(0)
    for bit in range(5):
        chosen = chosen + (apart >= (1 << bit)).astype(jnp.int32)
    linked = [neighbours[f, 0, source] for f in range(6)]
    present = [linked[f] >= 0 for f in range(6)]
    count = work[0, source]
    steps = jnp.full(TILE, count.astype(F32), F32)
    ratio = 2.0 * COARSE_STEP / steps
    share = 1.0 / steps

    def choose(first, planes):
        for n in range(planes):
            for f in range(5):
                value = held[0, f, first + n]
                for k in range(1, 6):
                    value = jnp.where(chosen == k, held[k, f, first + n], value)
                state[f, first + n + 1] = value

    def spread(x):
        cells = load_plane(state, x + 1)
        for d, spreader, outer in ((1, spread_y, outer_y), (2, spread_z, outer_z)):
            lower = rows() < 4 if d == 1 else lanes() % 32 < 16
            values = []
            for f in range(5):
                low = jnp.where(present[2 * d], spreader(ghosts.at[2 * d], f, x, 0), cells[f])
                high = jnp.where(present[2 * d + 1], spreader(ghosts.at[2 * d + 1], f, x, 1), cells[f])
                values.append(jnp.where(lower, low, high))
            flux, speed = half_flux(values, primitives(values), d)
            for i, v in enumerate(values + flux + [speed]):
                outer[i, x] = v

    def updater(substep):
        active = substep < count

        def update(x, cells, prims, change):
            borders = []
            for d, outer in ((1, outer_y), (2, outer_z)):

                def border(flux, speed, d=d, outer=outer):
                    return interface(
                        cells, flux, speed, [outer[i, x] for i in range(5)],
                        [outer[5 + i, x] for i in range(4)], outer[9, x], d, face_sign(d),
                    )

                part, values = across(cells, prims, d, border)
                borders.append(values)
                change = [change[i] + part[i] for i in range(5)]
            for i in range(5):
                value = jnp.where(direction == 1, borders[0][i], borders[1][i])
                value = jnp.where(active, value * share, 0.0)
                register[i, x] = value if substep == 0 else register[i, x] + value
            return [jnp.where(active, cells[i] - ratio * change[i], cells[i]) for i in range(5)]

        return update

    def outermost(substep, wanted, values):
        for i in range(5):
            value = jnp.where((substep < count) & (side == wanted), values[i] * share, 0.0)
            x_register[i] = value if substep == 0 and wanted == 0 else x_register[i] + value

    def pack_register(first, planes):
        for f in range(5):
            value = packed_z[f]
            for n in range(planes):
                value = pack_z(register[f, first + n], first + n, side, value)
            packed_z[f] = value

    def stores_of(piece):
        first = pl.multiple_of(piece * 8, 8)
        return [
            pltpu.make_async_copy(
                state.at[:, pl.ds(first + 1, 8), j, :],
                fine_out.at[0, 0, :, pl.ds(first, 8), pl.ds(j * 128, 128)],
                store_sem,
            )
            for j in range(8)
        ]

    each(BESIDE, CHUNK // PIECE + AHEAD, relay_on)
    wait_for(landed.at[pl.ds(1, 31)], ghost_recv)
    for f in range(6):
        turn = jnp.maximum(linked[f], 0) ^ slab
        for i in range(5):
            ghosts[f, i] = landed[turn, i]
    for piece in range(CHUNK // PIECE):
        arrive(piece)
    choose(0, CHUNK)
    for f in range(5):
        state[f, 0] = jnp.where(present[0], ghosts[0, f], state[f, 1])
        packed_z[f] = jnp.zeros(TILE, F32)
    for x in range(CHUNK - 1):
        spread(x)
    for substep in range(4):
        lowest = lowest_interface(state)
        outermost(substep, 0, lowest)
        reach = CHUNK - 1 - substep
        below = advance(state, 1, reach, lowest, updater(substep)) if reach > 0 else lowest
        for i in range(5):
            carry[substep, i] = below[i]

    def follow(first, planes):
        for n in range(planes // PIECE):
            arrive(first // PIECE + n)
        choose(first, planes)
        for n in range(planes):
            spread(first - 1 + n)
        for substep in range(4):
            below = [carry[substep, i] for i in range(5)]
            below = advance(state, first - substep, planes, below, updater(substep))
            for i in range(5):
                carry[substep, i] = below[i]

    def wave(c, _):
        for n in range(CHUNK // PIECE):
            piece = c * (CHUNK // PIECE) + AHEAD + n

            @pl.when(piece < PIECES)
            def _(piece=piece):
                relay_on(piece)

        follow(c * CHUNK, CHUNK)
        pack_register((c - 1) * CHUNK, CHUNK)

        @pl.when(c % 2 == 0)
        def _():
            for copy in stores_of(c // 2 - 1):
                copy.start()

        return 0

    lax.fori_loop(1, CHUNKS - 1, wave, 0)
    each(0, CHUNK // PIECE, lambda n: follow(32 - CHUNK + n * PIECE, PIECE))
    pack_register(32 - 2 * CHUNK, CHUNK)
    for f in range(5):
        state[f, 33] = jnp.where(present[1], ghosts[1, f], state[f, 32])
    spread(31)
    for substep in range(4):
        below = [carry[substep, i] for i in range(5)]
        outermost(substep, 1, advance(state, 32 - substep, substep + 1, below, updater(substep)))
    pack_register(32 - CHUNK, CHUNK)

    flat = register.reshape(5 * 32 * 8, 128)
    source_lane = lax.broadcasted_iota(jnp.int32, (128, 128), 0)
    target_lane = lax.broadcasted_iota(jnp.int32, (128, 128), 1)
    wanted = target_lane // 32 * 64 + target_lane % 32 * 2
    squeeze = ((source_lane == wanted) & (target_lane % 32 < 16) & (target_lane < 64)).astype(F32)
    for f in range(5):
        value = jnp.where(direction == 1, pack_y(flat, f * 256, side), packed_z[f])
        value = jnp.where(direction == 0, x_register[f], value)
        value = value + pltpu.roll(value, 127, 1)
        squeezed[pl.ds(f * 8, 8), :] = 0.25 * (value + pltpu.roll(value, 96, 1))
    squeezed[...] = jnp.dot(
        squeezed[...], squeeze, precision=lax.Precision.HIGHEST, preferred_element_type=F32
    )
    low_lanes = lax.broadcasted_iota(jnp.int32, (4, 128), 1) < 64
    for f in range(5):
        even = squeezed[pl.ds(f * 8, 4, stride=2), :]
        odd = squeezed[pl.ds(f * 8 + 1, 4, stride=2), :]
        small = jnp.where(low_lanes, even, pltpu.roll(odd, 64, 1))
        small = jnp.where(quarter_col == 0, small, pltpu.roll(small, 16, 1))
        note[f, pl.ds(0, 4), :] = jnp.where(quarter_row == 0, small, 0.0)
        note[f, pl.ds(4, 4), :] = jnp.where(quarter_row == 1, small, 0.0)
    place = level * 6 + (face ^ 1) + 1
    inside = (rows() // 4 == quarter_row) & (lanes() % 32 // 16 == quarter_col)
    note[5] = jnp.where(inside & valid, place.astype(F32), 0.0)
    for turn in range(1, 4):
        copy = pltpu.make_async_remote_copy(
            src_ref=note, dst_ref=notes.at[turn - 1],
            send_sem=note_send, recv_sem=note_recv,
            device_id=(slab, lvl ^ turn), device_id_type=MESH,
        )
        copy.start()
    for copy in stores_of(3):
        copy.start()

    wait_for(messages.at[pl.ds(1, 31)], ghost_send)

    wait_for(held, passed)

    wait_for(notes, note_recv)
    for g in range(6):
        key = (lvl * 6 + g + 1).astype(F32)
        parts = [note if n == 3 else notes.at[n] for n in range(4)]
        hits = [part[5] == key for part in parts]
        cover = jnp.zeros(TILE, F32)
        for n in range(4):
            cover = cover + jnp.where(hits[n], 1.0, 0.0)
        for f in range(5):
            total = jnp.zeros(TILE, F32)
            for n in range(4):
                total = total + jnp.where(hits[n], parts[n][f], 0.0)
            amounts[g, f] = (COARSE_STEP if g % 2 else -COARSE_STEP) * (cover * flux_faces[g, f] - total)
    wait_for(notes, note_send)
    coarse_store.wait()
    wait_for(state.at[:, pl.ds(1, 32)], store_sem)


def finish_kernel(
    fine, coarse, given, fine_out, coarse_out, fine_held, state, amounts,
    fine_sem, fine_out_sem, coarse_sem, given_sem, out_sem,
):
    def load(n):
        planes = pl.ds(n * 8, 8)
        return pltpu.make_async_copy(coarse.at[:, planes], state.at[:, planes], coarse_sem.at[n])

    def store(n, j):
        first = pl.multiple_of(n * 8, 8)
        return pltpu.make_async_copy(
            state.at[:, pl.ds(first, 8), j, :],
            coarse_out.at[0, 0, :, pl.ds(first, 8), pl.ds(j * 128, 128)],
            out_sem,
        )

    def fine_load(f):
        return pltpu.make_async_copy(fine.at[0, 0, f], fine_held.at[f], fine_sem)

    def fine_store(f):
        return pltpu.make_async_copy(fine_held.at[f], fine_out.at[0, 0, f], fine_out_sem)

    fetch = pltpu.make_async_copy(given, amounts, given_sem)
    fetch.start()
    each(0, 4, lambda n: load(n).start())
    each(0, 5, lambda f: fine_load(f).start())

    def correct(x):
        cells = load_plane(state, x)
        for d, spreader in ((1, spread_y), (2, spread_z)):
            lower, upper = edge_masks(d)
            for f in range(5):
                low = jnp.where(lower, spreader(amounts.at[2 * d], f, x, 0), 0.0)
                cells[f] = cells[f] + jnp.where(upper, spreader(amounts.at[2 * d + 1], f, x, 1), low)
        for f in range(5):
            state[f, x] = cells[f]

    def correct_eight(n):
        load(n).wait()
        for end in range(2):

            @pl.when(n == end * 3)
            def _(end=end):
                for f in range(5):
                    state[f, 31 * end] = state[f, 31 * end] + amounts[end, f]

        def correct_four(half):
            for k in range(4):
                correct(n * 8 + half * 4 + k)

        each(0, 2, correct_four)
        for j in range(8):
            store(n, j).start()

    fetch.wait()
    correct_eight(0)
    wait_for(fine_held, fine_sem)
    each(0, 5, lambda f: fine_store(f).start())
    each(1, 4, correct_eight)
    wait_for(fine_held, fine_out_sem)
    wait_for(state, out_sem)


SMEM = pl.BlockSpec(memory_space=pltpu.SMEM)
VMEM = pl.BlockSpec(memory_space=pltpu.VMEM)
HBM = pl.BlockSpec(memory_space=pltpu.HBM)
DMA = pltpu.SemaphoreType.DMA
LIMIT = 60 * 1024 * 1024


def step(partner, neighbours, work, link, fine_state, coarse_state):
    return pl.pallas_call(
        step_kernel,
        out_shape=(
            jax.ShapeDtypeStruct(fine_state.shape, F32),
            jax.ShapeDtypeStruct(PATCH, F32),
            jax.ShapeDtypeStruct((6, 5, *TILE), F32),
        ),
        in_specs=[SMEM, SMEM, SMEM, SMEM, HBM, HBM],
        out_specs=(HBM, HBM, VMEM),
        scratch_shapes=[
            pltpu.VMEM((6, *PATCH), F32),
            pltpu.VMEM(PATCH, F32),
            pltpu.VMEM((6, 5, *TILE), F32),
            pltpu.VMEM((32, 5, *TILE), F32),
            pltpu.VMEM((32, 5, *TILE), F32),
            pltpu.VMEM((6, 5, *TILE), F32),
            pltpu.VMEM((5, 34, *TILE), F32),
            pltpu.VMEM((10, 32, *TILE), F32),
            pltpu.VMEM((10, 32, *TILE), F32),
            pltpu.VMEM(PATCH, F32),
            pltpu.VMEM((5, *TILE), F32),
            pltpu.VMEM((5, *TILE), F32),
            pltpu.VMEM((4, 5, *TILE), F32),
            pltpu.VMEM((40, 128), F32),
            pltpu.VMEM((5, 34, *TILE), F32),
            pltpu.VMEM(PATCH, F32),
            pltpu.VMEM(PATCH, F32),
            pltpu.VMEM((6, 5, *TILE), F32),
            pltpu.VMEM((6, *TILE), F32),
            pltpu.VMEM((3, 6, *TILE), F32),
            *(DMA,) * 9, DMA((PIECES,)), DMA((PIECES,)),
        ],
        compiler_params=pltpu.CompilerParams(collective_id=0, has_side_effects=True, vmem_limit_bytes=LIMIT),
        name="step",
    )(partner, neighbours, work, link, fine_state, coarse_state)


def finish(fine_result, coarse_result, amounts):
    shape = jax.ShapeDtypeStruct(fine_result.shape, F32)
    return pl.pallas_call(
        finish_kernel,
        out_shape=(shape, shape),
        in_specs=[HBM, HBM, HBM],
        out_specs=(HBM, HBM),
        scratch_shapes=[
            pltpu.VMEM((5, 32, 1024), F32), pltpu.VMEM(PATCH, F32), pltpu.VMEM((6, 5, *TILE), F32),
            DMA, DMA, DMA((4,)), DMA, DMA,
        ],
        compiler_params=pltpu.CompilerParams(vmem_limit_bytes=LIMIT),
        name="finish",
    )(fine_result, coarse_result, amounts)


def body(fine_state, coarse_state, partner, mig_slot, neighbours, work, coarse_link):
    del mig_slot
    results = step(
        partner.T, jnp.transpose(neighbours, (2, 1, 0)), work.T, coarse_link, fine_state, coarse_state
    )
    return finish(*results)


def solution(mesh):
    return jax.shard_map(
        body,
        mesh=mesh,
        in_specs=(
            P("slab", "lvl", None, None, None),
            P("slab", "lvl", None, None, None),
            P(None, "lvl"),
            P(None, "lvl"),
            P(None, "lvl", None),
            P(None, "lvl"),
            P("slab", "lvl"),
        ),
        out_specs=(P("slab", "lvl", None, None, None), P("slab", "lvl", None, None, None)),
        check_vma=False,
    )
```

```python
import jax
import jax.numpy as jnp
from jax import lax
from jax.experimental import pallas as pl
from jax.experimental.pallas import tpu as pltpu
from jax.sharding import PartitionSpec as P

MESH = pl.DeviceIdType.MESH
F32 = jnp.float32
COARSE_STEP = 0.035
TILE = (8, 128)
PATCH = (5, 32, 8, 128)
CHUNK = 4
CHUNKS = 32 // CHUNK
PIECE = 2
PIECES = 32 // PIECE
FIRST = 2
QUEUE = 4
BESIDE = 4
AHEAD = 4


def lanes():
    return lax.broadcasted_iota(jnp.int32, TILE, 1)


def rows():
    return lax.broadcasted_iota(jnp.int32, TILE, 0)


def primitives(cells):
    density, mom_x, mom_y, mom_z, energy = cells
    inverse = 1.0 / density
    vel = [mom_x * inverse, mom_y * inverse, mom_z * inverse]
    kinetic = 0.5 * (mom_x * vel[0] + mom_y * vel[1] + mom_z * vel[2])
    pressure = 0.4 * (energy - kinetic)
    half_sound = 0.5 * jnp.sqrt(1.4 * pressure * inverse)
    return (*vel, pressure, half_sound)


def half_flux(cells, prims, direction):
    half_normal = 0.5 * prims[direction]
    pressure, half_sound = prims[3], prims[4]
    flux = [cells[1 + i] * half_normal for i in range(3)]
    flux[direction] = flux[direction] + 0.5 * pressure
    flux.append((cells[4] + pressure) * half_normal)
    return flux, jnp.abs(half_normal) + half_sound


def interface(low, low_flux, low_speed, high, high_flux, high_speed, direction, sign=None):
    fastest = jnp.maximum(low_speed, high_speed)
    if sign is not None:
        fastest = fastest * sign
    out = [0.5 * (low[1 + direction] + high[1 + direction]) - fastest * (high[0] - low[0])]
    for i in range(4):
        out.append((low_flux[i] + high_flux[i]) - fastest * (high[1 + i] - low[1 + i]))
    return out


def z_up(v):
    return pltpu.roll(v, 127, 1)


def z_down(v):
    return pltpu.roll(v, 1, 1)


def y_up(v):
    return pltpu.roll(jnp.where(lanes() < 32, pltpu.roll(v, 7, 0), v), 96, 1)


def y_down(v):
    return pltpu.roll(jnp.where(lanes() >= 96, pltpu.roll(v, 1, 0), v), 32, 1)


def edge_masks(direction):
    if direction == 1:
        return (rows() == 0) & (lanes() < 32), (rows() == 7) & (lanes() >= 96)
    return lanes() % 32 == 0, lanes() % 32 == 31


def face_sign(direction):
    lower = rows() < 4 if direction == 1 else lanes() % 32 < 16
    return jnp.where(lower, -1.0, 1.0).astype(F32)


def across(cells, prims, direction, outer):
    up, down = (y_up, y_down) if direction == 1 else (z_up, z_down)
    flux, speed = half_flux(cells, prims, direction)
    inner = interface(
        cells, flux, speed, [up(v) for v in cells], [up(v) for v in flux], up(speed), direction
    )
    border = outer(flux, speed)
    lower, upper = edge_masks(direction)
    change = [
        jnp.where(upper, border[i], inner[i]) - jnp.where(lower, border[i], down(inner[i])) for i in range(5)
    ]
    return change, border


def each(first, last, act):
    def one(i, _):
        act(i)
        return 0

    lax.fori_loop(first, last, one, 0)


def wait_for(ref, sem):
    pltpu.make_async_copy(ref, ref, sem).wait()


def load_plane(ref, x):
    return [ref[f, x] for f in range(5)]


def prepare(state, x):
    cells = load_plane(state, x)
    prims = primitives(cells)
    flux, speed = half_flux(cells, prims, 0)
    return cells, prims, flux, speed


def lowest_interface(state):
    ghost, _, ghost_flux, ghost_speed = prepare(state, 0)
    first, _, flux, speed = prepare(state, 1)
    return interface(ghost, ghost_flux, ghost_speed, first, flux, speed, 0)


def advance(state, first, count, below, update):
    cells, prims, flux, speed = prepare(state, first)
    for n in range(count):
        after = prepare(state, first + n + 1)
        above = interface(cells, flux, speed, after[0], after[2], after[3], 0)
        new = update(first + n - 1, cells, prims, [above[i] - below[i] for i in range(5)])
        for f in range(5):
            state[f, first + n] = new[f]
        cells, prims, flux, speed = after
        below = above
    return below


def pack_y(flat, first, side):
    out = None
    for g in range(4):
        part = flat[pl.ds(first + g * 8 + 7 * side, 8, stride=32), :]
        part = pltpu.roll(part, (32 * g - 96 * side) % 128, 1)
        out = part if g == 0 else jnp.where(lanes() // 32 == g, part, out)
    return out


def pack_z(plane, x, side, out):
    return jnp.where(lanes() % 32 == x, pltpu.roll(plane, (x + 128 - 31 * side) % 128, 1), out)


def pack_z_faces(ref, first):
    def pack(x, carried):
        return tuple(
            pack_z(ref[f, first + x], x, side, carried[side * 5 + f]) for side in range(2) for f in range(5)
        )

    return lax.fori_loop(0, 32, pack, (jnp.zeros(TILE, F32),) * 10, unroll=4)


def spread_y(face, field, x, side):
    row = jnp.broadcast_to(face[field, pl.ds(x // 4, 1), :], TILE)
    shift = (3 - x % 4) * 32 if side else (4 - x % 4) * 32
    return pltpu.roll(row, shift % 128, 1)


def spread_z(face, field, x, side):
    return pltpu.roll(face[field], (128 - x + 31 * side) % 128, 1)


def step_kernel(
    partner, neighbours, work, link, fine, coarse, fine_out, coarse_out, amounts,
    held, relay, faces, messages, landed, ghosts,
    state, outer_y, outer_z, register, x_register, packed_z, carry, squeezed,
    coarse_state, flux_y, flux_z, flux_faces, note, notes,
    load_sem, coarse_sem, store_sem, coarse_store_sem, ghost_send, ghost_recv, note_send, note_recv,
    passed, reached, ended,
):
    slab = lax.axis_index("slab")
    lvl = lax.axis_index("lvl")
    other_lvl = lvl ^ 2
    own = held.at[0]

    def loads_of(source, target, sem):
        return [
            pltpu.make_async_copy(source.at[0, 0, :, :, pl.ds(j * 128, 128)], target.at[:, :, j, :], sem)
            for j in range(8)
        ]

    fine_loads = loads_of(fine, own, load_sem)
    coarse_loads = loads_of(coarse, coarse_state.at[:, pl.ds(1, 32)], coarse_sem)
    for copy in fine_loads + coarse_loads:
        copy.start()

    barrier = pltpu.get_barrier_semaphore()

    def greet(device):
        pl.semaphore_signal(barrier, inc=1, device_id=device, device_id_type=MESH)

    each(1, 32, lambda turn: greet((slab ^ turn, lvl)))
    each(1, 4, lambda turn: greet((slab, lvl ^ turn)))
    greet((slab ^ 16, other_lvl))

    def span(ref, piece):
        return ref.at[:, pl.ds(piece * PIECE, PIECE)]

    def near(axis, piece):
        return pltpu.make_async_remote_copy(
            src_ref=span(own, piece), dst_ref=span(held.at[1 + 2 * axis], piece),
            send_sem=passed, recv_sem=reached.at[piece],
            device_id=(slab ^ (4 if axis else 1), lvl), device_id_type=MESH,
        )

    def far(axis, piece):
        return pltpu.make_async_remote_copy(
            src_ref=span(held.at[1 + 2 * axis], piece), dst_ref=span(held.at[2 + 2 * axis], piece),
            send_sem=passed, recv_sem=ended.at[piece],
            device_id=(slab ^ (12 if axis else 3), lvl), device_id_type=MESH,
        )

    def up(piece):
        return pltpu.make_async_remote_copy(
            src_ref=span(own, piece), dst_ref=span(relay, piece),
            send_sem=passed, recv_sem=reached.at[piece],
            device_id=(slab ^ (piece % 2 * 16), other_lvl), device_id_type=MESH,
        )

    def on(piece):
        return pltpu.make_async_remote_copy(
            src_ref=span(relay, piece), dst_ref=span(held.at[5], piece),
            send_sem=passed, recv_sem=ended.at[piece],
            device_id=(slab ^ ((piece + 1) % 2 * 16), other_lvl), device_id_type=MESH,
        )

    def send(piece):
        near(0, piece).start()
        near(1, piece).start()
        up(piece).start()

    def three(piece):
        return held.at[pl.ds(0, 3), :, pl.ds(piece * PIECE, PIECE)]

    def forward(piece):
        wait_for(three(piece), reached.at[piece])
        far(0, piece).start()
        far(1, piece).start()
        on(piece).start()

    def relay_on(piece):
        forward(piece)

        @pl.when(piece + QUEUE < PIECES)
        def _():
            send(piece + QUEUE)

    def arrive(piece):
        wait_for(three(piece), ended.at[piece])

    wait_for(own, load_sem)
    pl.semaphore_wait(barrier, 35)
    each(0, FIRST, send)

    flat = own.reshape(5 * 32 * 8, 128)
    for f in range(5):
        faces[0, f] = own[f, 0]
        faces[1, f] = own[f, 31]
        for side in range(2):
            faces[2 + side, f] = pack_y(flat, f * 256, side)
    packed = pack_z_faces(own, 0)
    for side in range(2):
        for f in range(5):
            faces[4 + side, f] = packed[side * 5 + f]

    mine = [neighbours[f, 0, slab] for f in range(6)]

    def compose(turn, target):
        patch = partner[0, slab ^ turn]
        which = jnp.int32(0)
        for f in range(1, 6):
            which = jnp.where(mine[f] == patch, f, which)
        for f in range(5):
            target[turn, f] = faces[which, f]

    def ghost(turn):
        return pltpu.make_async_remote_copy(
            src_ref=messages.at[turn], dst_ref=landed.at[turn],
            send_sem=ghost_send, recv_sem=ghost_recv,
            device_id=(slab ^ turn, lvl), device_id_type=MESH,
        )

    def send_ghost(turn):
        compose(turn, messages)
        ghost(turn).start()

    compose(0, landed)
    each(1, 32, send_ghost)
    each(FIRST, QUEUE, send)

    wait_for(coarse_state.at[:, pl.ds(1, 32)], coarse_sem)
    for f in range(5):
        coarse_state[f, 0] = coarse_state[f, 1]
        coarse_state[f, 33] = coarse_state[f, 32]

    def coarse_update(x, cells, prims, change):
        for d, kept in ((1, flux_y), (2, flux_z)):

            def border(flux, speed, d=d):
                return [cells[1 + d]] + [2.0 * v for v in flux]

            part, values = across(cells, prims, d, border)
            change = [change[i] + part[i] for i in range(5)]
            for i in range(5):
                kept[i, x] = values[i]
        return [cells[i] - COARSE_STEP * change[i] for i in range(5)]

    lowest = lowest_interface(coarse_state)

    def coarse_chunk(c, below):
        return tuple(advance(coarse_state, 1 + c * CHUNK, CHUNK, below, coarse_update))


    def coarse_part(n, below):
        below = lax.fori_loop(n * CHUNKS // BESIDE, (n + 1) * CHUNKS // BESIDE, coarse_chunk, below)
        relay_on(n)
        return below

    highest = lax.fori_loop(0, BESIDE, coarse_part, tuple(lowest))
    coarse_store = pltpu.make_async_copy(coarse_state.at[:, pl.ds(1, 32)], coarse_out, coarse_store_sem)
    coarse_store.start()
    for f in range(5):
        flux_faces[0, f] = lowest[f]
        flux_faces[1, f] = highest[f]
        for end in range(2):
            flux_faces[2 + end, f] = pack_y(flux_y.reshape(5 * 32 * 8, 128), f * 256, end)
    packed = pack_z_faces(flux_z, 0)
    for end in range(2):
        for f in range(5):
            flux_faces[4 + end, f] = packed[end * 5 + f]

    code = link[0, 0]
    valid = code >= 0
    level = jnp.maximum(code, 0) // 24
    face = jnp.maximum(code, 0) % 24 // 4
    quarter = jnp.maximum(code, 0) % 4
    direction, side = face // 2, face % 2
    quarter_row = jnp.where(direction == 2, quarter % 2, quarter // 2)
    quarter_col = jnp.where(direction == 2, quarter // 2, quarter % 2)

    source = partner[0, slab]
    apart = source ^ slab
    chosen = jnp.int32(0)
    for bit in range(5):
        chosen = chosen + (apart >= (1 << bit)).astype(jnp.int32)
    linked = [neighbours[f, 0, source] for f in range(6)]
    present = [linked[f] >= 0 for f in range(6)]
    count = work[0, source]
    steps = jnp.full(TILE, count.astype(F32), F32)
    ratio = 2.0 * COARSE_STEP / steps
    share = 1.0 / steps

    def choose(first, planes):
        for n in range(planes):
            for f in range(5):
                value = held[0, f, first + n]
                for k in range(1, 6):
                    value = jnp.where(chosen == k, held[k, f, first + n], value)
                state[f, first + n + 1] = value

    def spread(x):
        cells = load_plane(state, x + 1)
        for d, spreader, outer in ((1, spread_y, outer_y), (2, spread_z, outer_z)):
            lower = rows() < 4 if d == 1 else lanes() % 32 < 16
            values = []
            for f in range(5):
                low = jnp.where(present[2 * d], spreader(ghosts.at[2 * d], f, x, 0), cells[f])
                high = jnp.where(present[2 * d + 1], spreader(ghosts.at[2 * d + 1], f, x, 1), cells[f])
                values.append(jnp.where(lower, low, high))
            flux, speed = half_flux(values, primitives(values), d)
            for i, v in enumerate(values + flux + [speed]):
                outer[i, x] = v

    def updater(substep):
        active = substep < count

        def update(x, cells, prims, change):
            borders = []
            for d, outer in ((1, outer_y), (2, outer_z)):

                def border(flux, speed, d=d, outer=outer):
                    return interface(
                        cells, flux, speed, [outer[i, x] for i in range(5)],
                        [outer[5 + i, x] for i in range(4)], outer[9, x], d, face_sign(d),
                    )

                part, values = across(cells, prims, d, border)
                borders.append(values)
                change = [change[i] + part[i] for i in range(5)]
            for i in range(5):
                value = jnp.where(direction == 1, borders[0][i], borders[1][i])
                value = jnp.where(active, value * share, 0.0)
                register[i, x] = value if substep == 0 else register[i, x] + value
            return [jnp.where(active, cells[i] - ratio * change[i], cells[i]) for i in range(5)]

        return update

    def outermost(substep, wanted, values):
        for i in range(5):
            value = jnp.where((substep < count) & (side == wanted), values[i] * share, 0.0)
            x_register[i] = value if substep == 0 and wanted == 0 else x_register[i] + value

    def pack_register(first, planes):
        for f in range(5):
            value = packed_z[f]
            for n in range(planes):
                value = pack_z(register[f, first + n], first + n, side, value)
            packed_z[f] = value

    def stores_of(piece):
        first = pl.multiple_of(piece * 8, 8)
        return [
            pltpu.make_async_copy(
                state.at[:, pl.ds(first + 1, 8), j, :],
                fine_out.at[0, 0, :, pl.ds(first, 8), pl.ds(j * 128, 128)],
                store_sem,
            )
            for j in range(8)
        ]

    each(BESIDE, CHUNK // PIECE + AHEAD, relay_on)
    wait_for(landed.at[pl.ds(1, 31)], ghost_recv)
    for f in range(6):
        turn = jnp.maximum(linked[f], 0) ^ slab
        for i in range(5):
            ghosts[f, i] = landed[turn, i]
    for piece in range(CHUNK // PIECE):
        arrive(piece)
    choose(0, CHUNK)
    for f in range(5):
        state[f, 0] = jnp.where(present[0], ghosts[0, f], state[f, 1])
        packed_z[f] = jnp.zeros(TILE, F32)
    for x in range(CHUNK - 1):
        spread(x)
    for substep in range(4):
        lowest = lowest_interface(state)
        outermost(substep, 0, lowest)
        reach = CHUNK - 1 - substep
        below = advance(state, 1, reach, lowest, updater(substep)) if reach > 0 else lowest
        for i in range(5):
            carry[substep, i] = below[i]

    def follow(first, planes):
        for n in range(planes // PIECE):
            arrive(first // PIECE + n)
        choose(first, planes)
        for n in range(planes):
            spread(first - 1 + n)
        for substep in range(4):
            below = [carry[substep, i] for i in range(5)]
            below = advance(state, first - substep, planes, below, updater(substep))
            for i in range(5):
                carry[substep, i] = below[i]

    def wave(c, _):
        for n in range(CHUNK // PIECE):
            piece = c * (CHUNK // PIECE) + AHEAD + n

            @pl.when(piece < PIECES)
            def _(piece=piece):
                relay_on(piece)

        follow(c * CHUNK, CHUNK)
        pack_register((c - 1) * CHUNK, CHUNK)

        @pl.when(c % 2 == 0)
        def _():
            for copy in stores_of(c // 2 - 1):
                copy.start()

        return 0

    lax.fori_loop(1, CHUNKS - 1, wave, 0)
    each(0, CHUNK // PIECE, lambda n: follow(32 - CHUNK + n * PIECE, PIECE))
    pack_register(32 - 2 * CHUNK, CHUNK)
    for f in range(5):
        state[f, 33] = jnp.where(present[1], ghosts[1, f], state[f, 32])
    spread(31)
    for substep in range(4):
        below = [carry[substep, i] for i in range(5)]
        outermost(substep, 1, advance(state, 32 - substep, substep + 1, below, updater(substep)))
    pack_register(32 - CHUNK, CHUNK)

    flat = register.reshape(5 * 32 * 8, 128)
    source_lane = lax.broadcasted_iota(jnp.int32, (128, 128), 0)
    target_lane = lax.broadcasted_iota(jnp.int32, (128, 128), 1)
    wanted = target_lane // 32 * 64 + target_lane % 32 * 2
    squeeze = ((source_lane == wanted) & (target_lane % 32 < 16) & (target_lane < 64)).astype(F32)
    for f in range(5):
        value = jnp.where(direction == 1, pack_y(flat, f * 256, side), packed_z[f])
        value = jnp.where(direction == 0, x_register[f], value)
        value = value + pltpu.roll(value, 127, 1)
        squeezed[pl.ds(f * 8, 8), :] = 0.25 * (value + pltpu.roll(value, 96, 1))
    squeezed[...] = jnp.dot(
        squeezed[...], squeeze, precision=lax.Precision.HIGHEST, preferred_element_type=F32
    )
    low_lanes = lax.broadcasted_iota(jnp.int32, (4, 128), 1) < 64
    for f in range(5):
        even = squeezed[pl.ds(f * 8, 4, stride=2), :]
        odd = squeezed[pl.ds(f * 8 + 1, 4, stride=2), :]
        small = jnp.where(low_lanes, even, pltpu.roll(odd, 64, 1))
        small = jnp.where(quarter_col == 0, small, pltpu.roll(small, 16, 1))
        note[f // 2, pl.ds(f % 2 * 4, 4), :] = small
    place = (level * 6 + (face ^ 1)) * 2 + quarter_row + 1
    columns = lax.broadcasted_iota(jnp.int32, (4, 128), 1) % 32 // 16
    note[2, pl.ds(4, 4), :] = jnp.where((columns == quarter_col) & valid, place.astype(F32), 0.0)
    for turn in (2, 3, 1):
        copy = pltpu.make_async_remote_copy(
            src_ref=note, dst_ref=notes.at[turn - 1],
            send_sem=note_send, recv_sem=note_recv,
            device_id=(slab, lvl ^ turn), device_id_type=MESH,
        )
        copy.start()
    for copy in stores_of(3):
        copy.start()

    wait_for(messages.at[pl.ds(1, 31)], ghost_send)

    wait_for(held, passed)

    wait_for(notes, note_recv)
    parts = [note if n == 3 else notes.at[n] for n in range(4)]
    keys = [part[2, pl.ds(4, 4), :] for part in parts]
    for g in range(6):
        for half in range(2):
            here = pl.ds(half * 4, 4)
            key = ((lvl * 6 + g) * 2 + half + 1).astype(F32)
            hits = [value == key for value in keys]
            cover = jnp.zeros((4, 128), F32)
            for n in range(4):
                cover = cover + jnp.where(hits[n], 1.0, 0.0)
            for f in range(5):
                total = jnp.zeros((4, 128), F32)
                for n in range(4):
                    total = total + jnp.where(hits[n], parts[n][f // 2, pl.ds(f % 2 * 4, 4), :], 0.0)
                factor = COARSE_STEP if g % 2 else -COARSE_STEP
                amounts[g, f, here, :] = factor * (cover * flux_faces[g, f, here, :] - total)
    wait_for(notes, note_send)
    coarse_store.wait()
    wait_for(state.at[:, pl.ds(1, 32)], store_sem)


def finish_kernel(
    fine, coarse, given, fine_out, coarse_out, fine_held, state, amounts,
    fine_sem, fine_out_sem, coarse_sem, given_sem, out_sem,
):
    def load(n):
        planes = pl.ds(n * 8, 8)
        return pltpu.make_async_copy(coarse.at[:, planes], state.at[:, planes], coarse_sem.at[n])

    def store(n, j):
        first = pl.multiple_of(n * 8, 8)
        return pltpu.make_async_copy(
            state.at[:, pl.ds(first, 8), j, :],
            coarse_out.at[0, 0, :, pl.ds(first, 8), pl.ds(j * 128, 128)],
            out_sem,
        )

    def fine_load(f):
        return pltpu.make_async_copy(fine.at[0, 0, f], fine_held.at[f], fine_sem)

    def fine_store(f):
        return pltpu.make_async_copy(fine_held.at[f], fine_out.at[0, 0, f], fine_out_sem)

    fetch = pltpu.make_async_copy(given, amounts, given_sem)
    fetch.start()
    each(0, 4, lambda n: load(n).start())
    each(0, 5, lambda f: fine_load(f).start())

    def correct(x):
        cells = load_plane(state, x)
        for d, spreader in ((1, spread_y), (2, spread_z)):
            lower, upper = edge_masks(d)
            for f in range(5):
                low = jnp.where(lower, spreader(amounts.at[2 * d], f, x, 0), 0.0)
                cells[f] = cells[f] + jnp.where(upper, spreader(amounts.at[2 * d + 1], f, x, 1), low)
        for f in range(5):
            state[f, x] = cells[f]

    def correct_eight(n):
        load(n).wait()
        for end in range(2):

            @pl.when(n == end * 3)
            def _(end=end):
                for f in range(5):
                    state[f, 31 * end] = state[f, 31 * end] + amounts[end, f]

        def correct_four(half):
            for k in range(4):
                correct(n * 8 + half * 4 + k)

        each(0, 2, correct_four)
        for j in range(8):
            store(n, j).start()

    fetch.wait()
    correct_eight(0)
    wait_for(fine_held, fine_sem)
    each(0, 5, lambda f: fine_store(f).start())
    each(1, 4, correct_eight)
    wait_for(fine_held, fine_out_sem)
    wait_for(state, out_sem)


SMEM = pl.BlockSpec(memory_space=pltpu.SMEM)
VMEM = pl.BlockSpec(memory_space=pltpu.VMEM)
HBM = pl.BlockSpec(memory_space=pltpu.HBM)
DMA = pltpu.SemaphoreType.DMA
LIMIT = 60 * 1024 * 1024


def step(partner, neighbours, work, link, fine_state, coarse_state):
    return pl.pallas_call(
        step_kernel,
        out_shape=(
            jax.ShapeDtypeStruct(fine_state.shape, F32),
            jax.ShapeDtypeStruct(PATCH, F32),
            jax.ShapeDtypeStruct((6, 5, *TILE), F32),
        ),
        in_specs=[SMEM, SMEM, SMEM, SMEM, HBM, HBM],
        out_specs=(HBM, HBM, VMEM),
        scratch_shapes=[
            pltpu.VMEM((6, *PATCH), F32),
            pltpu.VMEM(PATCH, F32),
            pltpu.VMEM((6, 5, *TILE), F32),
            pltpu.VMEM((32, 5, *TILE), F32),
            pltpu.VMEM((32, 5, *TILE), F32),
            pltpu.VMEM((6, 5, *TILE), F32),
            pltpu.VMEM((5, 34, *TILE), F32),
            pltpu.VMEM((10, 32, *TILE), F32),
            pltpu.VMEM((10, 32, *TILE), F32),
            pltpu.VMEM(PATCH, F32),
            pltpu.VMEM((5, *TILE), F32),
            pltpu.VMEM((5, *TILE), F32),
            pltpu.VMEM((4, 5, *TILE), F32),
            pltpu.VMEM((40, 128), F32),
            pltpu.VMEM((5, 34, *TILE), F32),
            pltpu.VMEM(PATCH, F32),
            pltpu.VMEM(PATCH, F32),
            pltpu.VMEM((6, 5, *TILE), F32),
            pltpu.VMEM((3, *TILE), F32),
            pltpu.VMEM((3, 3, *TILE), F32),
            *(DMA,) * 9, DMA((PIECES,)), DMA((PIECES,)),
        ],
        compiler_params=pltpu.CompilerParams(collective_id=0, has_side_effects=True, vmem_limit_bytes=LIMIT),
        name="step",
    )(partner, neighbours, work, link, fine_state, coarse_state)


def finish(fine_result, coarse_result, amounts):
    shape = jax.ShapeDtypeStruct(fine_result.shape, F32)
    return pl.pallas_call(
        finish_kernel,
        out_shape=(shape, shape),
        in_specs=[HBM, HBM, HBM],
        out_specs=(HBM, HBM),
        scratch_shapes=[
            pltpu.VMEM((5, 32, 1024), F32), pltpu.VMEM(PATCH, F32), pltpu.VMEM((6, 5, *TILE), F32),
            DMA, DMA, DMA((4,)), DMA, DMA,
        ],
        compiler_params=pltpu.CompilerParams(vmem_limit_bytes=LIMIT),
        name="finish",
    )(fine_result, coarse_result, amounts)


def body(fine_state, coarse_state, partner, mig_slot, neighbours, work, coarse_link):
    del mig_slot
    results = step(
        partner.T, jnp.transpose(neighbours, (2, 1, 0)), work.T, coarse_link, fine_state, coarse_state
    )
    return finish(*results)


def solution(mesh):
    return jax.shard_map(
        body,
        mesh=mesh,
        in_specs=(
            P("slab", "lvl", None, None, None),
            P("slab", "lvl", None, None, None),
            P(None, "lvl"),
            P(None, "lvl"),
            P(None, "lvl", None),
            P(None, "lvl"),
            P("slab", "lvl"),
        ),
        out_specs=(P("slab", "lvl", None, None, None), P("slab", "lvl", None, None, None)),
        check_vma=False,
    )
```
